32 devices in a mesh: dp: 16 (over z, y, x), tensor: 2 (over core).
Axes of the slice: x: 2, y: 2, z: 4, core: 2. Of those that a mesh axis runs over, the one named last changes fastest.
Arguments:
- tokens: bfloat16 [16384, 768], P(('dp', 'tensor')), may hold values from -6 to 6
- qkv_weight: bfloat16 [768, 3, 768], P(None, None, 'tensor'), may hold values from -0.21875 to 0.21875
- qv_bias: float32 [2, 768], P(None, 'tensor'), may hold values from -3 to 3
- rel_table: float32 [256, 12], P(None, 'tensor'), may hold values from -4 to 4
- out_weight: bfloat16 [768, 768], P('tensor'), may hold values from -1.25 to 1.25
- out_bias: float32 [768], replicated, may hold values from -3 to 3
- norm1_gain: float32 [768], replicated, may hold values from 0.5 to 1.5
- norm1_bias: float32 [768], replicated, may hold values from -3 to 3
- up_weight: bfloat16 [768, 3072], P(None, 'tensor'), may hold values from -0.21875 to 0.21875
- up_bias: float32 [3072], P('tensor'), may hold values from -3 to 3
- down_weight: bfloat16 [3072, 768], P('tensor'), may hold values from -0.109375 to 0.109375
- down_bias: float32 [768], replicated, may hold values from -3 to 3
- norm2_gain: float32 [768], replicated, may hold values from 0.5 to 1.5
- norm2_bias: float32 [768], replicated, may hold values from -3 to 3
- rel_bucket: int32 [512, 512], replicated, may hold values from 0 to 127
- query_len: int32 [32], P('dp'), may hold values from 1 to 128
- key_mask: int32 [32, 512], P('dp'), may hold values from 0 to 1, as said below
- upstream: bfloat16 [16384, 768], P(('dp', 'tensor')), may hold values from -6 to 6
Outputs:
- out: bfloat16 [16384, 768], P(('dp', 'tensor'))
- grad_tokens: float32 [16384, 768], P(('dp', 'tensor'))
- grad_qkv_weight: float32 [768, 3, 768], P(None, None, 'tensor')
- grad_qv_bias: float32 [2, 768], P(None, 'tensor')
- grad_rel_table: float32 [256, 12], P(None, 'tensor')
- grad_out_weight: float32 [768, 768], P('tensor')
- grad_out_bias: float32 [768], replicated
- grad_norm1_gain: float32 [768], replicated
- grad_norm1_bias: float32 [768], replicated
- grad_up_weight: float32 [768, 3072], P(None, 'tensor')
- grad_up_bias: float32 [3072], P('tensor')
- grad_down_weight: float32 [3072, 768], P('tensor')
- grad_down_bias: float32 [768], replicated
- grad_norm2_gain: float32 [768], replicated
- grad_norm2_bias: float32 [768], replicated
The draws below stay inside these ranges and needn't reach their ends.
Inputs may be any that keep to these rules, and one draw needn't show every extreme that they name: Each row of key_mask is 1 on its first positions and 0 after them, with 256 or more ones; in every draw some pair has no padding.
All inputs are finite; a program needn't handle non-finite values.
Results may differ from the reference program's by a relative error of at most 0.017.
The reference program's roundings to bfloat16 on the way count: a program that leaves them out, or rounds other values in their place, can miss the bound.
Values may be sent and summed in bfloat16 or wider, within the bound.
A program may use at most 192 MiB of HBM per device.

```python
import math
import jax
import jax.numpy as jnp
from jax import lax

D = 768
HEADS = 12
HEAD_DIM = 64
FF = 3072
BUCKETS = 256
SEQ = 512
PAIRS = 32
TOKENS = 16384


def draw_key_mask(key, part):
    key = jax.random.fold_in(key, 7)
    key_len, key_pick = jax.random.split(key)
    lengths = jax.random.randint(key_len, (PAIRS,), SEQ // 2, SEQ + 1)
    chosen = jax.random.randint(key_pick, (), 0, PAIRS)
    lengths = jnp.where(jnp.arange(PAIRS) == chosen, SEQ, lengths)
    position = jnp.arange(SEQ)
    return (position[None, :] < lengths[:, None]).astype(jnp.int32)


def with_ends(entries, own_key, least, high):
    shape = entries.shape
    index_at = [jax.random.randint(jax.random.fold_in(own_key, axis), (), 0, shape[axis]) for axis in range(len(shape))]
    entries = entries.at[tuple(index_at)].set(least)
    longest = shape.index(max(shape))
    index_at[longest] = (index_at[longest] + 1) % shape[longest]
    return entries.at[tuple(index_at)].set(high)


def levels(own_key, dims, cuts, smallest, largest):
    level = 1.0
    for dim, parts in cuts:
        heights = jax.random.uniform(jax.random.fold_in(jax.random.fold_in(own_key, 6), dim), (parts,), jnp.float32, smallest / len(cuts), largest / len(cuts))
        level = level * jnp.repeat(jnp.exp(heights), dims[dim] // parts).reshape((-1,) + (1,) * (len(dims) - 1 - dim))
    return level


def scatter_about(rng, shape, scale, limit, cuts=(), kind=jnp.bfloat16):
    drawn = jax.random.normal(rng, shape, jnp.float32) * scale
    if len(cuts) > 0:
        drawn = levels(rng, shape, cuts, -0.22, 0.18) * drawn
    return jnp.clip(drawn, min=-limit, max=limit).astype(kind)


def setup_inputs(seed: int = 0) -> dict:
    arg_keys = jax.random.split(jax.random.key(seed), 19)
    tokens = scatter_about(arg_keys[0], (TOKENS, D), 1.0, 6.0, ((0, 32),))
    qkv_weight = scatter_about(arg_keys[1], (D, 3, D), D ** -0.5, 0.21875, ((2, 2),))
    qv_bias = scatter_about(arg_keys[2], (2, D), 0.5, 3.0, ((1, 2),), jnp.float32)
    rel_table = scatter_about(arg_keys[3], (BUCKETS, HEADS), 1.0, 4.0, ((1, 2),), jnp.float32)
    out_weight = scatter_about(arg_keys[4], (D, D), (D // 32) ** -0.5, 1.25, ((0, 2),))
    out_bias = scatter_about(arg_keys[5], (D,), 0.5, 3.0, (), jnp.float32)
    norm1_gain = jnp.clip(1.0 + 0.1 * jax.random.normal(arg_keys[6], (D,), jnp.float32), 0.5, 1.5)
    norm1_bias = scatter_about(arg_keys[7], (D,), 0.5, 3.0, (), jnp.float32)
    up_weight = scatter_about(arg_keys[8], (D, FF), D ** -0.5, 0.21875, ((1, 2),))
    up_bias = scatter_about(arg_keys[9], (FF,), 0.5, 3.0, ((0, 2),), jnp.float32)
    down_weight = scatter_about(arg_keys[10], (FF, D), FF ** -0.5, 0.109375, ((0, 2),))
    down_bias = scatter_about(arg_keys[11], (D,), 0.5, 3.0, (), jnp.float32)
    norm2_gain = jnp.clip(1.0 + 0.1 * jax.random.normal(arg_keys[12], (D,), jnp.float32), 0.5, 1.5)
    norm2_bias = scatter_about(arg_keys[13], (D,), 0.5, 3.0, (), jnp.float32)
    rel_bucket = with_ends(jax.random.randint(arg_keys[14], (SEQ, SEQ), 0, BUCKETS // 2), jax.random.fold_in(arg_keys[14], 1), 0, (BUCKETS // 2) - 1).astype(jnp.int32)
    query_len = with_ends(jax.random.randint(arg_keys[15], (PAIRS,), 1, SEQ // 4 + 1), jax.random.fold_in(arg_keys[15], 1), 1, (SEQ // 4 + 1) - 1).astype(jnp.int32)
    key_mask = draw_key_mask(jax.random.fold_in(arg_keys[18], 71), 0)
    upstream = scatter_about(arg_keys[17], (TOKENS, D), 1.0, 6.0, ((0, 32),))
    return {"tokens": tokens, "qkv_weight": qkv_weight, "qv_bias": qv_bias, "rel_table": rel_table, "out_weight": out_weight, "out_bias": out_bias, "norm1_gain": norm1_gain, "norm1_bias": norm1_bias, "up_weight": up_weight, "up_bias": up_bias, "down_weight": down_weight, "down_bias": down_bias, "norm2_gain": norm2_gain, "norm2_bias": norm2_bias, "rel_bucket": rel_bucket, "query_len": query_len, "key_mask": key_mask, "upstream": upstream}


EPSILON = 1e-05
FAR_BELOW = -1000000000.0

@jax.custom_vjp
def low(v):
    return lax.optimization_barrier(v.astype(jnp.bfloat16)).astype(jnp.float32)

@jax.custom_vjp
def low_back(v):
    return v

def low_keep(v):
    return (low(v), None)

def low_pass(kept, grad):
    return (grad,)

def back_keep(v):
    return (v, None)

def back_low(kept, grad):
    return (low(grad),)
low.defvjp(low_keep, low_pass)
low_back.defvjp(back_keep, back_low)

def layer_norm(values, gain, shift):
    center = values - lax.optimization_barrier(jnp.mean(values, axis=-1, keepdims=True))
    scaled = center * lax.rsqrt(lax.optimization_barrier(jnp.mean(center * center, axis=-1, keepdims=True)) + EPSILON)
    return scaled * gain + shift

def matmul(left, right):
    return jnp.dot(left, right, precision=lax.Precision.HIGHEST)

def reference(tokens, qkv_weight, qv_bias, rel_table, out_weight, out_bias, norm1_gain, norm1_bias, up_weight, up_bias, down_weight, down_bias, norm2_gain, norm2_bias, rel_bucket, query_len, key_mask, upstream):
    pairs = TOKENS // SEQ
    group = math.gcd(pairs, 4)
    blocks = pairs // group
    position = jnp.arange(SEQ, dtype=jnp.int32)
    bucket_base = rel_bucket.astype(jnp.int32)

    def layer(layer_in, mixed_weight, qv_shift, table, w_out, b_out, gain_one, shift_one, w_up, b_up, w_down, b_down, gain_two, shift_two):
        mixed = matmul(layer_in, mixed_weight.reshape(D, 3 * D))
        query = low(low_back((mixed[:, :D] + qv_shift[0]) * 0.125))
        keys = low(low_back(mixed[:, D:2 * D]))
        values = low(low_back(mixed[:, 2 * D:] + qv_shift[1]))
        shape = (blocks, group, SEQ, HEADS, HEAD_DIM)

        def attend(items):
            query_blk, key_blk, value_blk, lengths, valid = items
            segment = position[None, :] < lengths[:, None]
            bucket = bucket_base[None] + BUCKETS // 2 * (segment[:, :, None] != segment[:, None, :]).astype(jnp.int32)
            bias = jnp.transpose(table[bucket], (0, 3, 1, 2))
            scores = low_back(jnp.einsum('gihd,gjhd->ghij', query_blk, key_blk, precision=lax.Precision.HIGHEST))
            scores = jnp.where(valid[:, None, None, :] > 0, scores + bias, FAR_BELOW)
            chances = jax.nn.softmax(scores, axis=-1)
            return jnp.einsum('ghij,gjhd->gihd', low(chances), value_blk, precision=lax.Precision.HIGHEST)
        attended = lax.map(jax.checkpoint(attend), (query.reshape(shape), keys.reshape(shape), values.reshape(shape), query_len.reshape(blocks, group), key_mask.reshape(blocks, group, SEQ)))
        heads_out = low(low_back(attended.reshape(TOKENS, D)))
        first = layer_norm(low_back(matmul(heads_out, w_out)) + b_out + layer_in, gain_one, shift_one)
        hidden = low_back(matmul(low(first), w_up) + b_up)
        activated = low(jax.nn.gelu(hidden, approximate=False))
        second = low_back(matmul(activated, w_down)) + b_down + first
        return layer_norm(second, gain_two, shift_two)
    floats = tuple((array.astype(jnp.float32) for array in (tokens, qkv_weight, qv_bias, rel_table, out_weight, out_bias, norm1_gain, norm1_bias, up_weight, up_bias, down_weight, down_bias, norm2_gain, norm2_bias)))
    result, pullback = jax.vjp(layer, *floats)
    grads = pullback(upstream.astype(jnp.float32))
    return (result.astype(jnp.bfloat16), grads[0], grads[1], grads[2], grads[3], grads[4], grads[5], grads[6], grads[7], grads[8], grads[9], grads[10], grads[11], grads[12], grads[13])
```

```python
import functools
import math

import jax
import jax.numpy as jnp
from jax import lax
from jax.experimental import pallas as pl
from jax.experimental.pallas import tpu as pltpu
from jax.sharding import PartitionSpec as P

EPSILON = 1e-05
FAR_BELOW = -1000000000.0
MESH = pl.DeviceIdType.MESH
F32 = jnp.float32
BF16 = jnp.bfloat16
LANES = 128
NT = (((1,), (1,)), ((), ()))
TN = (((0,), (0,)), ((), ()))
VMEM_LIMIT = 62 * 2**20


def dot(left, right, dims=None):
    if dims is None:
        return jnp.dot(left, right, preferred_element_type=F32)
    return lax.dot_general(left, right, dims, preferred_element_type=F32)


def other_core():
    return {"tensor": 1 - lax.axis_index("tensor")}


def row(ref):
    return ref[...].reshape(1, ref.shape[-1])


def fold8(block):
    return jnp.sum(block.reshape(block.shape[0] // 8, 8, block.shape[1]), axis=0)


def pack_tables(tab, packed):
    step = jnp.maximum(jnp.max(jnp.abs(tab[...])), 1e-30) / 32000.0
    inverse = 1.0 / step
    heads = tab.shape[1]
    for core in range(2):
        for pair in range(heads // 2):
            high = tab[core, 2 * pair : 2 * pair + 1, :] * inverse
            low = jnp.round(tab[core, 2 * pair + 1 : 2 * pair + 2, :] * inverse)
            high = jnp.round(high - low * (1 / 65536.0))
            both = high.astype(jnp.int32) * 65536 + low.astype(jnp.int32)
            packed[core * (heads // 2) + pair] = jnp.broadcast_to(both, packed.shape[1:])
    return step


def attend_pair(pair, q, k, vt, packed, bucket, valid, length, step, expo, heads_t, recip):
    seq = q.shape[0]
    cols = pl.ds(pl.multiple_of(pair * LANES, LANES), LANES)
    keys = k[:, cols]
    queries = q[:, cols]
    lane = lax.broadcasted_iota(jnp.int32, (seq, LANES), 1)
    in_query = lax.broadcasted_iota(jnp.int32, (seq, LANES), 0) < length
    terms = packed[pair, 0:1, :]
    near = jnp.broadcast_to(terms[:, :LANES], (seq, LANES))
    far = jnp.broadcast_to(terms[:, LANES:], (seq, LANES))
    same = jnp.where(in_query, far, near)
    swap = jnp.where(in_query, near, far)
    pieces = ([], [])
    for start in range(0, seq, LANES):
        index = bucket[:, start : start + LANES]
        got = jnp.take_along_axis(same, index, axis=1, mode="promise_in_bounds")
        if start == 0:
            turned = jnp.take_along_axis(swap, index, axis=1, mode="promise_in_bounds")
            got = jnp.where(lane < length, turned, got)
        pieces[0].append(got.astype(F32) * (step * (1 / 65536.0)))
        pieces[1].append(jnp.left_shift(got, 16).astype(F32) * (step * (1 / 65536.0)))
    first = lane < LANES // 2
    real = jnp.concatenate([valid[...] > 0] * (seq // LANES), axis=1)
    for side in range(2):
        mine = first if side == 0 else jnp.logical_not(first)
        scores = dot(jnp.where(mine, keys, jnp.zeros_like(keys)), queries, NT)
        scores = scores + jnp.concatenate(pieces[side], axis=1)
        scores = jnp.where(real, scores, FAR_BELOW)
        highest = jnp.max(scores, axis=0, keepdims=True)
        weights = jnp.exp(scores - highest).astype(BF16)
        expo[2 * pair + side] = weights
        rows = pl.ds(pl.multiple_of(pair * LANES + side * 64, 64), 64)
        values = jnp.concatenate([vt[rows, :], jnp.ones((16, seq), BF16)], axis=0)
        got = dot(values, weights)
        inverse = 1.0 / got[64:65]
        heads_t[rows, :] = (got[:64] * inverse).astype(BF16)
        recip[2 * pair + side] = jnp.broadcast_to(inverse, recip.shape[1:])


def forward_kernel(
    tokens_h,
    qkvw_h,
    qvb_h,
    tab_h,
    outw_h,
    upw_h,
    upb_h,
    downw_h,
    upstream_h,
    outb,
    gain1,
    shift1,
    downb,
    gain2,
    shift2,
    bucket,
    length,
    mask,
    out_h,
    gsec_h,
    gbr_h,
    act_h,
    slope_h,
    first_h,
    normed1_h,
    inverse1_h,
    heads_h,
    q_h,
    k_h,
    v_h,
    expo_h,
    recip_h,
    qkvw_o,
    outw_o,
    upw_o,
    downw_o,
    sums,
    tokens,
    qkvw,
    qvb,
    tab,
    outw,
    upw,
    upb,
    downw,
    upstream,
    packed,
    valid,
    q,
    k,
    v,
    vt,
    heads_t,
    expo,
    recip,
    wide,
    first32,
    normed1,
    inverse1,
    first16,
    act,
    slope,
    gsec,
    gbr,
    out,
    in_sem,
    out_sem,
    send_sem,
    recv_sem,
):
    seq, width = tokens.shape
    inner = qkvw.shape[3]
    half_units = upw.shape[2]
    pairs = inner // LANES
    barrier = pltpu.get_barrier_semaphore()
    pl.semaphore_signal(barrier, inc=1, device_id=other_core(), device_id_type=MESH)

    loads = []
    for number, (source, target) in enumerate(
        (
            (tokens_h, tokens),
            (qkvw_h, qkvw.at[0]),
            (qvb_h, qvb.at[0]),
            (tab_h, tab.at[0]),
            (outw_h, outw.at[0]),
            (upw_h, upw.at[0]),
            (upb_h, upb.at[0]),
            (downw_h, downw.at[0]),
            (upstream_h, upstream),
        )
    ):
        copy = pltpu.make_async_copy(source, target, in_sem.at[number])
        copy.start()
        loads.append(copy)

    pl.semaphore_wait(barrier, 1)
    sends = []
    for number, (source, target) in enumerate(
        (
            (qkvw_h, qkvw.at[1]),
            (qvb_h, qvb.at[1]),
            (tab_h, tab.at[1]),
            (outw_h, outw.at[1]),
            (upw_h, upw.at[1]),
            (upb_h, upb.at[1]),
            (downw_h, downw.at[1]),
        )
    ):
        copy = pltpu.make_async_remote_copy(
            src_ref=source,
            dst_ref=target,
            send_sem=send_sem.at[number],
            recv_sem=recv_sem.at[number],
            device_id=other_core(),
            device_id_type=MESH,
        )
        copy.start()
        sends.append(copy)

    stores = []

    def store(source, target):
        copy = pltpu.make_async_copy(source, target, out_sem.at[len(stores)])
        copy.start()
        stores.append(copy)

    me = lax.axis_index("tensor")
    span = length[me]
    mine = mask[pl.ds(me, 1), :].astype(F32)
    valid[...] = jnp.transpose(jnp.broadcast_to(mine, (LANES, seq)))

    def mix(core):
        rows = tokens[...]
        cols = slice(core * inner, (core + 1) * inner)
        query = dot(rows, qkvw[core, 0])
        q[:, cols] = ((query + qvb[core, 0:1, :]) * 0.125).astype(BF16)
        k[:, cols] = dot(rows, qkvw[core, 1]).astype(BF16)
        value = (dot(rows, qkvw[core, 2]) + qvb[core, 1:2, :]).astype(BF16)
        v[:, cols] = value
        vt[cols, :] = jnp.transpose(value)

    loads[0].wait()
    loads[1].wait()
    loads[2].wait()
    mix(0)
    loads[3].wait()
    sends[0].wait_recv()
    sends[1].wait_recv()
    sends[2].wait_recv()
    mix(1)
    step = pack_tables(tab, packed)
    store(q, q_h)
    store(k, k_h)
    store(v, v_h)
    store(qkvw.at[1], qkvw_o)

    def attend(pair, carry):
        attend_pair(pair, q, k, vt, packed, bucket, valid, span, step, expo, heads_t, recip)
        return carry

    lax.fori_loop(0, 2 * pairs, attend, 0)
    store(expo, expo_h)
    store(recip, recip_h)
    store(heads_t, heads_h)

    loads[4].wait()
    sends[3].wait_recv()
    store(outw.at[1], outw_o)
    lower = jnp.transpose(heads_t[...])

    def project(tile, carry):
        cols = pl.ds(pl.multiple_of(tile * 256, 256), 256)
        wide[:, cols] = dot(lower[:, :inner], outw[0, :, cols]) + dot(
            lower[:, inner:], outw[1, :, cols]
        )
        return carry

    lax.fori_loop(0, width // 256, project, 0)
    block = 128

    def norm_one(number, carry):
        rows = pl.ds(pl.multiple_of(number * block, block), block)
        value = wide[rows, :] + row(outb) + tokens[rows, :].astype(F32)
        center = value - jnp.mean(value, axis=-1, keepdims=True)
        inverse = lax.rsqrt(jnp.mean(center * center, axis=-1, keepdims=True) + EPSILON)
        normed = center * inverse
        result = normed * row(gain1) + row(shift1)
        normed1[rows, :] = normed
        inverse1[rows, :] = jnp.broadcast_to(inverse, (block, LANES))
        first32[rows, :] = result
        first16[rows, :] = result.astype(BF16)
        return carry

    lax.fori_loop(0, seq // block, norm_one, 0)
    store(first16, first_h)
    store(normed1, normed1_h)
    store(inverse1, inverse1_h)

    for core in range(2):
        if core == 0:
            loads[5].wait()
            loads[6].wait()
        else:
            sends[4].wait_recv()
            sends[5].wait_recv()
            store(upw.at[1], upw_o)

        def expand(tile, carry, core=core):
            cols = pl.ds(pl.multiple_of(tile * 256, 256), 256)
            here = pl.ds(pl.multiple_of(core * half_units + tile * 256, 256), 256)
            hidden = dot(first16[...], upw[core, :, cols]) + upb[core, :, cols]
            chance = 0.5 * (1.0 + lax.erf(hidden * math.sqrt(0.5)))
            density = jnp.exp(hidden * hidden * -0.5) * (1.0 / math.sqrt(2.0 * math.pi))
            act[:, here] = (hidden * chance).astype(BF16)
            slope[:, here] = (chance + hidden * density).astype(BF16)
            return carry

        lax.fori_loop(0, half_units // 256, expand, 0)
    store(act, act_h)
    store(slope, slope_h)
    loads[7].wait()
    sends[6].wait_recv()
    store(downw.at[1], downw_o)

    def reduce_units(tile, carry):
        cols = pl.ds(pl.multiple_of(tile * 256, 256), 256)
        wide[:, cols] = dot(act[:, :half_units], downw[0, :, cols]) + dot(
            act[:, half_units:], downw[1, :, cols]
        )
        return carry

    lax.fori_loop(0, width // 256, reduce_units, 0)
    loads[8].wait()

    def norm_two(number, carry):
        rows = pl.ds(pl.multiple_of(number * block, block), block)
        value = wide[rows, :] + row(downb) + first32[rows, :]
        center = value - jnp.mean(value, axis=-1, keepdims=True)
        inverse = lax.rsqrt(jnp.mean(center * center, axis=-1, keepdims=True) + EPSILON)
        normed = center * inverse
        out[rows, :] = (normed * row(gain2) + row(shift2)).astype(BF16)
        grad = upstream[rows, :].astype(F32)
        scaled = grad * row(gain2)
        back = inverse * (
            scaled
            - jnp.mean(scaled, axis=-1, keepdims=True)
            - normed * jnp.mean(scaled * normed, axis=-1, keepdims=True)
        )
        gsec[rows, :] = back
        gbr[rows, :] = back.astype(BF16)
        return (
            carry[0] + fold8(grad * normed),
            carry[1] + fold8(grad),
            carry[2] + fold8(back),
        )

    zero = jnp.zeros((8, width), F32)
    totals = lax.fori_loop(0, seq // block, norm_two, (zero, zero, zero))
    for number, total in enumerate(totals):
        sums[number : number + 1, :] = jnp.sum(total, axis=0, keepdims=True)
    sums[3:, :] = jnp.zeros((5, width), F32)
    store(out, out_h)
    store(gsec, gsec_h)
    store(gbr, gbr_h)
    for copy in stores:
        copy.wait()
    for copy in sends:
        copy.wait_send()


def forward(
    tokens,
    qkvw,
    qvb,
    tab,
    outw,
    outb,
    gain1,
    shift1,
    upw,
    upb,
    downw,
    downb,
    gain2,
    shift2,
    bucket,
    length,
    mask,
    upstream,
):
    seq, width = tokens.shape
    inner = qkvw.shape[2]
    units = upw.shape[1]
    heads = 2 * tab.shape[0]
    shape = jax.ShapeDtypeStruct
    here = pl.BlockSpec(memory_space=pltpu.VMEM)
    away = pl.BlockSpec(memory_space=pl.ANY)
    scalar = pl.BlockSpec(memory_space=pltpu.SMEM)
    out_shape = (
        shape((seq, width), BF16),
        shape((seq, width), F32),
        shape((seq, width), BF16),
        shape((seq, 2 * units), BF16),
        shape((seq, 2 * units), BF16),
        shape((seq, width), BF16),
        shape((seq, width), F32),
        shape((seq, LANES), F32),
        shape((2 * inner, seq), BF16),
        shape((seq, 2 * inner), BF16),
        shape((seq, 2 * inner), BF16),
        shape((seq, 2 * inner), BF16),
        shape((heads, seq, seq), BF16),
        shape((heads, 8, seq), F32),
        shape(qkvw.shape, BF16),
        shape(outw.shape, BF16),
        shape(upw.shape, BF16),
        shape(downw.shape, BF16),
        shape((8, width), F32),
    )
    scratch = [
        pltpu.VMEM((seq, width), BF16),
        pltpu.VMEM((2,) + qkvw.shape, BF16),
        pltpu.VMEM((2,) + qvb.shape, F32),
        pltpu.VMEM((2,) + tab.shape, F32),
        pltpu.VMEM((2,) + outw.shape, BF16),
        pltpu.VMEM((2,) + upw.shape, BF16),
        pltpu.VMEM((2,) + upb.shape, F32),
        pltpu.VMEM((2,) + downw.shape, BF16),
        pltpu.VMEM((seq, width), BF16),
        pltpu.VMEM((heads // 2, 8, 2 * LANES), jnp.int32),
        pltpu.VMEM((seq, LANES), F32),
        pltpu.VMEM((seq, 2 * inner), BF16),
        pltpu.VMEM((seq, 2 * inner), BF16),
        pltpu.VMEM((seq, 2 * inner), BF16),
        pltpu.VMEM((2 * inner, seq), BF16),
        pltpu.VMEM((2 * inner, seq), BF16),
        pltpu.VMEM((heads, seq, seq), BF16),
        pltpu.VMEM((heads, 8, seq), F32),
        pltpu.VMEM((seq, width), F32),
        pltpu.VMEM((seq, width), F32),
        pltpu.VMEM((seq, width), F32),
        pltpu.VMEM((seq, LANES), F32),
        pltpu.VMEM((seq, width), BF16),
        pltpu.VMEM((seq, 2 * units), BF16),
        pltpu.VMEM((seq, 2 * units), BF16),
        pltpu.VMEM((seq, width), F32),
        pltpu.VMEM((seq, width), BF16),
        pltpu.VMEM((seq, width), BF16),
        pltpu.SemaphoreType.DMA((9,)),
        pltpu.SemaphoreType.DMA((20,)),
        pltpu.SemaphoreType.DMA((7,)),
        pltpu.SemaphoreType.DMA((7,)),
    ]
    return pl.pallas_call(
        forward_kernel,
        out_shape=out_shape,
        in_specs=[away] * 9 + [here] * 7 + [scalar, here],
        out_specs=(away,) * 18 + (here,),
        scratch_shapes=scratch,
        compiler_params=pltpu.CompilerParams(
            collective_id=0, has_side_effects=True, vmem_limit_bytes=VMEM_LIMIT
        ),
    )(
        tokens,
        qkvw,
        qvb,
        tab,
        outw,
        upw,
        upb,
        downw,
        upstream,
        outb,
        gain1,
        shift1,
        downb,
        gain2,
        shift2,
        bucket,
        length,
        mask,
    )


def dp_side(bit):
    return lax.rem(lax.axis_index("dp") // (1 << bit), 2)


def dp_partner(bit):
    return {"dp": lax.axis_index("dp") + (1 - 2 * dp_side(bit)) * (1 << bit)}


def flat_rows(start, size):
    return pl.ds(pl.multiple_of(start, 16), size)


class Kit:
    def __init__(self, acc, landing, result, send_sem, recv_sem, local_sem):
        self.acc, self.landing, self.result = acc, landing, result
        self.send_sem, self.recv_sem, self.local_sem = send_sem, recv_sem, local_sem
        self.used = 0
        self.landed = 0
        self.pieces = []

    def slot(self):
        self.used += 1
        return self.used - 1

    def room(self, size):
        self.landed += size
        return self.landed - size

    def remote(self, slot, source, target, device):
        return pltpu.make_async_remote_copy(
            src_ref=source,
            dst_ref=target,
            send_sem=self.send_sem.at[slot],
            recv_sem=self.recv_sem.at[slot],
            device_id=device,
            device_id_type=MESH,
        )


class Piece:
    def __init__(self, start, length, order, extra, kit):
        self.start, self.length = start, length
        self.bits, self.extra = order, extra
        self.kit = kit
        self.number = len(kit.pieces)
        self.steps = 2 * len(order) + 1
        kit.pieces.append(self)
        self.halving = [
            (kit.slot(), kit.room(length >> (level + 1))) for level in range(len(order))
        ]
        self.crossing = [(kit.slot(), kit.room(length >> len(order))) for _ in extra]
        self.spreading = [kit.slot() for _ in order]
        self.sent = []

    def begin(self, levels):
        at = self.start
        for level in range(levels):
            at = at + dp_side(self.bits[level]) * (self.length >> (level + 1))
        return at

    def halve(self, level):
        kit, bit = self.kit, self.bits[level]
        slot, room = self.halving[level]
        size = self.length >> (level + 1)
        away = self.begin(level) + (1 - dp_side(bit)) * size
        return kit.remote(
            slot,
            kit.acc.at[flat_rows(away, size), :],
            kit.landing.at[pl.ds(room, size), :],
            dp_partner(bit),
        )

    def swap(self, number):
        kit = self.kit
        slot, room = self.crossing[number]
        size = self.length >> len(self.bits)
        return kit.remote(
            slot,
            kit.acc.at[flat_rows(self.begin(len(self.bits)), size), :],
            kit.landing.at[pl.ds(room, size), :],
            dp_partner(self.extra[number]),
        )

    def keep(self):
        kit, levels = self.kit, len(self.bits)
        mine = flat_rows(self.begin(levels), self.length >> levels)
        return pltpu.make_async_copy(
            kit.acc.at[mine, :], kit.result.at[mine, :], kit.local_sem.at[self.number]
        )

    def spread(self, number):
        kit = self.kit
        level = len(self.bits) - number
        mine = flat_rows(self.begin(level), self.length >> level)
        source = kit.acc if number == 0 else kit.result
        return kit.remote(
            self.spreading[number],
            source.at[mine, :],
            kit.result.at[mine, :],
            dp_partner(self.bits[level - 1]),
        )

    def add(self, target, source, size):
        kit = self.kit
        chunk = math.gcd(size, 192)

        def some(number, carry):
            there = flat_rows(target + number * chunk, chunk)
            here = flat_rows(source + number * chunk, chunk)
            total = kit.acc[there, :].astype(F32) + kit.landing[here, :].astype(F32)
            kit.acc[there, :] = total.astype(BF16)
            return carry

        lax.fori_loop(0, size // chunk, some, 0)

    def run(self, step):
        levels = len(self.bits)
        if 0 < step <= levels:
            self.halve(step - 1).wait_recv()
            self.add(self.begin(step), self.halving[step - 1][1], self.length >> step)
        if step < levels:
            self.halve(step).start()
            self.sent.append(functools.partial(self.halve, step))
            return
        if step == levels:
            for number in range(len(self.extra)):
                both = self.swap(number)
                both.start()
                both.wait()
                self.add(self.begin(levels), self.crossing[number][1], self.length >> levels)
            self.keep().start()
        else:
            self.spread(step - levels - 1).wait_recv()
            if step == levels + 1:
                self.keep().wait()
        if step < 2 * levels:
            self.spread(step - levels).start()
            self.sent.append(functools.partial(self.spread, step - levels))

    def finish(self):
        for sent in self.sent:
            sent().wait_send()


class Vectors:
    def __init__(self, parts, landing, result, bits, kit, send_sem, recv_sem):
        self.parts, self.landing, self.result = parts, landing, result
        self.bits = bits
        self.steps = bits + 2
        self.send_sem, self.recv_sem = send_sem, recv_sem
        kit.pieces.append(self)

    def exchange(self, step):
        return pltpu.make_async_remote_copy(
            src_ref=self.parts.at[step],
            dst_ref=self.landing.at[step],
            send_sem=self.send_sem.at[step],
            recv_sem=self.recv_sem.at[step],
            device_id=other_core() if step == 0 else dp_partner(step - 1),
            device_id_type=MESH,
        )

    def run(self, step):
        if step > 0:
            self.exchange(step - 1).wait_recv()
            total = self.parts[max(step - 1, 1)] + self.landing[step - 1]
            if step <= self.bits:
                self.parts[step] = total
            else:
                self.result[...] = total
        if step <= self.bits:
            self.exchange(step).start()

    def finish(self):
        for step in range(self.bits + 1):
            self.exchange(step).wait_send()


def backward_kernel(
    plan,
    bits,
    gbr_h,
    act_h,
    slope_h,
    first_h,
    gsec_h,
    normed1_h,
    inverse1_h,
    heads_h,
    q_h,
    k_h,
    v_h,
    expo_h,
    recip_h,
    qkvw_h,
    outw_h,
    upw_h,
    downw_h,
    qkvw_o,
    outw_o,
    upw_o,
    downw_o,
    tokens_h,
    sums2,
    gain1,
    bucket,
    length,
    result_h,
    gtok_h,
    small,
    acc,
    xsend,
    xrecv,
    landing,
    gbr,
    gsec,
    normed1,
    inverse1,
    heads_t,
    outw,
    gmid16,
    wide,
    q,
    k,
    v,
    recip,
    ups,
    vparts,
    vland,
    in_sem,
    out_sem,
    send_sem,
    recv_sem,
    local_sem,
    xs_sem,
    xr_sem,
    vs_sem,
    vr_sem,
):
    seq, width = gsec.shape
    inner = outw.shape[1]
    units = upw_h.shape[1]
    heads = recip.shape[0]
    levels = min(4, bits)

    barrier = pltpu.get_barrier_semaphore()
    pl.semaphore_signal(barrier, inc=1, device_id=other_core(), device_id_type=MESH)
    for bit in range(bits):
        pl.semaphore_signal(barrier, inc=1, device_id=dp_partner(bit), device_id_type=MESH)

    used = []

    def load(source, target):
        copy = pltpu.make_async_copy(source, target, in_sem.at[len(used)])
        used.append(copy)
        copy.start()
        return copy

    kit = Kit(acc, landing, result_h, send_sem, recv_sem, local_sem)
    orders = {
        "x": tuple(range(levels)),
        "y": ((1, 0) + tuple(range(2, levels)))[:levels] if levels > 1 else tuple(range(levels)),
        "z": tuple(range(2, levels)) + tuple(range(min(2, levels))),
    }
    extra = tuple(range(levels, bits))
    crossed = []

    def cross(start, size, place):
        number = len(crossed)

        def copy():
            return pltpu.make_async_remote_copy(
                src_ref=xsend.at[pl.ds(place, size), :],
                dst_ref=xrecv.at[pl.ds(start, size), :],
                send_sem=xs_sem.at[number],
                recv_sem=xr_sem.at[number],
                device_id=other_core(),
                device_id_type=MESH,
            )

        copy().start()
        crossed.append(copy)

    polls = [0]

    def poll():
        for number, step in plan.get(polls[0], ()):
            kit.pieces[number].run(step)
        polls[0] += 1

    def begin_piece(start, size, order):
        fresh = Piece(start, size, orders[order], extra, kit)
        fresh.run(0)

    def give(place, tile):
        xsend[flat_rows(place, tile.shape[0]), :] = tile.astype(BF16)

    def take(start, tile):
        there = flat_rows(start, tile.shape[0])
        acc[there, :] = (tile + xrecv[there, :].astype(F32)).astype(BF16)

    third = acc.shape[0] // 3
    split = width // inner

    def unit_phase(act, slope, downw, upw, first, first_t):
        l_gbr = load(gbr_h, gbr)
        l_act = [None, load(act_h.at[:, pl.ds(units, units)], act.at[:, pl.ds(units, units)])]
        l_act[0] = load(act_h.at[:, pl.ds(0, units)], act.at[:, pl.ds(0, units)])
        l_down = [None, load(downw_o, downw.at[1])]
        l_slope = load(slope_h, slope)
        l_down[0] = load(downw_h, downw.at[0])
        l_first = load(first_h, first)
        l_up = [load(upw_h, upw.at[0]), load(upw_o, upw.at[1])]
        l_late = [
            load(source, target)
            for source, target in (
                (gsec_h, gsec),
                (normed1_h, normed1),
                (inverse1_h, inverse1),
                (heads_h, heads_t),
                (outw_h, outw.at[0]),
                (outw_o, outw.at[1]),
                (recip_h, recip),
                (q_h, q),
                (k_h, k),
                (v_h, v),
            )
        ]
        pl.semaphore_wait(barrier, 1 + bits)

        tiles = units // 256
        group = tiles // 3
        span = 256 * split
        l_gbr.wait()
        for core in (1, 0):
            l_act[core].wait()
            for part in range(3):
                if core == 0:
                    crossed[part]().wait_recv()

                def down_tile(number, carry, core=core):
                    cols = pl.ds(pl.multiple_of(core * units + number * 256, 256), 256)
                    tile = dot(act[:, cols], gbr[...], TN)
                    for side in range(split):
                        (give if core == 1 else take)(
                            number * span + side * 256,
                            tile[:, side * inner : (side + 1) * inner],
                        )
                    return carry

                lax.fori_loop(part * group, (part + 1) * group, down_tile, 0)
                start = part * group * span
                if core == 1:
                    cross(start, group * span, start)
                else:
                    begin_piece(start, group * span, "xyz"[part])
                    poll()

        l_slope.wait()
        for core in (1, 0):
            l_down[core].wait()
            for part in range(2):

                def slope_tile(number, carry, core=core):
                    here = pl.ds(pl.multiple_of(number * 256, 256), 256)
                    cols = pl.ds(pl.multiple_of(core * units + number * 256, 256), 256)
                    tile = dot(gbr[...], downw[core, here, :], NT) * slope[:, cols].astype(F32)
                    tile = tile.astype(BF16)
                    slope[:, cols] = tile
                    ups[core, :, here] = fold8(tile.astype(F32))
                    return carry

                lax.fori_loop(part * (tiles // 2), (part + 1) * (tiles // 2), slope_tile, 0)
                poll()

        l_first.wait()
        first_t[...] = jnp.transpose(first[...])
        for copy in crossed[:3]:
            copy().wait_send()
        blocks = units // inner
        for core in (1, 0):
            for part in range(2):
                if core == 0:
                    crossed[3 + part]().wait_recv()

                def up_tile(number, carry, core=core):
                    cols = pl.ds(pl.multiple_of(core * units + number * inner, LANES), inner)
                    for top in range(0, width, 256):
                        tile = dot(first_t[top : top + 256, :], slope[:, cols])
                        if core == 1:
                            give(number * width + top, tile)
                        else:
                            take(third + number * width + top, tile)
                    return carry

                lax.fori_loop(part * (blocks // 2), (part + 1) * (blocks // 2), up_tile, 0)
                size = (blocks // 2) * width
                if core == 1:
                    cross(third + part * size, size, part * size)
                else:
                    begin_piece(third + part * size, size, "xy"[part])
                poll()

        l_up[0].wait()
        l_up[1].wait()
        l_late[0].wait()

        def first_tile(number, carry):
            cols = pl.ds(pl.multiple_of(number * 256, 256), 256)
            wide[:, cols] = (
                gsec[:, cols]
                + dot(slope[:, :units], upw[0, cols, :], NT)
                + dot(slope[:, units:], upw[1, cols, :], NT)
            )
            return carry

        lax.fori_loop(0, width // 256, first_tile, 0)
        poll()
        for copy in l_late[1:]:
            copy.wait()

    pl.run_scoped(
        unit_phase,
        pltpu.VMEM((seq, 2 * units), BF16),
        pltpu.VMEM((seq, 2 * units), BF16),
        pltpu.VMEM((2, units, width), BF16),
        pltpu.VMEM((2, width, units), BF16),
        pltpu.VMEM((seq, width), BF16),
        pltpu.VMEM((width, seq), BF16),
    )

    block = 128

    def norm_one(number, carry):
        rows = pl.ds(pl.multiple_of(number * block, block), block)
        grad = wide[rows, :]
        normed = normed1[rows, :]
        scaled = grad * row(gain1)
        back = inverse1[rows, 0:1] * (
            scaled
            - jnp.mean(scaled, axis=-1, keepdims=True)
            - normed * jnp.mean(scaled * normed, axis=-1, keepdims=True)
        )
        wide[rows, :] = back
        gmid16[rows, :] = back.astype(BF16)
        return (
            carry[0] + fold8(back),
            carry[1] + fold8(grad * normed),
            carry[2] + fold8(grad),
        )

    zero = jnp.zeros((8, width), F32)
    totals = lax.fori_loop(0, seq // block, norm_one, (zero, zero, zero))
    both = [jnp.sum(total, axis=0, keepdims=True) for total in totals]
    both += [sums2[2:3, :], sums2[0:1, :], sums2[1:2, :]]
    vparts[0] = jnp.zeros(vparts.shape[1:], F32)
    vparts[1] = jnp.zeros(vparts.shape[1:], F32)
    for number, line in enumerate(both):
        for side in range(split):
            at = number * split + side
            part = line[:, side * inner : (side + 1) * inner]
            vparts[0, at : at + 1, :] = part
            vparts[1, at : at + 1, :] = part
    for core in range(2):
        line = jnp.sum(ups[core], axis=0, keepdims=True)
        for side in range(units // inner):
            at = 6 * split + side
            vparts[1 - core, at : at + 1, :] = line[:, side * inner : (side + 1) * inner]
    poll()

    def attend_phase(
        qkvw, tokens, tokens_t, kt, dheads_t, dheads, dk, dv, gq_t, gq, gk, gv, expo, spread
    ):
        columns = 256
        l_qkvw = [load(qkvw_h, qkvw.at[0]), load(qkvw_o, qkvw.at[1])]
        l_tokens = load(tokens_h, tokens)
        l_expo = load(expo_h.at[:, :, pl.ds(0, columns)], expo)

        for copy in crossed[3:5]:
            copy().wait_send()
        at = 2 * third
        for core in (1, 0):
            tile = dot(heads_t[core * inner : (core + 1) * inner, :], gmid16[...])
            if core == 0:
                crossed[5]().wait_recv()
            for side in range(split):
                part = tile[:, side * inner : (side + 1) * inner]
                if core == 1:
                    give(side * inner, part)
                else:
                    take(at + side * inner, part)
            if core == 1:
                cross(at, split * inner, 0)
            else:
                begin_piece(at, split * inner, "z")
        poll()
        per = heads // 2
        size = inner // per
        for core in range(2):
            tile = dot(outw[core], gmid16[...], NT)
            for head in range(per):
                rows = slice(core * inner + head * size, core * inner + (head + 1) * size)
                part = tile[head * size : (head + 1) * size] * recip[core * per + head, 0:1, :]
                dheads_t[rows, :] = part.astype(BF16)
        dheads[...] = jnp.transpose(dheads_t[...])
        kt[...] = jnp.transpose(k[...])
        poll()

        span = length[lax.axis_index("tensor")]
        lane = lax.broadcasted_iota(jnp.int32, (seq, LANES), 1)
        first = lane < size
        labels = lax.broadcasted_iota(jnp.int32, (LANES, columns), 0).astype(BF16)
        tab = jnp.zeros((32, LANES), F32)
        for part in range(seq // columns):
            start = part * columns
            here = slice(start, start + columns)
            l_expo.wait()

            def pair_back(pair, carry, here=here, part=part):
                cols = pl.ds(pl.multiple_of(pair * LANES, LANES), LANES)
                values, queries = v[:, cols], q[here, cols]
                grads, grads_t = dheads[here, cols], dheads_t[cols, here]
                gvs, gks = [], []
                for side in range(2):
                    head = 2 * pair + side
                    mine = first if side == 0 else jnp.logical_not(first)
                    back = dot(jnp.where(mine, values, jnp.zeros_like(values)), grads_t)
                    chance = expo[head].astype(F32)
                    product = chance * back
                    shift = jnp.sum(product, axis=0, keepdims=True) * recip[head, 0:1, here]
                    gscore = product - chance * shift
                    for half in range(columns // LANES):
                        spread[pl.ds(half * seq * 16 + head, seq, stride=16), :] = gscore[
                            :, half * LANES : (half + 1) * LANES
                        ]
                    gscore = gscore.astype(BF16)
                    gvs.append(dot(expo[head], grads))
                    gks.append(dot(gscore, queries))
                    rows = pl.ds(pl.multiple_of(pair * LANES + side * size, size), size)
                    gq_t[rows, here] = (dot(kt[rows, :], gscore) * 0.125).astype(BF16)
                gvalue = jnp.where(first, gvs[0], gvs[1])
                gkey = jnp.where(first, gks[0], gks[1])
                if part == 0:
                    dv[:, cols] = gvalue
                    dk[:, cols] = gkey
                else:
                    gv[:, cols] = (dv[:, cols] + gvalue).astype(BF16)
                    gk[:, cols] = (dk[:, cols] + gkey).astype(BF16)
                return carry

            for group in range(heads // 4):
                lax.fori_loop(2 * group, 2 * group + 2, pair_back, 0)
                poll()
            if part + 1 < seq // columns:
                l_expo = load(expo_h.at[:, :, pl.ds(start + columns, columns)], expo)

            position = lax.broadcasted_iota(jnp.int32, (1, columns), 1) + start
            inside = (position < span).astype(F32)

            def count(number, carry, here=here, inside=inside):
                rows = pl.ds(pl.multiple_of(number * 16, 16), 16)
                index = bucket[rows, here]
                grads = jnp.concatenate(
                    [
                        spread[pl.ds(pl.multiple_of(half * seq * 16 + number * 256, 256), 256), :]
                        for half in range(columns // LANES)
                    ],
                    axis=1,
                )
                for line in range(16):
                    hot = jnp.where(
                        labels == index[line : line + 1, :],
                        jnp.ones((), BF16),
                        jnp.zeros((), BF16),
                    )
                    other = jnp.where(number * 16 + line < span, 1.0 - inside, inside)
                    some = grads[16 * line : 16 * line + 16]
                    far = some * other
                    both = jnp.concatenate([some - far, far], axis=0).astype(BF16)
                    carry = carry + dot(both, hot, NT)
                return carry

            tab = lax.fori_loop(0, seq // 16, count, tab)
            poll()

        gq[...] = jnp.transpose(gq_t[...])
        l_tokens.wait()
        tokens_t[...] = jnp.transpose(tokens[...])
        at = 2 * third + split * inner
        kinds = (gq, gk, gv)
        for core in (1, 0):
            for kind in range(3):
                if core == 0:
                    crossed[6 + kind]().wait_recv()
                for top in range(0, width, 256):
                    tile = dot(
                        tokens_t[top : top + 256, :],
                        kinds[kind][:, core * inner : (core + 1) * inner],
                    )
                    if core == 1:
                        give(split * inner + kind * width + top, tile)
                    else:
                        take(at + kind * width + top, tile)
                if core == 1:
                    cross(at + kind * width, width, split * inner + kind * width)
                else:
                    begin_piece(at + kind * width, width, "xyz"[kind])
                poll()

        for core in range(2):
            mine = slice(core * inner, (core + 1) * inner)
            at = 6 * split + units // inner
            for number, kind in ((0, gq), (1, gv)):
                line = jnp.sum(fold8(kind[:, mine].astype(F32)), axis=0, keepdims=True)
                vparts[1 - core, at + number : at + number + 1, :] = line
            for half in range(2):
                rows = slice(half * 16 + core * per, half * 16 + (core + 1) * per)
                cols = slice(half * LANES, (half + 1) * LANES)
                vparts[1 - core, 24 : 24 + per, cols] = tab[rows]
        Vectors(vparts, vland, small, bits, kit, vs_sem, vr_sem).run(0)
        poll()

        l_qkvw[0].wait()
        l_qkvw[1].wait()

        def token_tile(number, carry):
            cols = pl.ds(pl.multiple_of(number * 256, 256), 256)
            total = wide[:, cols]
            for core in range(2):
                for kind in range(3):
                    total = total + dot(
                        kinds[kind][:, core * inner : (core + 1) * inner],
                        qkvw[core, kind, cols, :],
                        NT,
                    )
            wide[:, cols] = total
            return carry

        lax.fori_loop(0, width // 256, token_tile, 0)

    pl.run_scoped(
        attend_phase,
        pltpu.VMEM((2,) + qkvw_h.shape, BF16),
        pltpu.VMEM((seq, width), BF16),
        pltpu.VMEM((width, seq), BF16),
        pltpu.VMEM((2 * inner, seq), BF16),
        pltpu.VMEM((2 * inner, seq), BF16),
        pltpu.VMEM((seq, 2 * inner), BF16),
        pltpu.VMEM((seq, 2 * inner), F32),
        pltpu.VMEM((seq, 2 * inner), F32),
        pltpu.VMEM((2 * inner, seq), BF16),
        pltpu.VMEM((seq, 2 * inner), BF16),
        pltpu.VMEM((seq, 2 * inner), BF16),
        pltpu.VMEM((seq, 2 * inner), BF16),
        pltpu.VMEM((heads, seq, 256), BF16),
        pltpu.VMEM((2 * seq * 16, LANES), F32),
    )
    done = pltpu.make_async_copy(wide, gtok_h, out_sem.at[0])
    done.start()
    last = polls[0]
    for number in range(last, max(plan) + 1):
        for piece, step in plan.get(number, ()):
            kit.pieces[piece].run(step)
    done.wait()
    for piece in kit.pieces:
        piece.finish()
    for copy in crossed[5:]:
        copy().wait_send()


def backward(plan, bits, saved, weights, others, tokens, sums2, gain1, bucket, length):
    seq, width = tokens.shape
    qkvw, outw, upw, downw = weights
    inner = qkvw.shape[2]
    units = upw.shape[1]
    heads = saved[-1].shape[0]
    shape = jax.ShapeDtypeStruct
    here = pl.BlockSpec(memory_space=pltpu.VMEM)
    away = pl.BlockSpec(memory_space=pl.ANY)
    scalar = pl.BlockSpec(memory_space=pltpu.SMEM)
    rows = (3 * width * inner + inner * width + 2 * width * units) // inner
    levels = min(4, bits)
    lands = rows - (rows >> levels) + (bits - levels) * (rows >> levels)
    slots = 9 * (2 * levels + bits - levels)
    return pl.pallas_call(
        functools.partial(backward_kernel, plan, bits),
        out_shape=(
            shape((rows, inner), BF16),
            shape((seq, width), F32),
            shape((32, inner), F32),
        ),
        in_specs=[away] * 22 + [here] * 3 + [scalar],
        out_specs=(away, away, here),
        scratch_shapes=[
            pltpu.VMEM((rows, inner), BF16),
            pltpu.VMEM((rows // 3, inner), BF16),
            pltpu.VMEM((rows, inner), BF16),
            pltpu.VMEM((lands, inner), BF16),
            pltpu.VMEM((seq, width), BF16),
            pltpu.VMEM((seq, width), F32),
            pltpu.VMEM((seq, width), F32),
            pltpu.VMEM((seq, LANES), F32),
            pltpu.VMEM((2 * inner, seq), BF16),
            pltpu.VMEM((2, inner, width), BF16),
            pltpu.VMEM((seq, width), BF16),
            pltpu.VMEM((seq, width), F32),
            pltpu.VMEM((seq, 2 * inner), BF16),
            pltpu.VMEM((seq, 2 * inner), BF16),
            pltpu.VMEM((seq, 2 * inner), BF16),
            pltpu.VMEM((heads, 8, seq), F32),
            pltpu.VMEM((2, 8, units), F32),
            pltpu.VMEM((bits + 1, 32, inner), F32),
            pltpu.VMEM((bits + 1, 32, inner), F32),
            pltpu.SemaphoreType.DMA((32,)),
            pltpu.SemaphoreType.DMA((1,)),
            pltpu.SemaphoreType.DMA((slots,)),
            pltpu.SemaphoreType.DMA((slots,)),
            pltpu.SemaphoreType.DMA((9,)),
            pltpu.SemaphoreType.DMA((9,)),
            pltpu.SemaphoreType.DMA((9,)),
            pltpu.SemaphoreType.DMA((bits + 1,)),
            pltpu.SemaphoreType.DMA((bits + 1,)),
        ],
        compiler_params=pltpu.CompilerParams(
            collective_id=1, has_side_effects=True, vmem_limit_bytes=VMEM_LIMIT
        ),
    )(*saved, qkvw, outw, upw, downw, *others, tokens, sums2, gain1, bucket, length)


def order_of_steps(levels, bits):
    late = []
    for step in range(1, 2 * levels + 1):
        late += [(number, step) for number in range(9)]
        if step <= bits + 1:
            late.append((9, step))
    for step in range(2 * levels + 1, bits + 2):
        late.append((9, step))
    return {64: tuple(late)}


def on_device(
    dp,
    tokens,
    qkv_weight,
    qv_bias,
    rel_table,
    out_weight,
    out_bias,
    norm1_gain,
    norm1_bias,
    up_weight,
    up_bias,
    down_weight,
    down_bias,
    norm2_gain,
    norm2_bias,
    rel_bucket,
    query_len,
    key_mask,
    upstream,
):
    width = tokens.shape[1]
    inner = qkv_weight.shape[2]
    units = up_weight.shape[1]
    qkvw = jnp.transpose(qkv_weight, (1, 0, 2))
    bucket = rel_bucket.T
    saved = forward(
        tokens,
        qkvw,
        qv_bias,
        rel_table.T,
        out_weight,
        out_bias,
        norm1_gain,
        norm1_bias,
        up_weight,
        up_bias.reshape(1, units),
        down_weight,
        down_bias,
        norm2_gain,
        norm2_bias,
        bucket,
        query_len,
        key_mask,
        upstream,
    )
    (
        out,
        gsec,
        gbr,
        act,
        slope,
        first,
        normed1,
        inverse1,
        heads_t,
        q,
        k,
        v,
        expo,
        recip,
        qkvw_o,
        outw_o,
        upw_o,
        downw_o,
        sums2,
    ) = saved
    bits = int(math.log2(dp))
    flat, grad_tokens, small = backward(
        order_of_steps(min(4, bits), bits),
        bits,
        (gbr, act, slope, first, gsec, normed1, inverse1, heads_t, q, k, v, expo, recip),
        (qkvw, out_weight, up_weight, down_weight),
        (qkvw_o, outw_o, upw_o, downw_o),
        tokens,
        sums2,
        norm1_gain,
        bucket.astype(BF16),
        query_len,
    )
    split = width // inner
    third = flat.shape[0] // 3
    down = flat[:third].reshape(units // 256, split, 256, inner)
    grad_down = jnp.transpose(down, (0, 2, 1, 3)).reshape(units, width).astype(F32)
    up = flat[third : 2 * third].reshape(units // inner, width, inner)
    grad_up = jnp.transpose(up, (1, 0, 2)).reshape(width, units).astype(F32)
    grad_out = flat[2 * third : 2 * third + split * inner].reshape(split, inner, inner)
    grad_out = jnp.transpose(grad_out, (1, 0, 2)).reshape(inner, width).astype(F32)
    grad_mix = flat[2 * third + split * inner :].reshape(3, width, inner)
    grad_mix = jnp.transpose(grad_mix, (1, 0, 2)).astype(F32)

    def vector(number):
        return small[number * split : (number + 1) * split].reshape(width)

    at = 6 * split
    heads = rel_table.shape[1]
    return (
        out,
        grad_tokens,
        grad_mix,
        small[at + units // inner : at + units // inner + 2],
        small[24 : 24 + heads, : 2 * LANES].T,
        grad_out,
        vector(0),
        vector(1),
        vector(2),
        grad_up,
        small[at : at + units // inner].reshape(units),
        grad_down,
        vector(3),
        vector(4),
        vector(5),
    )


def solution(mesh):
    rows = P(("dp", "tensor"), None)
    whole = P()
    in_specs = (
        rows,
        P(None, None, "tensor"),
        P(None, "tensor"),
        P(None, "tensor"),
        P("tensor", None),
        whole,
        whole,
        whole,
        P(None, "tensor"),
        P("tensor"),
        P("tensor", None),
        whole,
        whole,
        whole,
        whole,
        P("dp"),
        P("dp", None),
        rows,
    )
    out_specs = (
        rows,
        rows,
        P(None, None, "tensor"),
        P(None, "tensor"),
        P(None, "tensor"),
        P("tensor", None),
        whole,
        whole,
        whole,
        P(None, "tensor"),
        P("tensor"),
        P("tensor", None),
        whole,
        whole,
        whole,
    )
    return jax.shard_map(
        functools.partial(on_device, mesh.shape["dp"]),
        mesh=mesh,
        in_specs=in_specs,
        out_specs=out_specs,
        check_vma=False,
    )
```

```python
import functools
import math

import jax
import jax.numpy as jnp
from jax import lax
from jax.experimental import pallas as pl
from jax.experimental.pallas import tpu as pltpu
from jax.sharding import PartitionSpec as P

EPSILON = 1e-05
FAR_BELOW = -1000000000.0
MESH = pl.DeviceIdType.MESH
F32 = jnp.float32
BF16 = jnp.bfloat16
LANES = 128
NT = (((1,), (1,)), ((), ()))
TN = (((0,), (0,)), ((), ()))
VMEM_LIMIT = 62 * 2**20
ORDERS = {
    "down": ((1, "xyzZ"), (2, "yxzZ"), (3, "zZyx")),
    "up": ((1, "xyzZ"), (1, "yxzZ"), (1, "xyzZ"), (1, "yxzZ")),
    "out": "xyzZ",
    "mix": ("xyzZ", "yzZx", "xyzZ"),
}
PAUSES = {
    5: ((0, 1),),
    12: ((1, 1),),
    13: ((0, 2),),
    17: ((2, 1), (0, 3)),
    18: ((3, 1), (4, 1)),
    19: ((1, 2),),
    20: ((6, 1),),
    21: ((3, 2), (5, 1)),
    22: ((2, 2), (4, 2)),
    23: ((0, 4), (1, 3)),
    24: ((5, 2), (3, 3)),
    25: ((4, 3), (7, 1), (2, 3), (0, 5)),
    26: ((1, 4), (5, 3), (6, 2)),
    27: ((3, 4), (2, 4), (7, 2), (4, 4), (0, 6)),
    28: ((1, 5),),
    29: ((2, 5), (5, 4), (6, 3), (0, 7), (3, 5)),
    30: ((7, 3), (4, 5)),
    31: ((1, 6), (2, 6), (5, 5)),
    32: ((0, 8), (6, 4), (3, 6)),
    33: ((7, 4), (4, 6)),
    34: ((1, 7),),
    35: ((3, 7),),
    36: ((4, 7),),
    37: ((5, 6),),
    40: ((2, 7), (3, 8), (1, 8)),
    41: ((6, 5), (7, 5)),
    47: ((4, 8),),
    48: ((5, 7),),
    49: ((8, 1),),
    50: ((2, 8),),
    51: ((9, 1), (6, 6), (7, 6)),
    52: ((10, 1), (8, 2)),
    53: ((9, 2), (7, 7)),
    54: ((8, 3), (5, 8)),
    55: ((10, 2),),
    56: ((9, 3), (6, 7)),
    57: ((8, 4),),
    58: ((10, 3),),
}
TAIL = ((8, 5), (7, 8), (10, 4), (9, 4), (6, 8), (8, 6), (9, 5), (10, 5), (8, 7), (9, 6), (10, 6), (9, 7), (10, 7), (8, 8), (9, 8), (10, 8))


def dot(left, right, dims=None):
    if dims is None:
        return jnp.dot(left, right, preferred_element_type=F32)
    return lax.dot_general(left, right, dims, preferred_element_type=F32)


def other_core():
    return {"tensor": 1 - lax.axis_index("tensor")}


def row(ref):
    return ref[...].reshape(1, ref.shape[-1])


def fold8(block):
    return jnp.sum(block.reshape(block.shape[0] // 8, 8, block.shape[1]), axis=0)


def pack_tables(tab, packed):
    step = jnp.maximum(jnp.max(jnp.abs(tab[...])), 1e-30) / 32000.0
    inverse = 1.0 / step
    heads = tab.shape[1]
    for core in range(2):
        for pair in range(heads // 2):
            high = tab[core, 2 * pair : 2 * pair + 1, :] * inverse
            low = jnp.round(tab[core, 2 * pair + 1 : 2 * pair + 2, :] * inverse)
            high = jnp.round(high - low * (1 / 65536.0))
            both = high.astype(jnp.int32) * 65536 + low.astype(jnp.int32)
            packed[core * (heads // 2) + pair] = jnp.broadcast_to(both, packed.shape[1:])
    return step


def attend_pair(pair, q, k, vt, packed, bucket, valid, length, step, expo, heads_t, recip):
    seq = q.shape[0]
    cols = pl.ds(pl.multiple_of(pair * LANES, LANES), LANES)
    keys = k[:, cols]
    queries = q[:, cols]
    lane = lax.broadcasted_iota(jnp.int32, (seq, LANES), 1)
    in_query = lax.broadcasted_iota(jnp.int32, (seq, LANES), 0) < length
    terms = packed[pair, 0:1, :]
    near = jnp.broadcast_to(terms[:, :LANES], (seq, LANES))
    far = jnp.broadcast_to(terms[:, LANES:], (seq, LANES))
    same = jnp.where(in_query, far, near)
    swap = jnp.where(in_query, near, far)
    pieces = ([], [])
    for start in range(0, seq, LANES):
        index = bucket[:, start : start + LANES]
        got = jnp.take_along_axis(same, index, axis=1, mode="promise_in_bounds")
        if start == 0:
            turned = jnp.take_along_axis(swap, index, axis=1, mode="promise_in_bounds")
            got = jnp.where(lane < length, turned, got)
        pieces[0].append(got.astype(F32) * (step * (1 / 65536.0)))
        pieces[1].append(jnp.left_shift(got, 16).astype(F32) * (step * (1 / 65536.0)))
    first = lane < LANES // 2
    real = jnp.concatenate([valid[...] > 0] * (seq // LANES), axis=1)
    for side in range(2):
        mine = first if side == 0 else jnp.logical_not(first)
        scores = dot(jnp.where(mine, keys, jnp.zeros_like(keys)), queries, NT)
        scores = scores + jnp.concatenate(pieces[side], axis=1)
        scores = jnp.where(real, scores, FAR_BELOW)
        highest = jnp.max(scores, axis=0, keepdims=True)
        weights = jnp.exp(scores - highest).astype(BF16)
        expo[2 * pair + side] = weights
        rows = pl.ds(pl.multiple_of(pair * LANES + side * 64, 64), 64)
        values = jnp.concatenate([vt[rows, :], jnp.ones((16, seq), BF16)], axis=0)
        got = dot(values, weights)
        inverse = 1.0 / got[64:65]
        heads_t[rows, :] = (got[:64] * inverse).astype(BF16)
        recip[2 * pair + side] = jnp.broadcast_to(inverse, recip.shape[1:])


def forward_kernel(
    tokens_h,
    qkvw_h,
    qvb_h,
    tab_h,
    outw_h,
    upw_h,
    upb_h,
    downw_h,
    upstream_h,
    outb,
    gain1,
    shift1,
    downb,
    gain2,
    shift2,
    bucket,
    length,
    mask,
    out_h,
    gsec_h,
    gbr_h,
    act_h,
    slope_h,
    first_h,
    normed1_h,
    inverse1_h,
    heads_h,
    q_h,
    k_h,
    v_h,
    expo_h,
    recip_h,
    qkvw_o,
    outw_o,
    upw_o,
    downw_o,
    bucket_o,
    sums,
    tokens,
    qkvw,
    qvb,
    tab,
    outw,
    upw,
    upb,
    upb_other,
    upb_rows,
    downw,
    upstream,
    bucket_t,
    packed,
    valid,
    q,
    k,
    v,
    vt,
    heads_t,
    expo,
    recip,
    wide,
    first32,
    normed1,
    inverse1,
    first16,
    act,
    slope,
    gsec,
    gbr,
    out,
    in_sem,
    out_sem,
    send_sem,
    recv_sem,
):
    seq, width = tokens.shape
    inner = qkvw.shape[3]
    half_units = upw.shape[2]
    pairs = inner // LANES
    barrier = pltpu.get_barrier_semaphore()
    pl.semaphore_signal(barrier, inc=1, device_id=other_core(), device_id_type=MESH)

    loads = []
    for number, (source, target) in enumerate(
        (
            (tokens_h, tokens),
            (qkvw_h, qkvw.at[0]),
            (qvb_h, qvb.at[0]),
            (tab_h, tab.at[0]),
            (outw_h, outw.at[0]),
            (upw_h, upw.at[0]),
            (upb_h, upb),
            (downw_h, downw.at[0]),
            (upstream_h, upstream),
        )
    ):
        copy = pltpu.make_async_copy(source, target, in_sem.at[number])
        copy.start()
        loads.append(copy)

    pl.semaphore_wait(barrier, 1)
    sends = []
    for number, (source, target) in enumerate(
        (
            (qkvw_h, qkvw.at[1]),
            (qvb_h, qvb.at[1]),
            (tab_h, tab.at[1]),
            (outw_h, outw.at[1]),
            (upw_h, upw.at[1]),
            (upb_h, upb_other),
            (downw_h, downw.at[1]),
        )
    ):
        copy = pltpu.make_async_remote_copy(
            src_ref=source,
            dst_ref=target,
            send_sem=send_sem.at[number],
            recv_sem=recv_sem.at[number],
            device_id=other_core(),
            device_id_type=MESH,
        )
        copy.start()
        sends.append(copy)

    stores = []

    def store(source, target):
        copy = pltpu.make_async_copy(source, target, out_sem.at[len(stores)])
        copy.start()
        stores.append(copy)

    me = lax.axis_index("tensor")
    span = length[me]
    mine = mask[pl.ds(me, 1), :].astype(F32)
    valid[...] = jnp.transpose(jnp.broadcast_to(mine, (LANES, seq)))
    bucket_t[...] = jnp.transpose(bucket[...])
    bucket_o[...] = bucket_t[...].astype(BF16)

    def mix(core):
        rows = tokens[...]
        cols = slice(core * inner, (core + 1) * inner)
        query = dot(rows, qkvw[core, 0])
        q[:, cols] = ((query + qvb[core, 0:1, :]) * 0.125).astype(BF16)
        k[:, cols] = dot(rows, qkvw[core, 1]).astype(BF16)
        value = (dot(rows, qkvw[core, 2]) + qvb[core, 1:2, :]).astype(BF16)
        v[:, cols] = value
        vt[cols, :] = jnp.transpose(value)

    loads[0].wait()
    loads[1].wait()
    loads[2].wait()
    mix(0)
    loads[3].wait()
    sends[0].wait_recv()
    sends[1].wait_recv()
    sends[2].wait_recv()
    mix(1)
    step = pack_tables(tab, packed)
    store(q, q_h)
    store(k, k_h)
    store(v, v_h)
    store(qkvw.at[1], qkvw_o)

    def attend(pair, carry):
        attend_pair(pair, q, k, vt, packed, bucket_t, valid, span, step, expo, heads_t, recip)
        return carry

    lax.fori_loop(0, 2 * pairs, attend, 0)
    store(expo, expo_h)
    store(recip, recip_h)
    store(heads_t, heads_h)

    loads[4].wait()
    sends[3].wait_recv()
    store(outw.at[1], outw_o)
    lower = jnp.transpose(heads_t[...])

    def project(tile, carry):
        cols = pl.ds(pl.multiple_of(tile * 256, 256), 256)
        wide[:, cols] = dot(lower[:, :inner], outw[0, :, cols]) + dot(
            lower[:, inner:], outw[1, :, cols]
        )
        return carry

    lax.fori_loop(0, width // 256, project, 0)
    block = 128

    def norm_one(number, carry):
        rows = pl.ds(pl.multiple_of(number * block, block), block)
        value = wide[rows, :] + row(outb) + tokens[rows, :].astype(F32)
        center = value - jnp.mean(value, axis=-1, keepdims=True)
        inverse = lax.rsqrt(jnp.mean(center * center, axis=-1, keepdims=True) + EPSILON)
        normed = center * inverse
        result = normed * row(gain1) + row(shift1)
        normed1[rows, :] = normed
        inverse1[rows, :] = jnp.broadcast_to(inverse, (block, LANES))
        first32[rows, :] = result
        first16[rows, :] = result.astype(BF16)
        return carry

    lax.fori_loop(0, seq // block, norm_one, 0)
    store(first16, first_h)
    store(normed1, normed1_h)
    store(inverse1, inverse1_h)

    for core in range(2):
        if core == 0:
            loads[5].wait()
            loads[6].wait()
            upb_rows[0] = row(upb)
        else:
            sends[4].wait_recv()
            sends[5].wait_recv()
            upb_rows[1] = row(upb_other)
            store(upw.at[1], upw_o)

        def expand(tile, carry, core=core):
            cols = pl.ds(pl.multiple_of(tile * 256, 256), 256)
            here = pl.ds(pl.multiple_of(core * half_units + tile * 256, 256), 256)
            hidden = dot(first16[...], upw[core, :, cols]) + upb_rows[core, :, cols]
            chance = 0.5 * (1.0 + lax.erf(hidden * math.sqrt(0.5)))
            density = jnp.exp(hidden * hidden * -0.5) * (1.0 / math.sqrt(2.0 * math.pi))
            act[:, here] = (hidden * chance).astype(BF16)
            slope[:, here] = (chance + hidden * density).astype(BF16)
            return carry

        lax.fori_loop(0, half_units // 256, expand, 0)
    store(act, act_h)
    store(slope, slope_h)
    loads[7].wait()
    sends[6].wait_recv()
    store(downw.at[1], downw_o)

    def reduce_units(tile, carry):
        cols = pl.ds(pl.multiple_of(tile * 256, 256), 256)
        wide[:, cols] = dot(act[:, :half_units], downw[0, :, cols]) + dot(
            act[:, half_units:], downw[1, :, cols]
        )
        return carry

    lax.fori_loop(0, width // 256, reduce_units, 0)
    loads[8].wait()

    def norm_two(number, carry):
        rows = pl.ds(pl.multiple_of(number * block, block), block)
        value = wide[rows, :] + row(downb) + first32[rows, :]
        center = value - jnp.mean(value, axis=-1, keepdims=True)
        inverse = lax.rsqrt(jnp.mean(center * center, axis=-1, keepdims=True) + EPSILON)
        normed = center * inverse
        out[rows, :] = (normed * row(gain2) + row(shift2)).astype(BF16)
        grad = upstream[rows, :].astype(F32)
        scaled = grad * row(gain2)
        back = inverse * (
            scaled
            - jnp.mean(scaled, axis=-1, keepdims=True)
            - normed * jnp.mean(scaled * normed, axis=-1, keepdims=True)
        )
        gsec[rows, :] = back
        gbr[rows, :] = back.astype(BF16)
        return (
            carry[0] + fold8(grad * normed),
            carry[1] + fold8(grad),
            carry[2] + fold8(back),
        )

    zero = jnp.zeros((8, width), F32)
    totals = lax.fori_loop(0, seq // block, norm_two, (zero, zero, zero))
    for number, total in enumerate(totals):
        sums[number : number + 1, :] = jnp.sum(total, axis=0, keepdims=True)
    sums[3:, :] = jnp.zeros((5, width), F32)
    store(out, out_h)
    store(gsec, gsec_h)
    store(gbr, gbr_h)
    for copy in stores:
        copy.wait()
    for copy in sends:
        copy.wait_send()


def forward(
    tokens,
    qkvw,
    qvb,
    tab,
    outw,
    outb,
    gain1,
    shift1,
    upw,
    upb,
    downw,
    downb,
    gain2,
    shift2,
    bucket,
    length,
    mask,
    upstream,
):
    seq, width = tokens.shape
    inner = qkvw.shape[2]
    units = upw.shape[1]
    heads = 2 * tab.shape[0]
    shape = jax.ShapeDtypeStruct
    here = pl.BlockSpec(memory_space=pltpu.VMEM)
    away = pl.BlockSpec(memory_space=pl.ANY)
    scalar = pl.BlockSpec(memory_space=pltpu.SMEM)
    out_shape = (
        shape((seq, width), BF16),
        shape((seq, width), F32),
        shape((seq, width), BF16),
        shape((seq, 2 * units), BF16),
        shape((seq, 2 * units), BF16),
        shape((seq, width), BF16),
        shape((seq, width), F32),
        shape((seq, LANES), F32),
        shape((2 * inner, seq), BF16),
        shape((seq, 2 * inner), BF16),
        shape((seq, 2 * inner), BF16),
        shape((seq, 2 * inner), BF16),
        shape((heads, seq, seq), BF16),
        shape((heads, 8, seq), F32),
        shape(qkvw.shape, BF16),
        shape(outw.shape, BF16),
        shape(upw.shape, BF16),
        shape(downw.shape, BF16),
        shape((seq, seq), BF16),
        shape((8, width), F32),
    )
    scratch = [
        pltpu.VMEM((seq, width), BF16),
        pltpu.VMEM((2,) + qkvw.shape, BF16),
        pltpu.VMEM((2,) + qvb.shape, F32),
        pltpu.VMEM((2,) + tab.shape, F32),
        pltpu.VMEM((2,) + outw.shape, BF16),
        pltpu.VMEM((2,) + upw.shape, BF16),
        pltpu.VMEM(upb.shape, F32),
        pltpu.VMEM(upb.shape, F32),
        pltpu.VMEM((2, 1, units), F32),
        pltpu.VMEM((2,) + downw.shape, BF16),
        pltpu.VMEM((seq, width), BF16),
        pltpu.VMEM((seq, seq), jnp.int32),
        pltpu.VMEM((heads // 2, 8, 2 * LANES), jnp.int32),
        pltpu.VMEM((seq, LANES), F32),
        pltpu.VMEM((seq, 2 * inner), BF16),
        pltpu.VMEM((seq, 2 * inner), BF16),
        pltpu.VMEM((seq, 2 * inner), BF16),
        pltpu.VMEM((2 * inner, seq), BF16),
        pltpu.VMEM((2 * inner, seq), BF16),
        pltpu.VMEM((heads, seq, seq), BF16),
        pltpu.VMEM((heads, 8, seq), F32),
        pltpu.VMEM((seq, width), F32),
        pltpu.VMEM((seq, width), F32),
        pltpu.VMEM((seq, width), F32),
        pltpu.VMEM((seq, LANES), F32),
        pltpu.VMEM((seq, width), BF16),
        pltpu.VMEM((seq, 2 * units), BF16),
        pltpu.VMEM((seq, 2 * units), BF16),
        pltpu.VMEM((seq, width), F32),
        pltpu.VMEM((seq, width), BF16),
        pltpu.VMEM((seq, width), BF16),
        pltpu.SemaphoreType.DMA((9,)),
        pltpu.SemaphoreType.DMA((20,)),
        pltpu.SemaphoreType.DMA((7,)),
        pltpu.SemaphoreType.DMA((7,)),
    ]
    return pl.pallas_call(
        forward_kernel,
        out_shape=out_shape,
        in_specs=[away] * 9 + [here] * 7 + [scalar, here],
        out_specs=(away,) * 18 + (here, here),
        scratch_shapes=scratch,
        compiler_params=pltpu.CompilerParams(
            collective_id=0, has_side_effects=True, vmem_limit_bytes=VMEM_LIMIT
        ),
    )(
        tokens,
        qkvw,
        qvb,
        tab,
        outw,
        upw,
        upb,
        downw,
        upstream,
        outb,
        gain1,
        shift1,
        downb,
        gain2,
        shift2,
        bucket,
        length,
        mask,
    )


def dp_side(bit):
    return lax.rem(lax.axis_index("dp") // (1 << bit), 2)


def dp_partner(bit):
    return {"dp": lax.axis_index("dp") + (1 - 2 * dp_side(bit)) * (1 << bit)}


def flat_rows(start, size):
    return pl.ds(pl.multiple_of(start, 16), size)


class Kit:
    def __init__(self, acc, landing, result, send_sem, recv_sem, local_sem):
        self.acc, self.landing, self.result = acc, landing, result
        self.send_sem, self.recv_sem, self.local_sem = send_sem, recv_sem, local_sem
        self.used = 0
        self.landed = 0
        self.pieces = []

    def slot(self):
        self.used += 1
        return self.used - 1

    def room(self, size):
        self.landed += size
        return self.landed - size

    def remote(self, slot, source, target, device):
        return pltpu.make_async_remote_copy(
            src_ref=source,
            dst_ref=target,
            send_sem=self.send_sem.at[slot],
            recv_sem=self.recv_sem.at[slot],
            device_id=device,
            device_id_type=MESH,
        )


class Piece:
    def __init__(self, start, length, order, extra, kit):
        self.start, self.length = start, length
        self.bits, self.extra = order, extra
        self.kit = kit
        self.number = len(kit.pieces)
        self.steps = 2 * len(order) + 1
        kit.pieces.append(self)
        self.halving = [
            (kit.slot(), kit.room(length >> (level + 1))) for level in range(len(order))
        ]
        self.crossing = [(kit.slot(), kit.room(length >> len(order))) for _ in extra]
        self.spreading = [kit.slot() for _ in order]

    def begin(self, levels):
        at = self.start
        for level in range(levels):
            at = at + dp_side(self.bits[level]) * (self.length >> (level + 1))
        return at

    def halve(self, level):
        kit, bit = self.kit, self.bits[level]
        slot, room = self.halving[level]
        size = self.length >> (level + 1)
        away = self.begin(level) + (1 - dp_side(bit)) * size
        return kit.remote(
            slot,
            kit.acc.at[flat_rows(away, size), :],
            kit.landing.at[pl.ds(room, size), :],
            dp_partner(bit),
        )

    def swap(self, number):
        kit = self.kit
        slot, room = self.crossing[number]
        size = self.length >> len(self.bits)
        return kit.remote(
            slot,
            kit.acc.at[flat_rows(self.begin(len(self.bits)), size), :],
            kit.landing.at[pl.ds(room, size), :],
            dp_partner(self.extra[number]),
        )

    def keep(self):
        kit, levels = self.kit, len(self.bits)
        mine = flat_rows(self.begin(levels), self.length >> levels)
        return pltpu.make_async_copy(
            kit.acc.at[mine, :], kit.result.at[mine, :], kit.local_sem.at[self.number]
        )

    def spread(self, number):
        kit = self.kit
        level = len(self.bits) - number
        mine = flat_rows(self.begin(level), self.length >> level)
        source = kit.acc if number == 0 else kit.result
        return kit.remote(
            self.spreading[number],
            source.at[mine, :],
            kit.result.at[mine, :],
            dp_partner(self.bits[level - 1]),
        )

    def add(self, target, source, size):
        kit = self.kit
        chunk = math.gcd(size, 192)

        def some(number, carry):
            there = flat_rows(target + number * chunk, chunk)
            here = flat_rows(source + number * chunk, chunk)
            total = kit.acc[there, :].astype(F32) + kit.landing[here, :].astype(F32)
            kit.acc[there, :] = total.astype(BF16)
            return carry

        lax.fori_loop(0, size // chunk, some, 0)

    def run(self, step):
        levels = len(self.bits)
        if 0 < step <= levels:
            self.halve(step - 1).wait_recv()
            self.add(self.begin(step), self.halving[step - 1][1], self.length >> step)
        if step < levels:
            self.halve(step).start()
            return
        if step == levels:
            for number in range(len(self.extra)):
                both = self.swap(number)
                both.start()
                both.wait()
                self.add(self.begin(levels), self.crossing[number][1], self.length >> levels)
            self.keep().start()
        else:
            self.spread(step - levels - 1).wait_recv()
            if step == levels + 1:
                self.keep().wait()
        if step < 2 * levels:
            self.spread(step - levels).start()

    def finish(self):
        for level in range(len(self.bits)):
            self.halve(level).wait_send()
            self.spread(level).wait_send()


class Vectors:
    def __init__(self, parts, landing, result, bits, kit, send_sem, recv_sem):
        self.parts, self.landing, self.result = parts, landing, result
        self.bits = bits
        self.steps = bits + 2
        self.send_sem, self.recv_sem = send_sem, recv_sem
        kit.pieces.append(self)

    def exchange(self, step):
        return pltpu.make_async_remote_copy(
            src_ref=self.parts.at[step],
            dst_ref=self.landing.at[step],
            send_sem=self.send_sem.at[step],
            recv_sem=self.recv_sem.at[step],
            device_id=other_core() if step == 0 else dp_partner(step - 1),
            device_id_type=MESH,
        )

    def run(self, step):
        if step > 0:
            self.exchange(step - 1).wait_recv()
            total = self.parts[max(step - 1, 1)] + self.landing[step - 1]
            if step <= self.bits:
                self.parts[step] = total
            else:
                self.result[...] = total
        if step <= self.bits:
            self.exchange(step).start()

    def finish(self):
        for step in range(self.bits + 1):
            self.exchange(step).wait_send()


def backward_kernel(
    plan,
    bits,
    gbr_h,
    act_h,
    slope_h,
    first_h,
    gsec_h,
    normed1_h,
    inverse1_h,
    heads_h,
    q_h,
    k_h,
    v_h,
    expo_h,
    recip_h,
    qkvw_h,
    outw_h,
    upw_h,
    downw_h,
    qkvw_o,
    outw_o,
    upw_o,
    downw_o,
    tokens_h,
    sums2,
    gain1,
    bucket,
    length,
    result_h,
    gtok_h,
    small,
    acc,
    xsend,
    xrecv,
    landing,
    gbr,
    gsec,
    normed1,
    inverse1,
    heads_t,
    outw,
    gmid16,
    wide,
    q,
    k,
    v,
    recip,
    ups,
    vparts,
    vland,
    in_sem,
    out_sem,
    send_sem,
    recv_sem,
    local_sem,
    xs_sem,
    xr_sem,
    vs_sem,
    vr_sem,
):
    seq, width = gsec.shape
    inner = outw.shape[1]
    units = upw_h.shape[1]
    heads = recip.shape[0]
    levels = 4

    barrier = pltpu.get_barrier_semaphore()
    pl.semaphore_signal(barrier, inc=1, device_id=other_core(), device_id_type=MESH)
    for bit in range(bits):
        pl.semaphore_signal(barrier, inc=1, device_id=dp_partner(bit), device_id_type=MESH)

    used = []

    def load(source, target):
        copy = pltpu.make_async_copy(source, target, in_sem.at[len(used)])
        used.append(copy)
        copy.start()
        return copy

    kit = Kit(acc, landing, result_h, send_sem, recv_sem, local_sem)
    extra = tuple(range(levels, bits))
    crossed = []

    def cross(start, size, place):
        number = len(crossed)

        def copy():
            return pltpu.make_async_remote_copy(
                src_ref=xsend.at[pl.ds(place, size), :],
                dst_ref=xrecv.at[pl.ds(start, size), :],
                send_sem=xs_sem.at[number],
                recv_sem=xr_sem.at[number],
                device_id=other_core(),
                device_id_type=MESH,
            )

        copy().start()
        crossed.append(copy)

    polls = [0]

    def run_steps(number):
        for piece, step in plan.get(number, ()):
            kit.pieces[piece].run(step)

    def poll():
        run_steps(polls[0])
        polls[0] += 1

    def polled_loop(low, high, body, initial, every=1):
        start = polls[0]
        pauses = (high - low) // every
        polls[0] += pauses
        busy = [number for number in range(pauses) if plan.get(start + number)]

        def turn(index, carry):
            carry = body(index, carry)
            for number in busy:

                @pl.when(index == low + (number + 1) * every - 1)
                def _():
                    run_steps(start + number)

            return carry

        return lax.fori_loop(low, high, turn, initial)

    def begin_piece(start, size, order):
        fresh = Piece(start, size, tuple("xyzZ".index(axis) for axis in order), extra, kit)
        fresh.run(0)

    def give(place, tile):
        xsend[flat_rows(place, tile.shape[0]), :] = tile.astype(BF16)

    def take(start, tile):
        there = flat_rows(start, tile.shape[0])
        acc[there, :] = (tile + xrecv[there, :].astype(F32)).astype(BF16)

    third = acc.shape[0] // 3
    split = width // inner

    def unit_phase(act, slope, downw, upw, first, first_t):
        l_gbr = load(gbr_h, gbr)
        l_act = [None, load(act_h.at[:, pl.ds(units, units)], act.at[:, pl.ds(units, units)])]
        l_act[0] = load(act_h.at[:, pl.ds(0, units)], act.at[:, pl.ds(0, units)])
        l_down = [None, load(downw_o, downw.at[1])]
        l_slope = load(slope_h, slope)
        l_down[0] = load(downw_h, downw.at[0])
        l_first = load(first_h, first)
        l_up = [load(upw_h, upw.at[0]), load(upw_o, upw.at[1])]
        l_late = [
            load(source, target)
            for source, target in (
                (gsec_h, gsec),
                (normed1_h, normed1),
                (inverse1_h, inverse1),
                (heads_h, heads_t),
                (outw_h, outw.at[0]),
                (outw_o, outw.at[1]),
                (recip_h, recip),
                (q_h, q),
                (k_h, k),
                (v_h, v),
            )
        ]
        pl.semaphore_wait(barrier, 1 + bits)

        tiles = units // 256
        span = 256 * split
        l_gbr.wait()
        for core in (1, 0):
            l_act[core].wait()
            low = 0
            for part, (count, order) in enumerate(ORDERS["down"]):
                if core == 0:
                    crossed[part]().wait_recv()

                def down_tile(number, carry, core=core):
                    cols = pl.ds(pl.multiple_of(core * units + number * 256, 256), 256)
                    tile = dot(act[:, cols], gbr[...], TN)
                    for side in range(split):
                        (give if core == 1 else take)(
                            number * span + side * 256,
                            tile[:, side * inner : (side + 1) * inner],
                        )
                    return carry

                lax.fori_loop(low, low + count, down_tile, 0)
                if core == 1:
                    cross(low * span, count * span, low * span)
                else:
                    begin_piece(low * span, count * span, order)
                    poll()
                low += count
        fed = len(crossed)

        l_slope.wait()
        for core in (1, 0):
            l_down[core].wait()

            def slope_tile(number, carry, core=core):
                here = pl.ds(pl.multiple_of(number * 256, 256), 256)
                cols = pl.ds(pl.multiple_of(core * units + number * 256, 256), 256)
                tile = dot(gbr[...], downw[core, here, :], NT) * slope[:, cols].astype(F32)
                tile = tile.astype(BF16)
                slope[:, cols] = tile
                ups[core, :, here] = fold8(tile.astype(F32))
                return carry

            polled_loop(0, tiles, slope_tile, 0, tiles // 2)

        l_first.wait()
        first_t[...] = jnp.transpose(first[...])
        for copy in crossed[:fed]:
            copy().wait_send()
        for core in (1, 0):
            low = 0
            for part, (count, order) in enumerate(ORDERS["up"]):
                if core == 0:
                    crossed[fed + part]().wait_recv()

                def up_tile(number, carry, core=core):
                    cols = pl.ds(pl.multiple_of(core * units + number * inner, LANES), inner)
                    for top in range(0, width, 256):
                        tile = dot(first_t[top : top + 256, :], slope[:, cols])
                        if core == 1:
                            give(number * width + top, tile)
                        else:
                            take(third + number * width + top, tile)
                    return carry

                lax.fori_loop(low, low + count, up_tile, 0)
                if core == 1:
                    cross(third + low * width, count * width, low * width)
                else:
                    begin_piece(third + low * width, count * width, order)
                poll()
                low += count
        l_up[0].wait()
        l_up[1].wait()
        l_late[0].wait()

        def first_tile(number, carry):
            cols = pl.ds(pl.multiple_of(number * 256, 256), 256)
            wide[:, cols] = (
                gsec[:, cols]
                + dot(slope[:, :units], upw[0, cols, :], NT)
                + dot(slope[:, units:], upw[1, cols, :], NT)
            )
            return carry

        polled_loop(0, width // 256, first_tile, 0)
        for copy in l_late[1:]:
            copy.wait()

    pl.run_scoped(
        unit_phase,
        pltpu.VMEM((seq, 2 * units), BF16),
        pltpu.VMEM((seq, 2 * units), BF16),
        pltpu.VMEM((2, units, width), BF16),
        pltpu.VMEM((2, width, units), BF16),
        pltpu.VMEM((seq, width), BF16),
        pltpu.VMEM((width, seq), BF16),
    )

    block = 128

    def norm_one(number, carry):
        rows = pl.ds(pl.multiple_of(number * block, block), block)
        grad = wide[rows, :]
        normed = normed1[rows, :]
        scaled = grad * row(gain1)
        back = inverse1[rows, 0:1] * (
            scaled
            - jnp.mean(scaled, axis=-1, keepdims=True)
            - normed * jnp.mean(scaled * normed, axis=-1, keepdims=True)
        )
        wide[rows, :] = back
        gmid16[rows, :] = back.astype(BF16)
        return (
            carry[0] + fold8(back),
            carry[1] + fold8(grad * normed),
            carry[2] + fold8(grad),
        )

    zero = jnp.zeros((8, width), F32)
    totals = lax.fori_loop(0, seq // block, norm_one, (zero, zero, zero))
    both = [jnp.sum(total, axis=0, keepdims=True) for total in totals]
    both += [sums2[2:3, :], sums2[0:1, :], sums2[1:2, :]]
    vparts[0] = jnp.zeros(vparts.shape[1:], F32)
    vparts[1] = jnp.zeros(vparts.shape[1:], F32)
    for number, line in enumerate(both):
        vparts[0, number : number + 1, :] = line
        vparts[1, number : number + 1, :] = line
    for core in range(2):
        line = jnp.sum(ups[core], axis=0, keepdims=True)
        for side in range(units // width):
            vparts[1 - core, 6 + side : 7 + side, :] = line[:, side * width : (side + 1) * width]
    poll()

    def attend_phase(
        qkvw, tokens, tokens_t, kt, dheads_t, dheads, dk, dv, gq_t, gq, gk, gv, expo, spread
    ):
        columns = 256
        l_qkvw = [load(qkvw_h, qkvw.at[0]), load(qkvw_o, qkvw.at[1])]
        l_tokens = load(tokens_h, tokens)
        l_expo = load(expo_h.at[:, :, pl.ds(0, columns)], expo)

        full = len(crossed)
        for copy in crossed[full - len(ORDERS["up"]) :]:
            copy().wait_send()
        at = 2 * third
        for core in (1, 0):
            tile = dot(heads_t[core * inner : (core + 1) * inner, :], gmid16[...])
            if core == 0:
                crossed[full]().wait_recv()
            for side in range(split):
                part = tile[:, side * inner : (side + 1) * inner]
                if core == 1:
                    give(side * inner, part)
                else:
                    take(at + side * inner, part)
            if core == 1:
                cross(at, split * inner, 0)
            else:
                begin_piece(at, split * inner, ORDERS["out"])
        poll()
        per = heads // 2
        size = inner // per
        for core in range(2):
            tile = dot(outw[core], gmid16[...], NT)
            for head in range(per):
                rows = slice(core * inner + head * size, core * inner + (head + 1) * size)
                part = tile[head * size : (head + 1) * size] * recip[core * per + head, 0:1, :]
                dheads_t[rows, :] = part.astype(BF16)
        dheads[...] = jnp.transpose(dheads_t[...])
        kt[...] = jnp.transpose(k[...])
        poll()

        span = length[lax.axis_index("tensor")]
        lane = lax.broadcasted_iota(jnp.int32, (seq, LANES), 1)
        first = lane < size
        labels = lax.broadcasted_iota(jnp.int32, (LANES, columns), 0).astype(BF16)
        tab = jnp.zeros((32, LANES), F32)
        for part in range(seq // columns):
            start = part * columns
            here = slice(start, start + columns)
            l_expo.wait()

            def pair_back(pair, carry, here=here, part=part):
                cols = pl.ds(pl.multiple_of(pair * LANES, LANES), LANES)
                values, queries = v[:, cols], q[here, cols]
                grads, grads_t = dheads[here, cols], dheads_t[cols, here]
                gvs, gks = [], []
                for side in range(2):
                    head = 2 * pair + side
                    mine = first if side == 0 else jnp.logical_not(first)
                    back = dot(jnp.where(mine, values, jnp.zeros_like(values)), grads_t)
                    chance = expo[head].astype(F32)
                    product = chance * back
                    shift = jnp.sum(product, axis=0, keepdims=True) * recip[head, 0:1, here]
                    gscore = product - chance * shift
                    for half in range(columns // LANES):
                        spread[pl.ds(half * seq * 16 + head, seq, stride=16), :] = gscore[
                            :, half * LANES : (half + 1) * LANES
                        ]
                    gscore = gscore.astype(BF16)
                    gvs.append(dot(expo[head], grads))
                    gks.append(dot(gscore, queries))
                    rows = pl.ds(pl.multiple_of(pair * LANES + side * size, size), size)
                    gq_t[rows, here] = (dot(kt[rows, :], gscore) * 0.125).astype(BF16)
                gvalue = jnp.where(first, gvs[0], gvs[1])
                gkey = jnp.where(first, gks[0], gks[1])
                if part == 0:
                    dv[:, cols] = gvalue
                    dk[:, cols] = gkey
                else:
                    gv[:, cols] = (dv[:, cols] + gvalue).astype(BF16)
                    gk[:, cols] = (dk[:, cols] + gkey).astype(BF16)
                return carry

            polled_loop(0, heads // 2, pair_back, 0)
            if part + 1 < seq // columns:
                l_expo = load(expo_h.at[:, :, pl.ds(start + columns, columns)], expo)

            position = lax.broadcasted_iota(jnp.int32, (1, columns), 1) + start
            inside = (position < span).astype(F32)

            def count(number, carry, here=here, inside=inside):
                rows = pl.ds(pl.multiple_of(number * 16, 16), 16)
                index = bucket[rows, here]
                grads = jnp.concatenate(
                    [
                        spread[pl.ds(pl.multiple_of(half * seq * 16 + number * 256, 256), 256), :]
                        for half in range(columns // LANES)
                    ],
                    axis=1,
                )
                for line in range(16):
                    hot = jnp.where(
                        labels == index[line : line + 1, :],
                        jnp.ones((), BF16),
                        jnp.zeros((), BF16),
                    )
                    other = jnp.where(number * 16 + line < span, 1.0 - inside, inside)
                    some = grads[16 * line : 16 * line + 16]
                    far = some * other
                    both = jnp.concatenate([some - far, far], axis=0).astype(BF16)
                    carry = carry + dot(both, hot, NT)
                return carry

            if part + 1 < seq // columns:
                tab = polled_loop(0, seq // 16, count, tab, 4)

        gq[...] = jnp.transpose(gq_t[...])
        l_tokens.wait()
        tokens_t[...] = jnp.transpose(tokens[...])
        at = 2 * third + split * inner
        kinds = (gq, gk, gv)
        for core in (1, 0):
            for kind in range(3):
                if core == 0:
                    crossed[full + 1 + kind]().wait_recv()
                for top in range(0, width, 256):
                    tile = dot(
                        tokens_t[top : top + 256, :],
                        kinds[kind][:, core * inner : (core + 1) * inner],
                    )
                    if core == 1:
                        give(split * inner + kind * width + top, tile)
                    else:
                        take(at + kind * width + top, tile)
                if core == 1:
                    cross(at + kind * width, width, split * inner + kind * width)
                else:
                    begin_piece(at + kind * width, width, ORDERS["mix"][kind])
                poll()

        tab = polled_loop(0, seq // 16, count, tab, 4)

        for core in range(2):
            mine = slice(core * inner, (core + 1) * inner)
            for number, kind in ((0, gq), (1, gv)):
                line = jnp.sum(fold8(kind[:, mine].astype(F32)), axis=0, keepdims=True)
                vparts[1 - core, 8:9, number * inner : (number + 1) * inner] = line
            for half in range(2):
                rows = slice(half * 16 + core * per, half * 16 + (core + 1) * per)
                cols = slice(half * LANES, (half + 1) * LANES)
                vparts[1 - core, 10 : 10 + per, cols] = tab[rows]
        Vectors(vparts, vland, small, bits, kit, vs_sem, vr_sem).run(0)
        poll()

        l_qkvw[0].wait()
        l_qkvw[1].wait()

        def token_tile(number, carry):
            cols = pl.ds(pl.multiple_of(number * 256, 256), 256)
            total = wide[:, cols]
            for core in range(2):
                for kind in range(3):
                    total = total + dot(
                        kinds[kind][:, core * inner : (core + 1) * inner],
                        qkvw[core, kind, cols, :],
                        NT,
                    )
            wide[:, cols] = total
            return carry

        polled_loop(0, width // 256, token_tile, 0)

    pl.run_scoped(
        attend_phase,
        pltpu.VMEM((2,) + qkvw_h.shape, BF16),
        pltpu.VMEM((seq, width), BF16),
        pltpu.VMEM((width, seq), BF16),
        pltpu.VMEM((2 * inner, seq), BF16),
        pltpu.VMEM((2 * inner, seq), BF16),
        pltpu.VMEM((seq, 2 * inner), BF16),
        pltpu.VMEM((seq, 2 * inner), F32),
        pltpu.VMEM((seq, 2 * inner), F32),
        pltpu.VMEM((2 * inner, seq), BF16),
        pltpu.VMEM((seq, 2 * inner), BF16),
        pltpu.VMEM((seq, 2 * inner), BF16),
        pltpu.VMEM((seq, 2 * inner), BF16),
        pltpu.VMEM((heads, seq, 256), BF16),
        pltpu.VMEM((2 * seq * 16, LANES), F32),
    )
    done = pltpu.make_async_copy(wide, gtok_h, out_sem.at[0])
    done.start()
    run_steps("tail")
    done.wait()
    for piece in kit.pieces:
        piece.finish()
    for copy in crossed[-4:]:
        copy().wait_send()


def backward(plan, bits, saved, weights, others, tokens, sums2, gain1, bucket, length):
    seq, width = tokens.shape
    qkvw, outw, upw, downw = weights
    inner = qkvw.shape[2]
    units = upw.shape[1]
    heads = saved[-1].shape[0]
    shape = jax.ShapeDtypeStruct
    here = pl.BlockSpec(memory_space=pltpu.VMEM)
    away = pl.BlockSpec(memory_space=pl.ANY)
    scalar = pl.BlockSpec(memory_space=pltpu.SMEM)
    rows = (3 * width * inner + inner * width + 2 * width * units) // inner
    levels = 4
    lands = rows - (rows >> levels) + (bits - levels) * (rows >> levels)
    pieces = len(ORDERS["down"]) + len(ORDERS["up"]) + 4
    slots = pieces * (2 * levels + bits - levels)
    return pl.pallas_call(
        functools.partial(backward_kernel, plan, bits),
        out_shape=(
            shape((rows, inner), BF16),
            shape((seq, width), F32),
            shape((16, width), F32),
        ),
        in_specs=[away] * 22 + [here] * 3 + [scalar],
        out_specs=(away, away, here),
        scratch_shapes=[
            pltpu.VMEM((rows, inner), BF16),
            pltpu.VMEM((rows // 3, inner), BF16),
            pltpu.VMEM((rows, inner), BF16),
            pltpu.VMEM((lands, inner), BF16),
            pltpu.VMEM((seq, width), BF16),
            pltpu.VMEM((seq, width), F32),
            pltpu.VMEM((seq, width), F32),
            pltpu.VMEM((seq, LANES), F32),
            pltpu.VMEM((2 * inner, seq), BF16),
            pltpu.VMEM((2, inner, width), BF16),
            pltpu.VMEM((seq, width), BF16),
            pltpu.VMEM((seq, width), F32),
            pltpu.VMEM((seq, 2 * inner), BF16),
            pltpu.VMEM((seq, 2 * inner), BF16),
            pltpu.VMEM((seq, 2 * inner), BF16),
            pltpu.VMEM((heads, 8, seq), F32),
            pltpu.VMEM((2, 8, units), F32),
            pltpu.VMEM((bits + 1, 16, width), F32),
            pltpu.VMEM((bits + 1, 16, width), F32),
            pltpu.SemaphoreType.DMA((32,)),
            pltpu.SemaphoreType.DMA((1,)),
            pltpu.SemaphoreType.DMA((slots,)),
            pltpu.SemaphoreType.DMA((slots,)),
            pltpu.SemaphoreType.DMA((pieces,)),
            pltpu.SemaphoreType.DMA((pieces,)),
            pltpu.SemaphoreType.DMA((pieces,)),
            pltpu.SemaphoreType.DMA((bits + 1,)),
            pltpu.SemaphoreType.DMA((bits + 1,)),
        ],
        compiler_params=pltpu.CompilerParams(
            collective_id=1, has_side_effects=True, vmem_limit_bytes=VMEM_LIMIT
        ),
    )(*saved, qkvw, outw, upw, downw, *others, tokens, sums2, gain1, bucket, length)


def finish_kernel(
    flat_h,
    out_h,
    gtok_h,
    small,
    out_f,
    gtok_f,
    mix_f,
    gqv,
    gtab,
    gout_f,
    goutb,
    gain1,
    shift1,
    up_f,
    gupb,
    down_f,
    gdownb,
    gain2,
    shift2,
    flat,
    mix,
    gout,
    up,
    down,
    gtok,
    out,
    in_sem,
    out_sem,
):
    rows, inner = flat.shape
    units, width = down.shape
    split = width // inner
    third = rows // 3
    copies = []
    tiles = units // 256
    span = 256 * split
    sizes = (
        [span] * tiles + [width] * (units // inner) + [split * inner] + [width] * 3
    )
    loads = []
    at = 0
    for number, size in enumerate(sizes):
        here = pl.ds(at, size)
        loads.append(pltpu.make_async_copy(flat_h.at[here, :], flat.at[here, :], in_sem.at[number]))
        loads[-1].start()
        at += size

    for source, target in ((gtok_h, gtok), (out_h, out)):
        loads.append(pltpu.make_async_copy(source, target, in_sem.at[len(loads)]))
        loads[-1].start()

    def store(source, target):
        copies.append(pltpu.make_async_copy(source, target, out_sem.at[len(copies)]))
        copies[-1].start()

    def wide(start, size):
        return flat[start : start + size, :].astype(F32)

    for tile in range(tiles):
        loads[tile].wait()
        here = slice(tile * 256, tile * 256 + 256)
        for side in range(split):
            down[here, side * inner : (side + 1) * inner] = wide(tile * span + side * 256, 256)
        here = pl.ds(tile * 256, 256)
        store(down.at[here, :], down_f.at[here, :])
    for part in range(units // inner):
        loads[tiles + part].wait()
        cols = pl.ds(part * inner, inner)
        up[:, cols] = wide(third + part * width, width)
        store(up.at[:, cols], up_f.at[:, cols])
    at = 2 * third
    loads[-6].wait()
    for side in range(split):
        gout[:, side * inner : (side + 1) * inner] = wide(at + side * inner, inner)
    store(gout, gout_f)
    at += split * inner
    for kind in range(3):
        loads[kind - 5].wait()
        mix[kind] = wide(at + kind * width, width)
        store(mix.at[kind], mix_f.at[kind])
    loads[-2].wait()
    store(gtok, gtok_f)
    loads[-1].wait()
    store(out, out_f)
    for number, vector in enumerate((goutb, gain1, shift1, gdownb, gain2, shift2)):
        vector[...] = small[number : number + 1, :].reshape(width)
    gupb[...] = jnp.concatenate(
        [small[6 + side : 7 + side, :] for side in range(units // width)], axis=1
    ).reshape(units)
    for kind in range(2):
        gqv[kind : kind + 1, :] = small[8:9, kind * inner : (kind + 1) * inner]
    gtab[...] = small[10 : 10 + gtab.shape[0], : gtab.shape[1]]
    for copy in copies:
        copy.wait()


def finish(flat, small, out, grad_tokens, width, units, heads):
    shape = jax.ShapeDtypeStruct
    here = pl.BlockSpec(memory_space=pltpu.VMEM)
    away = pl.BlockSpec(memory_space=pl.ANY)
    inner = flat.shape[1]
    vector = shape((width,), F32)
    got = pl.pallas_call(
        finish_kernel,
        out_shape=(
            shape(out.shape, BF16),
            shape(grad_tokens.shape, F32),
            shape((3, width, inner), F32),
            shape((2, inner), F32),
            shape((heads, 2 * LANES), F32),
            shape((inner, width), F32),
            vector,
            vector,
            vector,
            shape((width, units), F32),
            shape((units,), F32),
            shape((units, width), F32),
            vector,
            vector,
            vector,
        ),
        in_specs=[away] * 3 + [here],
        out_specs=(away, away, away, here, here, away, here, here, here, away, here, away)
        + (here,) * 3,
        scratch_shapes=[
            pltpu.VMEM(flat.shape, BF16),
            pltpu.VMEM((3, width, inner), F32),
            pltpu.VMEM((inner, width), F32),
            pltpu.VMEM((width, units), F32),
            pltpu.VMEM((units, width), F32),
            pltpu.VMEM(grad_tokens.shape, F32),
            pltpu.VMEM(out.shape, BF16),
            pltpu.SemaphoreType.DMA((units // 256 + units // inner + 6,)),
            pltpu.SemaphoreType.DMA((units // 256 + units // inner + 6,)),
        ],
        compiler_params=pltpu.CompilerParams(vmem_limit_bytes=VMEM_LIMIT),
    )(flat, out, grad_tokens, small)
    got = list(got)
    got[2] = jnp.transpose(got[2], (1, 0, 2))
    got[4] = got[4].T
    return tuple(got)


def order_of_steps(bits):
    pieces = len(ORDERS["down"]) + len(ORDERS["up"]) + 4
    plan = dict(PAUSES)
    done = {(piece, step) for steps in PAUSES.values() for piece, step in steps}
    rest = [(piece, step) for piece, step in TAIL if (piece, step) not in done]
    small = [(pieces, step) for step in range(1, bits + 2)]
    every = max(1, len(rest) // (len(small) + 1))
    tail = []
    for number, step in enumerate(rest):
        tail.append(step)
        if number % every == every - 1 and small:
            tail.append(small.pop(0))
    plan["tail"] = tuple(tail + small)
    return plan


def on_device(
    dp,
    tokens,
    qkv_weight,
    qv_bias,
    rel_table,
    out_weight,
    out_bias,
    norm1_gain,
    norm1_bias,
    up_weight,
    up_bias,
    down_weight,
    down_bias,
    norm2_gain,
    norm2_bias,
    rel_bucket,
    query_len,
    key_mask,
    upstream,
):
    width = tokens.shape[1]
    inner = qkv_weight.shape[2]
    units = up_weight.shape[1]
    qkvw = jnp.transpose(qkv_weight, (1, 0, 2))
    saved = forward(
        tokens,
        qkvw,
        qv_bias,
        rel_table.T,
        out_weight,
        out_bias,
        norm1_gain,
        norm1_bias,
        up_weight,
        up_bias,
        down_weight,
        down_bias,
        norm2_gain,
        norm2_bias,
        rel_bucket,
        query_len,
        key_mask,
        upstream,
    )
    (
        out,
        gsec,
        gbr,
        act,
        slope,
        first,
        normed1,
        inverse1,
        heads_t,
        q,
        k,
        v,
        expo,
        recip,
        qkvw_o,
        outw_o,
        upw_o,
        downw_o,
        bucket,
        sums2,
    ) = saved
    bits = int(math.log2(dp))
    flat, grad_tokens, small = backward(
        order_of_steps(bits),
        bits,
        (gbr, act, slope, first, gsec, normed1, inverse1, heads_t, q, k, v, expo, recip),
        (qkvw, out_weight, up_weight, down_weight),
        (qkvw_o, outw_o, upw_o, downw_o),
        tokens,
        sums2,
        norm1_gain,
        bucket,
        query_len,
    )
    return finish(flat, small, out, grad_tokens, width, units, rel_table.shape[1])


def solution(mesh):
    rows = P(("dp", "tensor"), None)
    whole = P()
    in_specs = (
        rows,
        P(None, None, "tensor"),
        P(None, "tensor"),
        P(None, "tensor"),
        P("tensor", None),
        whole,
        whole,
        whole,
        P(None, "tensor"),
        P("tensor"),
        P("tensor", None),
        whole,
        whole,
        whole,
        whole,
        P("dp"),
        P("dp", None),
        rows,
    )
    out_specs = (
        rows,
        rows,
        P(None, None, "tensor"),
        P(None, "tensor"),
        P(None, "tensor"),
        P("tensor", None),
        whole,
        whole,
        whole,
        P(None, "tensor"),
        P("tensor"),
        P("tensor", None),
        whole,
        whole,
        whole,
    )
    return jax.shard_map(
        functools.partial(on_device, mesh.shape["dp"]),
        mesh=mesh,
        in_specs=in_specs,
        out_specs=out_specs,
        check_vma=False,
    )
```

```python
import functools
import math

import jax
import jax.numpy as jnp
from jax import lax
from jax.experimental import pallas as pl
from jax.experimental.pallas import tpu as pltpu
from jax.sharding import PartitionSpec as P

EPSILON = 1e-05
FAR_BELOW = -1000000000.0
MESH = pl.DeviceIdType.MESH
F32 = jnp.float32
BF16 = jnp.bfloat16
LANES = 128
NT = (((1,), (1,)), ((), ()))
TN = (((0,), (0,)), ((), ()))
VMEM_LIMIT = 62 * 2**20
ORDERS = {
    "down": ((2, "zZyx", "xyzZ"), (4, "yxzZ", "zZxy")),
    "up": ((2, "xyD", "yxD"), (2, "xyD", "yxD")),
    "out": ("zZyx", "xyzZ"),
    "mix": (("xyD", "yxD"), ("xyD", "xyD"), ("xyD", "yxD")),
}
PAUSES = {
    8: ((0, 1),),
    14: ((1, 1),),
    15: ((2, 1), (0, 2)),
    18: ((4, 1), (3, 1)),
    19: ((1, 2), (0, 3)),
    20: ((2, 2), (4, 2)),
    21: ((3, 2),),
    22: ((1, 3), (0, 4)),
    27: ((4, 3),),
    28: ((2, 3),),
    32: ((5, 1),),
    33: ((3, 3),),
    34: ((1, 4),),
    35: ((0, 5),),
    36: ((6, 1),),
    38: ((7, 1), (4, 4)),
    40: ((5, 2),),
    41: ((2, 4), (6, 2)),
    42: ((7, 2),),
    45: ((3, 4),),
    46: ((8, 1), (2, 5), (0, 6), (1, 5), (4, 5)),
}
TAIL = ((5, 3), (3, 5), (8, 2), (6, 3), (7, 3), (2, 6), (1, 6), (0, 7), (4, 6), (5, 4), (3, 6), (8, 3), (6, 4), (7, 4), (6, 5), (5, 5), (7, 5), (0, 8), (1, 7), (8, 4), (4, 7), (6, 6), (5, 6), (7, 6), (8, 5), (1, 8), (4, 8))


def dot(left, right, dims=None):
    if dims is None:
        return jnp.dot(left, right, preferred_element_type=F32)
    return lax.dot_general(left, right, dims, preferred_element_type=F32)


def other_core():
    return {"tensor": 1 - lax.axis_index("tensor")}


def row(ref):
    return ref[...].reshape(1, ref.shape[-1])


def fold8(block):
    return jnp.sum(block.reshape(block.shape[0] // 8, 8, block.shape[1]), axis=0)


def pack_tables(tab, packed):
    step = jnp.maximum(jnp.max(jnp.abs(tab[...])), 1e-30) / 32000.0
    inverse = 1.0 / step
    heads = tab.shape[1]
    for core in range(2):
        for pair in range(heads // 2):
            high = tab[core, 2 * pair : 2 * pair + 1, :] * inverse
            low = jnp.round(tab[core, 2 * pair + 1 : 2 * pair + 2, :] * inverse)
            high = jnp.round(high - low * (1 / 65536.0))
            both = high.astype(jnp.int32) * 65536 + low.astype(jnp.int32)
            packed[core * (heads // 2) + pair] = jnp.broadcast_to(both, packed.shape[1:])
    return step


def attend_pair(pair, q, k, vt, packed, bucket, valid, length, step, expo, heads_t, recip):
    seq = q.shape[0]
    cols = pl.ds(pl.multiple_of(pair * LANES, LANES), LANES)
    keys = k[:, cols]
    queries = q[:, cols]
    lane = lax.broadcasted_iota(jnp.int32, (seq, LANES), 1)
    in_query = lax.broadcasted_iota(jnp.int32, (seq, LANES), 0) < length
    terms = packed[pair, 0:1, :]
    near = jnp.broadcast_to(terms[:, :LANES], (seq, LANES))
    far = jnp.broadcast_to(terms[:, LANES:], (seq, LANES))
    same = jnp.where(in_query, far, near)
    swap = jnp.where(in_query, near, far)
    pieces = ([], [])
    for start in range(0, seq, LANES):
        index = bucket[:, start : start + LANES]
        got = jnp.take_along_axis(same, index, axis=1, mode="promise_in_bounds")
        if start == 0:
            turned = jnp.take_along_axis(swap, index, axis=1, mode="promise_in_bounds")
            got = jnp.where(lane < length, turned, got)
        pieces[0].append(got.astype(F32) * (step * (1 / 65536.0)))
        pieces[1].append(jnp.left_shift(got, 16).astype(F32) * (step * (1 / 65536.0)))
    first = lane < LANES // 2
    real = jnp.concatenate([valid[...] > 0] * (seq // LANES), axis=1)
    for side in range(2):
        mine = first if side == 0 else jnp.logical_not(first)
        scores = dot(jnp.where(mine, keys, jnp.zeros_like(keys)), queries, NT)
        scores = scores + jnp.concatenate(pieces[side], axis=1)
        scores = jnp.where(real, scores, FAR_BELOW)
        highest = jnp.max(scores, axis=0, keepdims=True)
        weights = jnp.exp(scores - highest).astype(BF16)
        expo[2 * pair + side] = weights
        rows = pl.ds(pl.multiple_of(pair * LANES + side * 64, 64), 64)
        values = jnp.concatenate([vt[rows, :], jnp.ones((16, seq), BF16)], axis=0)
        got = dot(values, weights)
        inverse = 1.0 / got[64:65]
        heads_t[rows, :] = (got[:64] * inverse).astype(BF16)
        recip[2 * pair + side] = jnp.broadcast_to(inverse, recip.shape[1:])


def dp_stride(bits):
    first, second = 1 << bits[0], 1 << bits[1]
    if first == second:
        return first
    return first + lax.axis_index("tensor") * (second - first)


def dp_side(bits):
    return lax.rem(lax.div(lax.axis_index("dp"), dp_stride(bits)), 2)


def dp_partner(bits):
    return {"dp": lax.axis_index("dp") + (1 - 2 * dp_side(bits)) * dp_stride(bits)}


def dp_quarter(ahead):
    return lax.rem(lax.div(lax.axis_index("dp"), 4) + ahead, 4)


def dp_ahead(ahead):
    return {"dp": lax.axis_index("dp") + 4 * (dp_quarter(ahead) - dp_quarter(0))}


def flat_rows(start, size):
    return pl.ds(pl.multiple_of(start, 16), size)


class Kit:
    def __init__(self, acc, landing, result, send_sem, recv_sem, local_sem):
        self.acc, self.landing, self.result = acc, landing, result
        self.send_sem, self.recv_sem, self.local_sem = send_sem, recv_sem, local_sem
        self.used = 0
        self.landed = 0
        self.pieces = []

    def slot(self):
        self.used += 1
        return self.used - 1

    def room(self, size):
        self.landed += size
        return self.landed - size

    def remote(self, slot, source, target, device):
        return pltpu.make_async_remote_copy(
            src_ref=source,
            dst_ref=target,
            send_sem=self.send_sem.at[slot],
            recv_sem=self.recv_sem.at[slot],
            device_id=device,
            device_id_type=MESH,
        )


class Piece:
    def __init__(self, start, length, stages, extra, kit):
        self.start = start
        self.stages, self.extra = stages, extra
        self.kit = kit
        self.number = len(kit.pieces)
        self.steps = 2 * len(stages) + 1
        kit.pieces.append(self)
        self.sizes = [length]
        self.cutting, self.spreading = [], []
        for stage in stages:
            parts = 4 if stage is None else 2
            size = self.sizes[-1] // parts
            self.sizes.append(size)
            self.cutting.append([(kit.slot(), kit.room(size)) for _ in range(parts - 1)])
            self.spreading.append([kit.slot() for _ in range(parts - 1)])
        self.crossing = [(kit.slot(), kit.room(self.sizes[-1])) for _ in extra]

    def begin(self, levels):
        at = self.start
        for level in range(levels):
            stage = self.stages[level]
            at = at + (dp_quarter(0) if stage is None else dp_side(stage)) * self.sizes[level + 1]
        return at

    def partners(self, stage):
        if stage is None:
            return [(dp_quarter(ahead), dp_ahead(ahead)) for ahead in (1, 2, 3)]
        return [(1 - dp_side(stage), dp_partner(stage))]

    def cut(self, level):
        kit, size = self.kit, self.sizes[level + 1]
        at = self.begin(level)
        return [
            kit.remote(
                slot,
                kit.acc.at[flat_rows(at + part * size, size), :],
                kit.landing.at[pl.ds(room, size), :],
                device,
            )
            for (slot, room), (part, device) in zip(
                self.cutting[level], self.partners(self.stages[level])
            )
        ]

    def swap(self, number):
        kit = self.kit
        slot, room = self.crossing[number]
        size = self.sizes[-1]
        return kit.remote(
            slot,
            kit.acc.at[flat_rows(self.begin(len(self.stages)), size), :],
            kit.landing.at[pl.ds(room, size), :],
            dp_partner(self.extra[number]),
        )

    def keep(self):
        kit = self.kit
        mine = flat_rows(self.begin(len(self.stages)), self.sizes[-1])
        return pltpu.make_async_copy(
            kit.acc.at[mine, :], kit.result.at[mine, :], kit.local_sem.at[self.number]
        )

    def spread(self, level):
        kit = self.kit
        mine = flat_rows(self.begin(level + 1), self.sizes[level + 1])
        source = kit.acc if level == len(self.stages) - 1 else kit.result
        return [
            kit.remote(slot, source.at[mine, :], kit.result.at[mine, :], device)
            for slot, (_, device) in zip(
                self.spreading[level], self.partners(self.stages[level])
            )
        ]

    def add(self, target, rooms, size):
        kit = self.kit
        chunk = math.gcd(size, 192)

        def some(number, carry):
            there = flat_rows(target + number * chunk, chunk)
            total = kit.acc[there, :].astype(F32)
            for room in rooms:
                total = total + kit.landing[flat_rows(room + number * chunk, chunk), :].astype(F32)
            kit.acc[there, :] = total.astype(BF16)
            return carry

        lax.fori_loop(0, size // chunk, some, 0)

    def run(self, step):
        levels = len(self.stages)
        if 0 < step <= levels:
            for copy in self.cut(step - 1):
                copy.wait_recv()
            rooms = [room for _, room in self.cutting[step - 1]]
            self.add(self.begin(step), rooms, self.sizes[step])
        if step < levels:
            for copy in self.cut(step):
                copy.start()
            return
        if step == levels:
            for number in range(len(self.extra)):
                both = self.swap(number)
                both.start()
                both.wait()
                self.add(self.begin(levels), [self.crossing[number][1]], self.sizes[-1])
            self.keep().start()
        else:
            for copy in self.spread(2 * levels - step):
                copy.wait_recv()
            if step == levels + 1:
                self.keep().wait()
        if step < 2 * levels:
            for copy in self.spread(2 * levels - 1 - step):
                copy.start()

    def finish(self):
        for level in range(len(self.stages)):
            for copy in self.cut(level) + self.spread(level):
                copy.wait_send()


class Vectors:
    def __init__(self, parts, landing, result, bits, kit, send_sem, recv_sem):
        self.parts, self.landing, self.result = parts, landing, result
        self.bits = bits
        self.steps = bits + 2
        self.send_sem, self.recv_sem = send_sem, recv_sem
        kit.pieces.append(self)

    def exchange(self, step):
        return pltpu.make_async_remote_copy(
            src_ref=self.parts.at[step],
            dst_ref=self.landing.at[step],
            send_sem=self.send_sem.at[step],
            recv_sem=self.recv_sem.at[step],
            device_id=other_core() if step == 0 else dp_partner((step - 1, step - 1)),
            device_id_type=MESH,
        )

    def run(self, step):
        if step > 0:
            self.exchange(step - 1).wait_recv()
            total = self.parts[max(step - 1, 1)] + self.landing[step - 1]
            if step <= self.bits:
                self.parts[step] = total
            else:
                self.result[...] = total
        if step <= self.bits:
            self.exchange(step).start()

    def finish(self):
        for step in range(self.bits + 1):
            self.exchange(step).wait_send()


def layer_kernel(
    plan,
    bits,
    tokens_h,
    qkvw_h,
    qvb_h,
    tab_h,
    outw_h,
    upw_h,
    upb_h,
    downw_h,
    upstream_h,
    bucket_h,
    outb,
    gain1,
    shift1,
    downb,
    gain2,
    shift2,
    mask,
    length,
    result_h,
    gtok_h,
    out_h,
    small,
    qkvw_o,
    outw_o,
    upw_o,
    downw_o,
    expo_h,
    acc,
    xsend,
    xrecv,
    landing,
    tokens,
    qvb,
    tab,
    upb,
    upb_other,
    upb_rows,
    outw,
    q,
    k,
    v,
    heads_t,
    recip,
    bucket,
    wide,
    gmid16,
    upstream,
    ups,
    vparts,
    vland,
    in_sem,
    out_sem,
    send_sem,
    recv_sem,
    local_sem,
    xs_sem,
    xr_sem,
    vs_sem,
    vr_sem,
    ws_sem,
    wr_sem,
):
    seq, width = tokens.shape
    inner = outw.shape[1]
    units = upw_h.shape[1]
    heads = recip.shape[0]
    pairs = inner // LANES
    split = width // inner
    third = acc.shape[0] // 3

    barrier = pltpu.get_barrier_semaphore()
    pl.semaphore_signal(barrier, inc=1, device_id=other_core(), device_id_type=MESH)
    for bit in range(bits):
        pl.semaphore_signal(barrier, inc=1, device_id=dp_partner((bit, bit)), device_id_type=MESH)
    pl.semaphore_signal(
        barrier,
        inc=1,
        device_id={"dp": lax.axis_index("dp") + 12 - 8 * dp_quarter(0)},
        device_id_type=MESH,
    )

    used, stored = [], []

    def load(source, target):
        copy = pltpu.make_async_copy(source, target, in_sem.at[len(used)])
        used.append(copy)
        copy.start()
        return copy

    loaded = []

    def early(source, target):
        number = len(used)
        used.append(None)
        loaded.append(lambda: pltpu.make_async_copy(source, target(), in_sem.at[number]))
        loaded[-1]().start()

    def store(source, target):
        copy = pltpu.make_async_copy(source, target, out_sem.at[len(stored)])
        stored.append(copy)
        copy.start()
        return copy

    halves = [
        (qkvw_h, qkvw_o),
        (qvb_h, qvb.at[1]),
        (tab_h, tab.at[1]),
        (outw_h, outw_o),
        (upw_h, upw_o),
        (upb_h, upb_other),
        (downw_h, downw_o),
    ]

    def half(number):
        source, target = halves[number]
        return pltpu.make_async_remote_copy(
            src_ref=source,
            dst_ref=target,
            send_sem=ws_sem.at[number],
            recv_sem=wr_sem.at[number],
            device_id=other_core(),
            device_id_type=MESH,
        )

    kit = Kit(acc, landing, result_h, send_sem, recv_sem, local_sem)
    extra = tuple((bit, bit) for bit in range(4, bits))
    crossed = []

    def cross(start, size, place):
        number = len(crossed)

        def copy():
            return pltpu.make_async_remote_copy(
                src_ref=xsend.at[pl.ds(place, size), :],
                dst_ref=xrecv.at[pl.ds(start, size), :],
                send_sem=xs_sem.at[number],
                recv_sem=xr_sem.at[number],
                device_id=other_core(),
                device_id_type=MESH,
            )

        copy().start()
        crossed.append(copy)

    polls = [0]

    def run_steps(number):
        for piece, step in plan.get(number, ()):
            kit.pieces[piece].run(step)

    def poll():
        run_steps(polls[0])
        polls[0] += 1

    def polled_loop(low, high, body, initial, every=1):
        start = polls[0]
        pauses = (high - low) // every
        polls[0] += pauses
        busy = [number for number in range(pauses) if plan.get(start + number)]

        def turn(index, carry):
            carry = body(index, carry)
            for number in busy:

                @pl.when(index == low + (number + 1) * every - 1)
                def _():
                    run_steps(start + number)

            return carry

        return lax.fori_loop(low, high, turn, initial)

    def begin_piece(start, size, orders):
        order = tuple(
            None if one == "D" else ("xyzZ".index(one), "xyzZ".index(two))
            for one, two in zip(*orders)
        )
        fresh = Piece(start, size, order, extra, kit)
        fresh.run(0)

    def give(place, tile):
        xsend[flat_rows(place, tile.shape[0]), :] = tile.astype(BF16)

    def take(start, tile):
        there = flat_rows(start, tile.shape[0])
        acc[there, :] = (tile + xrecv[there, :].astype(F32)).astype(BF16)

    me = lax.axis_index("tensor")

    def attend_phase(upw, downw, qkvw, vt, bucket_i, bucket_t, valid, packed, expo):
        l_tokens = load(tokens_h, tokens)
        l_qkvw = load(qkvw_h, qkvw.at[0])
        l_qvb = load(qvb_h, qvb.at[0])
        l_bucket = load(bucket_h, bucket_i)
        l_tab = load(tab_h, tab.at[0])
        l_late = [load(outw_h, outw.at[0]), load(upb_h, upb)]
        early(upw_h, lambda: upw.at[0])
        early(downw_h, lambda: downw.at[0])
        early(upstream_h, lambda: upstream)
        pl.semaphore_wait(barrier, 2 + bits)
        for number in range(3):
            half(number).start()
        span = length[me]
        mine = mask[pl.ds(me, 1), :].astype(F32)
        valid[...] = jnp.transpose(jnp.broadcast_to(mine, (LANES, seq)))

        def mix(core):
            rows = tokens[...]
            cols = slice(core * inner, (core + 1) * inner)
            query = dot(rows, qkvw[core, 0])
            q[:, cols] = ((query + qvb[core, 0:1, :]) * 0.125).astype(BF16)
            k[:, cols] = dot(rows, qkvw[core, 1]).astype(BF16)
            value = (dot(rows, qkvw[core, 2]) + qvb[core, 1:2, :]).astype(BF16)
            v[:, cols] = value
            vt[cols, :] = jnp.transpose(value)

        l_tokens.wait()
        l_qkvw.wait()
        l_qvb.wait()
        mix(0)
        l_bucket.wait()
        bucket_t[...] = jnp.transpose(bucket_i[...])
        bucket[...] = bucket_t[...].astype(BF16)
        l_tab.wait()
        half(2).wait_recv()
        step = pack_tables(tab, packed)

        def attend(pair, carry):
            attend_pair(pair, q, k, vt, packed, bucket_t, valid, span, step, expo, heads_t, recip)
            return carry

        kept = []

        def keep(low, high):
            here = pl.ds(2 * low, 2 * (high - low))
            kept.append(store(expo.at[here], expo_h.at[here]))

        lax.fori_loop(0, 1, attend, 0)
        half(0).wait_recv()
        half(1).wait_recv()
        l_other = load(qkvw_o, qkvw.at[1])
        for number in range(3, 6):
            half(number).start()
        lax.fori_loop(1, pairs, attend, 0, unroll=2)
        keep(0, pairs)
        l_other.wait()
        mix(1)
        lax.fori_loop(pairs, pairs + 1, attend, 0)
        keep(pairs, pairs + 1)
        half(6).start()
        half(3).wait_recv()
        l_late.append(load(outw_o, outw.at[1]))
        lax.fori_loop(pairs + 1, 2 * pairs, attend, 0, unroll=2)
        keep(pairs + 1, 2 * pairs)
        half(4).wait_recv()
        early(upw_o, lambda: upw.at[1])
        for copy in l_late:
            copy.wait()
        lower = jnp.transpose(heads_t[...])

        def project(tile, carry):
            cols = pl.ds(pl.multiple_of(tile * 256, 256), 256)
            wide[:, cols] = dot(lower[:, :inner], outw[0, :, cols]) + dot(
                lower[:, inner:], outw[1, :, cols]
            )
            return carry

        lax.fori_loop(0, width // 256, project, 0, unroll=3)
        for copy in kept:
            copy.wait()

    def unit_phase(
        upw, downw, act, slope, first, first_t, first32, normed1, inverse1, gsec, gbr, out
    ):
        half(5).wait_recv()
        upb_rows[0] = row(upb)
        upb_rows[1] = row(upb_other)
        block = 128

        def norm_one(number, carry):
            rows = pl.ds(pl.multiple_of(number * block, block), block)
            value = wide[rows, :] + row(outb) + tokens[rows, :].astype(F32)
            center = value - jnp.mean(value, axis=-1, keepdims=True)
            inverse = lax.rsqrt(jnp.mean(center * center, axis=-1, keepdims=True) + EPSILON)
            normed = center * inverse
            result = normed * row(gain1) + row(shift1)
            normed1[rows, :] = normed
            inverse1[rows, :] = jnp.broadcast_to(inverse, (block, LANES))
            first32[rows, :] = result
            first[rows, :] = result.astype(BF16)
            return carry

        lax.fori_loop(0, seq // block, norm_one, 0, unroll=4)

        for core in range(2):
            loaded[3 * core]().wait()

            def expand(tile, carry, core=core):
                cols = pl.ds(pl.multiple_of(tile * 256, 256), 256)
                here = pl.ds(pl.multiple_of(core * units + tile * 256, 256), 256)
                hidden = dot(first[...], upw[core, :, cols]) + upb_rows[core, :, cols]
                chance = 0.5 * (1.0 + lax.erf(hidden * math.sqrt(0.5)))
                density = jnp.exp(hidden * hidden * -0.5) * (1.0 / math.sqrt(2.0 * math.pi))
                act[:, here] = (hidden * chance).astype(BF16)
                slope[:, here] = (chance + hidden * density).astype(BF16)
                return carry

            lax.fori_loop(0, units // 256, expand, 0, unroll=2)
        half(6).wait_recv()
        l_down = load(downw_o, downw.at[1])
        first_t[...] = jnp.transpose(first[...])
        loaded[1]().wait()
        l_down.wait()

        def reduce_units(tile, carry):
            cols = pl.ds(pl.multiple_of(tile * 256, 256), 256)
            wide[:, cols] = dot(act[:, :units], downw[0, :, cols]) + dot(
                act[:, units:], downw[1, :, cols]
            )
            return carry

        lax.fori_loop(0, width // 256, reduce_units, 0, unroll=3)
        loaded[2]().wait()

        def norm_two(number, carry):
            rows = pl.ds(pl.multiple_of(number * block, block), block)
            value = wide[rows, :] + row(downb) + first32[rows, :]
            center = value - jnp.mean(value, axis=-1, keepdims=True)
            inverse = lax.rsqrt(jnp.mean(center * center, axis=-1, keepdims=True) + EPSILON)
            normed = center * inverse
            out[rows, :] = (normed * row(gain2) + row(shift2)).astype(BF16)
            grad = upstream[rows, :].astype(F32)
            scaled = grad * row(gain2)
            back = inverse * (
                scaled
                - jnp.mean(scaled, axis=-1, keepdims=True)
                - normed * jnp.mean(scaled * normed, axis=-1, keepdims=True)
            )
            gsec[rows, :] = back
            gbr[rows, :] = back.astype(BF16)
            return (
                carry[0] + fold8(back),
                carry[1] + fold8(grad * normed),
                carry[2] + fold8(grad),
            )

        zero = jnp.zeros((8, width), F32)
        later = lax.fori_loop(0, seq // block, norm_two, (zero, zero, zero), unroll=4)
        kept = store(out, out_h)

        tiles = units // 256
        span = 256 * split
        for core in (1, 0):
            low = 0
            for part, (count, *order) in enumerate(ORDERS["down"]):
                if core == 0:
                    crossed[part]().wait_recv()

                def down_tile(number, carry, core=core):
                    cols = pl.ds(pl.multiple_of(core * units + number * 256, 256), 256)
                    tile = dot(act[:, cols], gbr[...], TN)
                    for side in range(split):
                        (give if core == 1 else take)(
                            number * span + side * 256,
                            tile[:, side * inner : (side + 1) * inner],
                        )
                    return carry

                lax.fori_loop(low, low + count, down_tile, 0, unroll=count)
                if core == 1:
                    cross(low * span, count * span, low * span)
                else:
                    begin_piece(low * span, count * span, order)
                    poll()
                low += count
        fed = len(crossed)

        for core in (1, 0):

            def slope_tile(number, carry, core=core):
                here = pl.ds(pl.multiple_of(number * 256, 256), 256)
                cols = pl.ds(pl.multiple_of(core * units + number * 256, 256), 256)
                tile = dot(gbr[...], downw[core, here, :], NT) * slope[:, cols].astype(F32)
                tile = tile.astype(BF16)
                slope[:, cols] = tile
                ups[core, :, here] = fold8(tile.astype(F32))
                return carry

            polled_loop(0, tiles, slope_tile, 0, tiles // 2)

        for copy in crossed[:fed]:
            copy().wait_send()
        for core in (1, 0):
            low = 0
            for part, (count, *order) in enumerate(ORDERS["up"]):
                if core == 0:
                    crossed[fed + part]().wait_recv()

                def up_tile(number, carry, core=core):
                    cols = pl.ds(pl.multiple_of(core * units + number * inner, LANES), inner)
                    for top in range(0, width, 256):
                        tile = dot(first_t[top : top + 256, :], slope[:, cols])
                        if core == 1:
                            give(number * width + top, tile)
                        else:
                            take(third + number * width + top, tile)
                    return carry

                lax.fori_loop(low, low + count, up_tile, 0)
                if core == 1:
                    cross(third + low * width, count * width, low * width)
                else:
                    begin_piece(third + low * width, count * width, order)
                poll()
                low += count

        def first_tile(number, carry):
            cols = pl.ds(pl.multiple_of(number * 256, 256), 256)
            wide[:, cols] = (
                gsec[:, cols]
                + dot(slope[:, :units], upw[0, cols, :], NT)
                + dot(slope[:, units:], upw[1, cols, :], NT)
            )
            return carry

        polled_loop(0, width // 256, first_tile, 0)
        def norm_back(number, carry):
            rows = pl.ds(pl.multiple_of(number * block, block), block)
            grad = wide[rows, :]
            normed = normed1[rows, :]
            scaled = grad * row(gain1)
            back = inverse1[rows, 0:1] * (
                scaled
                - jnp.mean(scaled, axis=-1, keepdims=True)
                - normed * jnp.mean(scaled * normed, axis=-1, keepdims=True)
            )
            wide[rows, :] = back
            gmid16[rows, :] = back.astype(BF16)
            return (
                carry[0] + fold8(back),
                carry[1] + fold8(grad * normed),
                carry[2] + fold8(grad),
            )

        totals = lax.fori_loop(0, seq // block, norm_back, (zero, zero, zero), unroll=4)
        both = [jnp.sum(total, axis=0, keepdims=True) for total in totals]
        both += [jnp.sum(total, axis=0, keepdims=True) for total in later]
        vparts[0] = jnp.zeros(vparts.shape[1:], F32)
        vparts[1] = jnp.zeros(vparts.shape[1:], F32)
        for number, line in enumerate(both):
            vparts[0, number : number + 1, :] = line
            vparts[1, number : number + 1, :] = line
        for core in range(2):
            line = jnp.sum(ups[core], axis=0, keepdims=True)
            for side in range(units // width):
                vparts[1 - core, 6 + side : 7 + side, :] = line[:, side * width : (side + 1) * width]
        poll()
        kept.wait()

    def front(upw, downw):
        pl.run_scoped(
            functools.partial(attend_phase, upw, downw),
            pltpu.VMEM((2,) + qkvw_h.shape, BF16),
            pltpu.VMEM((2 * inner, seq), BF16),
            pltpu.VMEM((seq, seq), jnp.int32),
            pltpu.VMEM((seq, seq), jnp.int32),
            pltpu.VMEM((seq, LANES), F32),
            pltpu.VMEM((heads // 2, 8, 2 * LANES), jnp.int32),
            pltpu.VMEM((heads, seq, seq), BF16),
        )
        pl.run_scoped(
            functools.partial(unit_phase, upw, downw),
            pltpu.VMEM((seq, 2 * units), BF16),
            pltpu.VMEM((seq, 2 * units), BF16),
            pltpu.VMEM((seq, width), BF16),
            pltpu.VMEM((width, seq), BF16),
            pltpu.VMEM((seq, width), F32),
            pltpu.VMEM((seq, width), F32),
            pltpu.VMEM((seq, LANES), F32),
            pltpu.VMEM((seq, width), F32),
            pltpu.VMEM((seq, width), BF16),
            pltpu.VMEM((seq, width), BF16),
        )

    pl.run_scoped(
        front,
        pltpu.VMEM((2, width, units), BF16),
        pltpu.VMEM((2, units, width), BF16),
    )

    def pair_phase(spread, gq, gk, gv, kt, dheads_t, dheads, expo, expo_sem):
        def fetch(pair):
            slot = pair % 2 if isinstance(pair, int) else lax.rem(pair, 2)
            return pltpu.make_async_copy(
                expo_h.at[pl.ds(2 * pair, 2)], expo.at[slot], expo_sem.at[slot]
            )

        fetch(0).start()

        full = len(crossed)
        for copy in crossed[full - len(ORDERS["up"]) :]:
            copy().wait_send()
        at = 2 * third
        for core in (1, 0):
            tile = dot(heads_t[core * inner : (core + 1) * inner, :], gmid16[...])
            if core == 0:
                crossed[full]().wait_recv()
            for side in range(split):
                part = tile[:, side * inner : (side + 1) * inner]
                if core == 1:
                    give(side * inner, part)
                else:
                    take(at + side * inner, part)
            if core == 1:
                cross(at, split * inner, 0)
            else:
                begin_piece(at, split * inner, ORDERS["out"])
        poll()
        for core in range(2):
            tile = dot(outw[core], gmid16[...], NT)
            for head in range(per):
                rows = slice(core * inner + head * size, core * inner + (head + 1) * size)
                part = tile[head * size : (head + 1) * size] * recip[core * per + head, 0:1, :]
                dheads_t[rows, :] = part.astype(BF16)
        dheads[...] = jnp.transpose(dheads_t[...])
        kt[...] = jnp.transpose(k[...])
        poll()
        first = lax.broadcasted_iota(jnp.int32, (seq, LANES), 1) < size

        def pair_back(pair, carry):
            cols = pl.ds(pl.multiple_of(pair * LANES, LANES), LANES)
            fetch(pair).wait()

            @pl.when(pair + 1 < heads // 2)
            def _():
                fetch(pair + 1).start()

            slot = lax.rem(pair, 2)
            values, queries = v[:, cols], q[:, cols]
            grads, grads_t = dheads[:, cols], dheads_t[cols, :]
            gvs, gks, gqs = [], [], []
            for side in range(2):
                head = 2 * pair + side
                mine = first if side == 0 else jnp.logical_not(first)
                rows = pl.ds(pl.multiple_of(pair * LANES + side * size, size), size)
                shift = jnp.sum(
                    dheads_t[rows, :].astype(F32) * heads_t[rows, :].astype(F32),
                    axis=0,
                    keepdims=True,
                )
                back = dot(jnp.where(mine, values, jnp.zeros_like(values)), grads_t)
                gscore = expo[slot, side].astype(F32) * (back - shift)
                for tile in range(seq // LANES):
                    spread[pl.ds(tile * seq * 16 + head, seq, stride=16), :] = gscore[
                        :, tile * LANES : (tile + 1) * LANES
                    ]
                gscore = gscore.astype(BF16)
                gvs.append(dot(expo[slot, side], grads))
                gks.append(dot(gscore, queries))
                gqs.append(dot(kt[rows, :], gscore) * 0.125)
            gv[:, cols] = jnp.where(first, gvs[0], gvs[1]).astype(BF16)
            gk[:, cols] = jnp.where(first, gks[0], gks[1]).astype(BF16)
            gq[:, cols] = jnp.transpose(jnp.concatenate(gqs, axis=0)).astype(BF16)
            return carry

        polled_loop(0, heads // 2, pair_back, 0)

    def mix_phase(spread, gq, gk, gv, qkvw, tokens_t):
        l_qkvw = [load(qkvw_h, qkvw.at[0]), load(qkvw_o, qkvw.at[1])]
        tokens_t[...] = jnp.transpose(tokens[...])
        full = len(crossed)
        at = 2 * third + split * inner
        kinds = (gq, gk, gv)
        for core in (1, 0):
            for kind in range(3):
                if core == 0:
                    crossed[full + kind]().wait_recv()
                for top in range(0, width, 256):
                    tile = dot(
                        tokens_t[top : top + 256, :],
                        kinds[kind][:, core * inner : (core + 1) * inner],
                    )
                    if core == 1:
                        give(split * inner + kind * width + top, tile)
                    else:
                        take(at + kind * width + top, tile)
                if core == 1:
                    cross(at + kind * width, width, split * inner + kind * width)
                else:
                    begin_piece(at + kind * width, width, ORDERS["mix"][kind])
                poll()

        span = length[me]
        columns = 256
        half_range = LANES // 2
        labels = lax.broadcasted_iota(jnp.int32, (half_range, columns), 0).astype(BF16)
        tab_sum = jnp.zeros((64, half_range), F32)
        for start in range(0, seq, columns):
            here = slice(start, start + columns)
            position = lax.broadcasted_iota(jnp.int32, (1, columns), 1) + start
            inside = (position < span).astype(F32)

            def count(number, carry, here=here, start=start, inside=inside):
                for line in range(64):
                    if line % 16 == 0:
                        at = pl.multiple_of(number * 64 + line, 16)
                        index = bucket[pl.ds(at, 16), here].astype(F32)
                        upper = (index >= half_range).astype(F32)
                        index = (index - upper * half_range).astype(BF16)
                        at = pl.multiple_of(at * 16, 256)
                        grads = jnp.concatenate(
                            [
                                spread[pl.ds(tile * seq * 16 + at, 256), :]
                                for tile in range(start // LANES, (start + columns) // LANES)
                            ],
                            axis=1,
                        )
                    turn = line % 16
                    hot = jnp.where(
                        labels == index[turn : turn + 1, :],
                        jnp.ones((), BF16),
                        jnp.zeros((), BF16),
                    )
                    other = jnp.where(number * 64 + line < span, 1.0 - inside, inside)
                    some = grads[16 * turn : 16 * turn + 16]
                    far = some * other
                    both = jnp.concatenate([some - far, far], axis=0)
                    high = both * upper[turn : turn + 1, :]
                    both = jnp.concatenate([both - high, high], axis=0).astype(BF16)
                    carry = carry + dot(both, hot, NT)
                return carry

            tab_sum = polled_loop(0, seq // 64, count, tab_sum)

        for core in range(2):
            mine = slice(core * inner, (core + 1) * inner)
            for number, kind in ((0, gq), (1, gv)):
                line = jnp.sum(fold8(kind[:, mine].astype(F32)), axis=0, keepdims=True)
                vparts[1 - core, 8:9, number * inner : (number + 1) * inner] = line
            for part in range(2):
                lines = []
                for upper in range(2):
                    at = upper * 32 + part * 16 + core * per
                    lines.append(tab_sum[at : at + per])
                cols = slice(part * LANES, (part + 1) * LANES)
                vparts[1 - core, 10 : 10 + per, cols] = jnp.concatenate(lines, axis=1)
        Vectors(vparts, vland, small, bits, kit, vs_sem, vr_sem).run(0)
        poll()

        l_qkvw[0].wait()
        l_qkvw[1].wait()

        def token_tile(number, carry):
            cols = pl.ds(pl.multiple_of(number * 256, 256), 256)
            total = wide[:, cols]
            for core in range(2):
                for kind in range(3):
                    total = total + dot(
                        kinds[kind][:, core * inner : (core + 1) * inner],
                        qkvw[core, kind, cols, :],
                        NT,
                    )
            wide[:, cols] = total
            return carry

        polled_loop(0, width // 256, token_tile, 0)

    per = heads // 2
    size = inner // per

    def back(spread, gq, gk, gv):
        pl.run_scoped(
            functools.partial(pair_phase, spread, gq, gk, gv),
            pltpu.VMEM((2 * inner, seq), BF16),
            pltpu.VMEM((2 * inner, seq), BF16),
            pltpu.VMEM((seq, 2 * inner), BF16),
            pltpu.VMEM((2, 2, seq, seq), BF16),
            pltpu.SemaphoreType.DMA((2,)),
        )
        pl.run_scoped(
            functools.partial(mix_phase, spread, gq, gk, gv),
            pltpu.VMEM((2,) + qkvw_h.shape, BF16),
            pltpu.VMEM((width, seq), BF16),
        )

    pl.run_scoped(
        back,
        pltpu.VMEM((seq // LANES * seq * 16, LANES), F32),
        pltpu.VMEM((seq, 2 * inner), BF16),
        pltpu.VMEM((seq, 2 * inner), BF16),
        pltpu.VMEM((seq, 2 * inner), BF16),
    )
    done = store(wide, gtok_h)
    for number in range(polls[0], 1 + max(number for number in plan if number != "tail")):
        run_steps(number)
    run_steps("tail")
    done.wait()
    for piece in kit.pieces:
        piece.finish()
    for copy in crossed[-4:]:
        copy().wait_send()
    for number in range(len(halves)):
        half(number).wait_send()


def layer(plan, bits, operands):
    tokens, qkvw, qvb, tab, outw, upw, upb, downw = operands[:8]
    seq, width = tokens.shape
    inner = qkvw.shape[2]
    units = upw.shape[1]
    heads = 2 * tab.shape[0]
    shape = jax.ShapeDtypeStruct
    here = pl.BlockSpec(memory_space=pltpu.VMEM)
    away = pl.BlockSpec(memory_space=pl.ANY)
    scalar = pl.BlockSpec(memory_space=pltpu.SMEM)
    rows = (3 * width * inner + inner * width + 2 * width * units) // inner
    lands = rows - (rows >> 4) + (bits - 4) * (rows >> 4)
    pieces = len(ORDERS["down"]) + len(ORDERS["up"]) + 4
    slots = pieces * (6 + bits)
    return pl.pallas_call(
        functools.partial(layer_kernel, plan, bits),
        out_shape=(
            shape((rows, inner), BF16),
            shape((seq, width), F32),
            shape((seq, width), BF16),
            shape((16, width), F32),
            shape(qkvw.shape, BF16),
            shape(outw.shape, BF16),
            shape(upw.shape, BF16),
            shape(downw.shape, BF16),
            shape((heads, seq, seq), BF16),
        ),
        in_specs=[away] * 10 + [here] * 7 + [scalar],
        out_specs=(away, away, away, here) + (away,) * 5,
        scratch_shapes=[
            pltpu.VMEM((rows, inner), BF16),
            pltpu.VMEM((rows // 3, inner), BF16),
            pltpu.VMEM((rows, inner), BF16),
            pltpu.VMEM((lands, inner), BF16),
            pltpu.VMEM((seq, width), BF16),
            pltpu.VMEM((2,) + qvb.shape, F32),
            pltpu.VMEM((2,) + tab.shape, F32),
            pltpu.VMEM(upb.shape, F32),
            pltpu.VMEM(upb.shape, F32),
            pltpu.VMEM((2, 1, units), F32),
            pltpu.VMEM((2,) + outw.shape, BF16),
            pltpu.VMEM((seq, 2 * inner), BF16),
            pltpu.VMEM((seq, 2 * inner), BF16),
            pltpu.VMEM((seq, 2 * inner), BF16),
            pltpu.VMEM((2 * inner, seq), BF16),
            pltpu.VMEM((heads, 8, seq), F32),
            pltpu.VMEM((seq, seq), BF16),
            pltpu.VMEM((seq, width), F32),
            pltpu.VMEM((seq, width), BF16),
            pltpu.VMEM((seq, width), BF16),
            pltpu.VMEM((2, 8, units), F32),
            pltpu.VMEM((bits + 1, 16, width), F32),
            pltpu.VMEM((bits + 1, 16, width), F32),
            pltpu.SemaphoreType.DMA((24,)),
            pltpu.SemaphoreType.DMA((8,)),
            pltpu.SemaphoreType.DMA((slots,)),
            pltpu.SemaphoreType.DMA((slots,)),
            pltpu.SemaphoreType.DMA((pieces,)),
            pltpu.SemaphoreType.DMA((pieces,)),
            pltpu.SemaphoreType.DMA((pieces,)),
            pltpu.SemaphoreType.DMA((bits + 1,)),
            pltpu.SemaphoreType.DMA((bits + 1,)),
            pltpu.SemaphoreType.DMA((7,)),
            pltpu.SemaphoreType.DMA((7,)),
        ],
        compiler_params=pltpu.CompilerParams(
            collective_id=0, has_side_effects=True, vmem_limit_bytes=VMEM_LIMIT
        ),
    )(*operands)


def finish_kernel(
    flat_h,
    out_h,
    gtok_h,
    small,
    out_f,
    gtok_f,
    mix_f,
    gqv,
    gtab,
    gout_f,
    goutb,
    gain1,
    shift1,
    up_f,
    gupb,
    down_f,
    gdownb,
    gain2,
    shift2,
    flat,
    mix,
    gout,
    up,
    down,
    gtok,
    out,
    in_sem,
    out_sem,
):
    rows, inner = flat.shape
    units, width = down.shape
    split = width // inner
    third = rows // 3
    copies = []
    tiles = units // 256
    span = 256 * split
    sizes = (
        [span] * tiles + [width] * (units // inner) + [split * inner] + [width] * 3
    )
    loads = []
    at = 0
    for number, size in enumerate(sizes):
        here = pl.ds(at, size)
        loads.append(pltpu.make_async_copy(flat_h.at[here, :], flat.at[here, :], in_sem.at[number]))
        loads[-1].start()
        at += size

    for source, target in ((gtok_h, gtok), (out_h, out)):
        loads.append(pltpu.make_async_copy(source, target, in_sem.at[len(loads)]))
        loads[-1].start()

    def store(source, target):
        copies.append(pltpu.make_async_copy(source, target, out_sem.at[len(copies)]))
        copies[-1].start()

    def wide(start, size):
        return flat[start : start + size, :].astype(F32)

    for tile in range(tiles):
        loads[tile].wait()
        here = slice(tile * 256, tile * 256 + 256)
        for side in range(split):
            down[here, side * inner : (side + 1) * inner] = wide(tile * span + side * 256, 256)
        here = pl.ds(tile * 256, 256)
        store(down.at[here, :], down_f.at[here, :])
    for part in range(units // inner):
        loads[tiles + part].wait()
        cols = pl.ds(part * inner, inner)
        up[:, cols] = wide(third + part * width, width)
        store(up.at[:, cols], up_f.at[:, cols])
    at = 2 * third
    loads[-6].wait()
    for side in range(split):
        gout[:, side * inner : (side + 1) * inner] = wide(at + side * inner, inner)
    store(gout, gout_f)
    at += split * inner
    for kind in range(3):
        loads[kind - 5].wait()
        mix[kind] = wide(at + kind * width, width)
        store(mix.at[kind], mix_f.at[kind])
    loads[-2].wait()
    store(gtok, gtok_f)
    loads[-1].wait()
    store(out, out_f)
    for number, vector in enumerate((goutb, gain1, shift1, gdownb, gain2, shift2)):
        vector[...] = small[number : number + 1, :].reshape(width)
    gupb[...] = jnp.concatenate(
        [small[6 + side : 7 + side, :] for side in range(units // width)], axis=1
    ).reshape(units)
    for kind in range(2):
        gqv[kind : kind + 1, :] = small[8:9, kind * inner : (kind + 1) * inner]
    gtab[...] = small[10 : 10 + gtab.shape[0], : gtab.shape[1]]
    for copy in copies:
        copy.wait()


def finish(flat, small, out, grad_tokens, width, units, heads):
    shape = jax.ShapeDtypeStruct
    here = pl.BlockSpec(memory_space=pltpu.VMEM)
    away = pl.BlockSpec(memory_space=pl.ANY)
    inner = flat.shape[1]
    vector = shape((width,), F32)
    got = pl.pallas_call(
        finish_kernel,
        out_shape=(
            shape(out.shape, BF16),
            shape(grad_tokens.shape, F32),
            shape((3, width, inner), F32),
            shape((2, inner), F32),
            shape((heads, 2 * LANES), F32),
            shape((inner, width), F32),
            vector,
            vector,
            vector,
            shape((width, units), F32),
            shape((units,), F32),
            shape((units, width), F32),
            vector,
            vector,
            vector,
        ),
        in_specs=[away] * 3 + [here],
        out_specs=(away, away, away, here, here, away, here, here, here, away, here, away)
        + (here,) * 3,
        scratch_shapes=[
            pltpu.VMEM(flat.shape, BF16),
            pltpu.VMEM((3, width, inner), F32),
            pltpu.VMEM((inner, width), F32),
            pltpu.VMEM((width, units), F32),
            pltpu.VMEM((units, width), F32),
            pltpu.VMEM(grad_tokens.shape, F32),
            pltpu.VMEM(out.shape, BF16),
            pltpu.SemaphoreType.DMA((units // 256 + units // inner + 6,)),
            pltpu.SemaphoreType.DMA((units // 256 + units // inner + 6,)),
        ],
        compiler_params=pltpu.CompilerParams(vmem_limit_bytes=VMEM_LIMIT),
    )(flat, out, grad_tokens, small)
    got = list(got)
    got[2] = jnp.transpose(got[2], (1, 0, 2))
    got[4] = got[4].T
    return tuple(got)


def order_of_steps(bits):
    pieces = len(ORDERS["down"]) + len(ORDERS["up"]) + 4
    plan = dict(PAUSES)
    known = {step for steps in PAUSES.values() for step in steps} | set(TAIL)
    more = tuple((pieces, step) for step in range(1, bits + 2) if (pieces, step) not in known)
    plan["tail"] = TAIL + more
    return plan


def on_device(
    dp,
    tokens,
    qkv_weight,
    qv_bias,
    rel_table,
    out_weight,
    out_bias,
    norm1_gain,
    norm1_bias,
    up_weight,
    up_bias,
    down_weight,
    down_bias,
    norm2_gain,
    norm2_bias,
    rel_bucket,
    query_len,
    key_mask,
    upstream,
):
    width = tokens.shape[1]
    units = up_weight.shape[1]
    bits = int(math.log2(dp))
    flat, grad_tokens, out, small = layer(
        order_of_steps(bits),
        bits,
        (
            tokens,
            jnp.transpose(qkv_weight, (1, 0, 2)),
            qv_bias,
            rel_table.T,
            out_weight,
            up_weight,
            up_bias,
            down_weight,
            upstream,
            rel_bucket,
            out_bias,
            norm1_gain,
            norm1_bias,
            down_bias,
            norm2_gain,
            norm2_bias,
            key_mask,
            query_len,
        ),
    )[:4]
    return finish(flat, small, out, grad_tokens, width, units, rel_table.shape[1])


def solution(mesh):
    rows = P(("dp", "tensor"), None)
    whole = P()
    in_specs = (
        rows,
        P(None, None, "tensor"),
        P(None, "tensor"),
        P(None, "tensor"),
        P("tensor", None),
        whole,
        whole,
        whole,
        P(None, "tensor"),
        P("tensor"),
        P("tensor", None),
        whole,
        whole,
        whole,
        whole,
        P("dp"),
        P("dp", None),
        rows,
    )
    out_specs = (
        rows,
        rows,
        P(None, None, "tensor"),
        P(None, "tensor"),
        P(None, "tensor"),
        P("tensor", None),
        whole,
        whole,
        whole,
        P(None, "tensor"),
        P("tensor"),
        P("tensor", None),
        whole,
        whole,
        whole,
    )
    return jax.shard_map(
        functools.partial(on_device, mesh.shape["dp"]),
        mesh=mesh,
        in_specs=in_specs,
        out_specs=out_specs,
        check_vma=False,
    )
```

```python
import functools
import math

import jax
import jax.numpy as jnp
from jax import lax
from jax.experimental import pallas as pl
from jax.experimental.pallas import tpu as pltpu
from jax.sharding import PartitionSpec as P

EPSILON = 1e-05
FAR_BELOW = -1000000000.0
MESH = pl.DeviceIdType.MESH
F32 = jnp.float32
BF16 = jnp.bfloat16
LANES = 128
NT = (((1,), (1,)), ((), ()))
TN = (((0,), (0,)), ((), ()))
VMEM_LIMIT = 62 * 2**20
ORDERS = {
    "down": ((2, "xyD", "yxD"), (3, "yxzZ", "zZxy"), (1, "xyzZ", "xzZy")),
    "up": ((2, "xyzZ", "xyzZ"), (1, "xyzZ", "zZxy"), (1, "yxzZ", "yzZx")),
    "out": ("xyzZ", "yxzZ"),
    "mix": (("xyD", "yxD"), ("yxD", "yxD"), ("yxD", "xyD")),
}
PAUSES = {
    12: ((0, 1),),
    15: ((2, 1),),
    16: ((1, 1),),
    18: ((0, 2),),
    19: ((5, 1),),
    20: ((2, 2),),
    22: ((3, 1), (0, 3), (4, 1), (2, 3)),
    24: ((1, 2),),
    25: ((6, 1), (0, 4), (3, 2), (2, 4)),
    26: ((5, 2),),
    27: ((1, 3),),
    28: ((4, 2),),
    29: ((6, 2),),
    31: ((3, 3),),
    32: ((2, 5), (0, 5)),
    33: ((5, 3),),
    35: ((1, 4), (4, 3)),
    36: ((6, 3),),
    37: ((7, 1), (3, 4), (2, 6)),
    39: ((5, 4),),
    42: ((6, 4), (8, 1)),
    43: ((9, 1), (3, 5)),
    44: ((5, 5),),
    45: ((7, 2), (6, 5)),
    46: ((8, 2), (2, 7)),
    47: ((1, 5), (0, 6), (3, 6), (4, 4)),
    48: ((5, 6), (10, 1), (9, 2)),
    50: ((7, 3), (6, 6), (2, 8)),
}
TAIL = ((8, 3), (3, 7), (10, 2), (4, 5), (1, 6), (5, 7), (10, 3), (6, 7), (9, 3), (7, 4), (8, 4), (5, 8), (4, 6), (3, 8), (7, 5), (10, 4), (1, 7), (9, 4), (6, 8), (4, 7), (8, 5), (10, 5), (7, 6), (9, 5), (1, 8), (8, 6), (4, 8), (9, 6))


def dot(left, right, dims=None):
    if dims is None:
        return jnp.dot(left, right, preferred_element_type=F32)
    return lax.dot_general(left, right, dims, preferred_element_type=F32)


def other_core():
    return {"tensor": 1 - lax.axis_index("tensor")}


def row(ref):
    return ref[...].reshape(1, ref.shape[-1])


def fold8(block):
    return jnp.sum(block.reshape(block.shape[0] // 8, 8, block.shape[1]), axis=0)


def pack_tables(tab, packed, core):
    step = jnp.maximum(jnp.max(jnp.abs(tab[core])), 1e-30) / 32000.0
    inverse = 1.0 / step
    heads = tab.shape[1]
    for pair in range(heads // 2):
        high = tab[core, 2 * pair : 2 * pair + 1, :] * inverse
        low = jnp.round(tab[core, 2 * pair + 1 : 2 * pair + 2, :] * inverse)
        high = jnp.round(high - low * (1 / 65536.0))
        both = high.astype(jnp.int32) * 65536 + low.astype(jnp.int32)
        packed[core * (heads // 2) + pair] = jnp.broadcast_to(both, packed.shape[1:])
    return step


def attend_pair(pair, q, k, vt, packed, bucket, valid, length, step, expo, heads_t, recip):
    seq = q.shape[0]
    cols = pl.ds(pl.multiple_of(pair * LANES, LANES), LANES)
    keys = k[:, cols]
    queries = q[:, cols]
    lane = lax.broadcasted_iota(jnp.int32, (seq, LANES), 1)
    in_query = lax.broadcasted_iota(jnp.int32, (seq, LANES), 0) < length
    terms = packed[pair, 0:1, :]
    near = jnp.broadcast_to(terms[:, :LANES], (seq, LANES))
    far = jnp.broadcast_to(terms[:, LANES:], (seq, LANES))
    same = jnp.where(in_query, far, near)
    swap = jnp.where(in_query, near, far)
    pieces = ([], [])
    for start in range(0, seq, LANES):
        index = bucket[:, start : start + LANES]
        got = jnp.take_along_axis(same, index, axis=1, mode="promise_in_bounds")
        if start == 0:
            turned = jnp.take_along_axis(swap, index, axis=1, mode="promise_in_bounds")
            got = jnp.where(lane < length, turned, got)
        pieces[0].append(got.astype(F32) * (step * (1 / 65536.0)))
        pieces[1].append(jnp.left_shift(got, 16).astype(F32) * (step * (1 / 65536.0)))
    first = lane < LANES // 2
    real = jnp.concatenate([valid[...] > 0] * (seq // LANES), axis=1)
    for side in range(2):
        mine = first if side == 0 else jnp.logical_not(first)
        scores = dot(jnp.where(mine, keys, jnp.zeros_like(keys)), queries, NT)
        scores = scores + jnp.concatenate(pieces[side], axis=1)
        scores = jnp.where(real, scores, FAR_BELOW)
        highest = jnp.max(scores, axis=0, keepdims=True)
        weights = jnp.exp(scores - highest).astype(BF16)
        expo[2 * pair + side] = weights
        rows = pl.ds(pl.multiple_of(pair * LANES + side * 64, 64), 64)
        values = jnp.concatenate([vt[rows, :], jnp.ones((16, seq), BF16)], axis=0)
        got = dot(values, weights)
        inverse = 1.0 / got[64:65]
        heads_t[rows, :] = (got[:64] * inverse).astype(BF16)
        recip[2 * pair + side] = jnp.broadcast_to(inverse, recip.shape[1:])


def dp_stride(bits):
    first, second = 1 << bits[0], 1 << bits[1]
    if first == second:
        return first
    return first + lax.axis_index("tensor") * (second - first)


def dp_side(bits):
    return lax.rem(lax.div(lax.axis_index("dp"), dp_stride(bits)), 2)


def dp_partner(bits):
    return {"dp": lax.axis_index("dp") + (1 - 2 * dp_side(bits)) * dp_stride(bits)}


def dp_quarter(ahead):
    return lax.rem(lax.div(lax.axis_index("dp"), 4) + ahead, 4)


def dp_ahead(ahead):
    return {"dp": lax.axis_index("dp") + 4 * (dp_quarter(ahead) - dp_quarter(0))}


def flat_rows(start, size):
    return pl.ds(pl.multiple_of(start, 16), size)


class Kit:
    def __init__(self, acc, landing, result, send_sem, recv_sem, local_sem):
        self.acc, self.landing, self.result = acc, landing, result
        self.send_sem, self.recv_sem, self.local_sem = send_sem, recv_sem, local_sem
        self.used = [0, 0]
        self.landed = 0
        self.pieces = []

    def slot(self, kind):
        self.used[kind] += 1
        return self.used[kind] - 1

    def room(self, size):
        self.landed += size
        return self.landed - size

    def remote(self, slot, source, target, device):
        return pltpu.make_async_remote_copy(
            src_ref=source,
            dst_ref=target,
            send_sem=self.send_sem.at[slot[0]],
            recv_sem=self.recv_sem.at[slot[1]],
            device_id=device,
            device_id_type=MESH,
        )


class Piece:
    def __init__(self, start, length, stages, extra, kit):
        self.start = start
        self.stages, self.extra = stages, extra
        self.kit = kit
        self.number = len(kit.pieces)
        self.steps = 2 * len(stages) + 1
        kit.pieces.append(self)
        self.sizes = [length]
        self.cutting, self.spreading = [], []
        for stage in stages:
            parts = 4 if stage is None else 2
            size = self.sizes[-1] // parts
            self.sizes.append(size)
            leaving = [kit.slot(0) for _ in range(parts - 1)]
            self.cutting.append([((slot, kit.slot(1)), kit.room(size)) for slot in leaving])
            self.spreading.append([(slot, kit.slot(1)) for slot in leaving])
        self.crossing = [((kit.slot(0), kit.slot(1)), kit.room(self.sizes[-1])) for _ in extra]

    def begin(self, levels):
        at = self.start
        for level in range(levels):
            stage = self.stages[level]
            at = at + (dp_quarter(0) if stage is None else dp_side(stage)) * self.sizes[level + 1]
        return at

    def partners(self, stage):
        if stage is None:
            return [(dp_quarter(ahead), dp_ahead(ahead)) for ahead in (1, 2, 3)]
        return [(1 - dp_side(stage), dp_partner(stage))]

    def cut(self, level):
        kit, size = self.kit, self.sizes[level + 1]
        at = self.begin(level)
        return [
            kit.remote(
                slot,
                kit.acc.at[flat_rows(at + part * size, size), :],
                kit.landing.at[pl.ds(room, size), :],
                device,
            )
            for (slot, room), (part, device) in zip(
                self.cutting[level], self.partners(self.stages[level])
            )
        ]

    def swap(self, number):
        kit = self.kit
        slot, room = self.crossing[number]
        size = self.sizes[-1]
        return kit.remote(
            slot,
            kit.acc.at[flat_rows(self.begin(len(self.stages)), size), :],
            kit.landing.at[pl.ds(room, size), :],
            dp_partner(self.extra[number]),
        )

    def keep(self):
        kit = self.kit
        mine = flat_rows(self.begin(len(self.stages)), self.sizes[-1])
        return pltpu.make_async_copy(
            kit.acc.at[mine, :], kit.result.at[mine, :], kit.local_sem.at[self.number]
        )

    def spread(self, level):
        kit = self.kit
        mine = flat_rows(self.begin(level + 1), self.sizes[level + 1])
        source = kit.acc if level == len(self.stages) - 1 else kit.result
        return [
            kit.remote(slot, source.at[mine, :], kit.result.at[mine, :], device)
            for slot, (_, device) in zip(
                self.spreading[level], self.partners(self.stages[level])
            )
        ]

    def add(self, target, rooms, size):
        kit = self.kit
        chunk = math.gcd(size, 192)

        def some(number, carry):
            there = flat_rows(target + number * chunk, chunk)
            total = kit.acc[there, :].astype(F32)
            for room in rooms:
                total = total + kit.landing[flat_rows(room + number * chunk, chunk), :].astype(F32)
            kit.acc[there, :] = total.astype(BF16)
            return carry

        lax.fori_loop(0, size // chunk, some, 0)

    def run(self, step):
        levels = len(self.stages)
        if 0 < step <= levels:
            for copy in self.cut(step - 1):
                copy.wait_recv()
            rooms = [room for _, room in self.cutting[step - 1]]
            self.add(self.begin(step), rooms, self.sizes[step])
        if step < levels:
            for copy in self.cut(step):
                copy.start()
            return
        if step == levels:
            for number in range(len(self.extra)):
                both = self.swap(number)
                both.start()
                both.wait()
                self.add(self.begin(levels), [self.crossing[number][1]], self.sizes[-1])
            self.keep().start()
        else:
            for copy in self.spread(2 * levels - step):
                copy.wait_recv()
            if step == levels + 1:
                self.keep().wait()
        if step < 2 * levels:
            for copy in self.cut(2 * levels - 1 - step):
                copy.wait_send()
            for copy in self.spread(2 * levels - 1 - step):
                copy.start()

    def finish(self):
        for level in range(len(self.stages)):
            for copy in self.spread(level):
                copy.wait_send()


class Vectors:
    def __init__(self, parts, landing, result, bits, kit, send_sem, recv_sem):
        self.parts, self.landing, self.result = parts, landing, result
        self.bits = bits
        self.steps = bits + 2
        self.send_sem, self.recv_sem = send_sem, recv_sem
        kit.pieces.append(self)

    def exchange(self, step):
        return pltpu.make_async_remote_copy(
            src_ref=self.parts.at[step],
            dst_ref=self.landing.at[step],
            send_sem=self.send_sem.at[step],
            recv_sem=self.recv_sem.at[step],
            device_id=other_core() if step == 0 else dp_partner((step - 1, step - 1)),
            device_id_type=MESH,
        )

    def run(self, step):
        if step > 0:
            self.exchange(step - 1).wait_recv()
            total = self.parts[max(step - 1, 1)] + self.landing[step - 1]
            if step <= self.bits:
                self.parts[step] = total
            else:
                self.result[...] = total
        if step <= self.bits:
            self.exchange(step).start()

    def finish(self):
        for step in range(self.bits + 1):
            self.exchange(step).wait_send()


def layer_kernel(
    plan,
    bits,
    tokens_h,
    qkvw_h,
    qvb_h,
    tab_h,
    outw_h,
    upw_h,
    upb_h,
    downw_h,
    upstream_h,
    bucket_h,
    outb,
    gain1,
    shift1,
    downb,
    gain2,
    shift2,
    mask,
    length,
    result_h,
    gtok_h,
    out_h,
    small,
    qkvw_o,
    outw_o,
    upw_o,
    downw_o,
    expo_h,
    acc,
    xsend,
    xrecv,
    landing,
    tokens,
    qvb,
    tab,
    upb,
    upb_other,
    upb_rows,
    outw,
    q,
    k,
    v,
    heads_t,
    recip,
    bucket,
    wide,
    gmid16,
    upstream,
    ups,
    vparts,
    vland,
    in_sem,
    out_sem,
    send_sem,
    recv_sem,
    local_sem,
    xs_sem,
    xr_sem,
    vs_sem,
    vr_sem,
    ws_sem,
    wr_sem,
):
    seq, width = tokens.shape
    inner = outw.shape[1]
    units = upw_h.shape[1]
    heads = recip.shape[0]
    pairs = inner // LANES
    split = width // inner
    third = acc.shape[0] // 3

    barrier = pltpu.get_barrier_semaphore()
    pl.semaphore_signal(barrier, inc=1, device_id=other_core(), device_id_type=MESH)
    for bit in range(bits):
        pl.semaphore_signal(barrier, inc=1, device_id=dp_partner((bit, bit)), device_id_type=MESH)
    pl.semaphore_signal(
        barrier,
        inc=1,
        device_id={"dp": lax.axis_index("dp") + 12 - 8 * dp_quarter(0)},
        device_id_type=MESH,
    )

    used, stored = [], []

    def load(source, target):
        copy = pltpu.make_async_copy(source, target, in_sem.at[len(used)])
        used.append(copy)
        copy.start()
        return copy

    loaded = []

    def early(source, target):
        number = len(used)
        used.append(None)
        loaded.append(lambda: pltpu.make_async_copy(source, target(), in_sem.at[number]))
        loaded[-1]().start()

    def store(source, target):
        copy = pltpu.make_async_copy(source, target, out_sem.at[len(stored)])
        stored.append(copy)
        copy.start()
        return copy

    halves = [
        (qkvw_h, qkvw_o),
        (qvb_h, qvb.at[1]),
        (tab_h, tab.at[1]),
        (outw_h, outw_o),
        (upw_h, upw_o),
        (upb_h, upb_other),
        (downw_h, downw_o),
    ]

    def half(number):
        source, target = halves[number]
        return pltpu.make_async_remote_copy(
            src_ref=source,
            dst_ref=target,
            send_sem=ws_sem.at[number],
            recv_sem=wr_sem.at[number],
            device_id=other_core(),
            device_id_type=MESH,
        )

    kit = Kit(acc, landing, result_h, send_sem, recv_sem, local_sem)
    extra = tuple((bit, bit) for bit in range(4, bits))
    crossed = []

    def cross(start, size, place):
        number = len(crossed)

        def copy():
            return pltpu.make_async_remote_copy(
                src_ref=xsend.at[pl.ds(place, size), :],
                dst_ref=xrecv.at[pl.ds(start, size), :],
                send_sem=xs_sem.at[number],
                recv_sem=xr_sem.at[number],
                device_id=other_core(),
                device_id_type=MESH,
            )

        copy().start()
        crossed.append(copy)

    polls = [0]

    def run_steps(number):
        for piece, step in plan.get(number, ()):
            kit.pieces[piece].run(step)

    def poll():
        run_steps(polls[0])
        polls[0] += 1

    def polled_loop(low, high, body, initial, every=1):
        start = polls[0]
        pauses = (high - low) // every
        polls[0] += pauses
        busy = [number for number in range(pauses) if plan.get(start + number)]

        def turn(index, carry):
            carry = body(index, carry)
            for number in busy:

                @pl.when(index == low + (number + 1) * every - 1)
                def _():
                    run_steps(start + number)

            return carry

        return lax.fori_loop(low, high, turn, initial)

    def begin_piece(start, size, orders):
        order = tuple(
            None if one == "D" else ("xyzZ".index(one), "xyzZ".index(two))
            for one, two in zip(*orders)
        )
        fresh = Piece(start, size, order, extra, kit)
        if not any((fresh.number, 0) in steps for steps in plan.values()):
            fresh.run(0)

    def give(place, tile):
        xsend[flat_rows(place, tile.shape[0]), :] = tile.astype(BF16)

    def take(start, tile):
        there = flat_rows(start, tile.shape[0])
        acc[there, :] = (tile + xrecv[there, :].astype(F32)).astype(BF16)

    me = lax.axis_index("tensor")

    def attend_phase(upw, downw, qkvw, vt, bucket_i, bucket_t, valid, packed, expo):
        l_tokens = load(tokens_h, tokens)
        l_qkvw = load(qkvw_h, qkvw.at[0])
        l_qvb = load(qvb_h, qvb.at[0])
        l_bucket = load(bucket_h, bucket_i)
        l_tab = load(tab_h, tab.at[0])
        l_late = [load(outw_h, outw.at[0]), load(upb_h, upb)]
        early(upw_h, lambda: upw.at[0])
        early(downw_h, lambda: downw.at[0])
        early(upstream_h, lambda: upstream)
        span = length[me]
        mine = mask[pl.ds(me, 1), :].astype(F32)
        valid[...] = jnp.transpose(jnp.broadcast_to(mine, (LANES, seq)))

        def mix(core):
            rows = tokens[...]
            cols = slice(core * inner, (core + 1) * inner)
            query = dot(rows, qkvw[core, 0])
            q[:, cols] = ((query + qvb[core, 0:1, :]) * 0.125).astype(BF16)
            k[:, cols] = dot(rows, qkvw[core, 1]).astype(BF16)
            value = (dot(rows, qkvw[core, 2]) + qvb[core, 1:2, :]).astype(BF16)
            v[:, cols] = value
            vt[cols, :] = jnp.transpose(value)

        l_tokens.wait()
        l_qkvw.wait()
        l_qvb.wait()
        mix(0)
        pl.semaphore_wait(barrier, 2 + bits)
        for number in range(3):
            half(number).start()
        l_bucket.wait()
        bucket_t[...] = jnp.transpose(bucket_i[...])
        bucket[...] = bucket_t[...].astype(BF16)
        l_tab.wait()

        def attend(step, pair, carry):
            attend_pair(pair, q, k, vt, packed, bucket_t, valid, span, step, expo, heads_t, recip)
            return carry

        attend_own = functools.partial(attend, pack_tables(tab, packed, 0))

        kept = []

        def keep(low, high):
            here = pl.ds(2 * low, 2 * (high - low))
            kept.append(store(expo.at[here], expo_h.at[here]))

        lax.fori_loop(0, 2, attend_own, 0, unroll=2)
        half(0).wait_recv()
        half(1).wait_recv()
        half(2).wait_recv()
        l_other = load(qkvw_o, qkvw.at[1])
        for number in range(3, 6):
            half(number).start()
        lax.fori_loop(2, pairs, attend_own, 0, unroll=2)
        keep(0, pairs)
        l_other.wait()
        mix(1)
        attend_other = functools.partial(attend, pack_tables(tab, packed, 1))
        lax.fori_loop(pairs, pairs + 1, attend_other, 0)
        keep(pairs, pairs + 1)
        half(6).start()
        half(3).wait_recv()
        l_late.append(load(outw_o, outw.at[1]))
        lax.fori_loop(pairs + 1, 2 * pairs, attend_other, 0, unroll=2)
        keep(pairs + 1, 2 * pairs)
        half(4).wait_recv()
        early(upw_o, lambda: upw.at[1])
        for copy in l_late:
            copy.wait()
        lower = jnp.transpose(heads_t[...])

        def project(tile, carry):
            cols = pl.ds(pl.multiple_of(tile * 256, 256), 256)
            wide[:, cols] = dot(lower[:, :inner], outw[0, :, cols]) + dot(
                lower[:, inner:], outw[1, :, cols]
            )
            return carry

        lax.fori_loop(0, width // 256, project, 0, unroll=3)
        for copy in kept:
            copy.wait()

    def unit_phase(
        upw, downw, act, slope, first, first_t, first32, normed1, inverse1, gsec, gbr, out
    ):
        half(5).wait_recv()
        upb_rows[0] = row(upb)
        upb_rows[1] = row(upb_other)
        block = 128

        def norm_one(number, carry):
            rows = pl.ds(pl.multiple_of(number * block, block), block)
            value = wide[rows, :] + row(outb) + tokens[rows, :].astype(F32)
            center = value - jnp.mean(value, axis=-1, keepdims=True)
            inverse = lax.rsqrt(jnp.mean(center * center, axis=-1, keepdims=True) + EPSILON)
            normed = center * inverse
            result = normed * row(gain1) + row(shift1)
            normed1[rows, :] = normed
            inverse1[rows, :] = jnp.broadcast_to(inverse, (block, LANES))
            first32[rows, :] = result
            first[rows, :] = result.astype(BF16)
            return carry

        lax.fori_loop(0, seq // block, norm_one, 0, unroll=4)

        for core in range(2):
            loaded[3 * core]().wait()

            def expand(tile, carry, core=core):
                cols = pl.ds(pl.multiple_of(tile * 256, 256), 256)
                here = pl.ds(pl.multiple_of(core * units + tile * 256, 256), 256)
                hidden = dot(first[...], upw[core, :, cols]) + upb_rows[core, :, cols]
                chance = 0.5 * (1.0 + lax.erf(hidden * math.sqrt(0.5)))
                density = jnp.exp(hidden * hidden * -0.5) * (1.0 / math.sqrt(2.0 * math.pi))
                act[:, here] = (hidden * chance).astype(BF16)
                slope[:, here] = (chance + hidden * density).astype(BF16)
                return carry

            lax.fori_loop(0, units // 256, expand, 0, unroll=2)
        half(6).wait_recv()
        l_down = load(downw_o, downw.at[1])
        first_t[...] = jnp.transpose(first[...])
        loaded[1]().wait()
        l_down.wait()

        def reduce_units(tile, carry):
            cols = pl.ds(pl.multiple_of(tile * 256, 256), 256)
            wide[:, cols] = dot(act[:, :units], downw[0, :, cols]) + dot(
                act[:, units:], downw[1, :, cols]
            )
            return carry

        lax.fori_loop(0, width // 256, reduce_units, 0, unroll=3)
        loaded[2]().wait()

        def norm_two(number, carry):
            rows = pl.ds(pl.multiple_of(number * block, block), block)
            value = wide[rows, :] + row(downb) + first32[rows, :]
            center = value - jnp.mean(value, axis=-1, keepdims=True)
            inverse = lax.rsqrt(jnp.mean(center * center, axis=-1, keepdims=True) + EPSILON)
            normed = center * inverse
            out[rows, :] = (normed * row(gain2) + row(shift2)).astype(BF16)
            grad = upstream[rows, :].astype(F32)
            scaled = grad * row(gain2)
            back = inverse * (
                scaled
                - jnp.mean(scaled, axis=-1, keepdims=True)
                - normed * jnp.mean(scaled * normed, axis=-1, keepdims=True)
            )
            gsec[rows, :] = back
            gbr[rows, :] = back.astype(BF16)
            return (
                carry[0] + fold8(back),
                carry[1] + fold8(grad * normed),
                carry[2] + fold8(grad),
            )

        zero = jnp.zeros((8, width), F32)
        later = lax.fori_loop(0, seq // block, norm_two, (zero, zero, zero), unroll=4)
        kept = store(out, out_h)

        tiles = units // 256
        span = 256 * split

        def down(core):
            low = 0
            for part, (count, *order) in enumerate(ORDERS["down"]):
                if core == 0:
                    crossed[part]().wait_recv()

                def down_tile(number, carry, core=core):
                    cols = pl.ds(pl.multiple_of(core * units + number * 256, 256), 256)
                    tile = dot(act[:, cols], gbr[...], TN)
                    for side in range(split):
                        (give if core == 1 else take)(
                            number * span + side * 256,
                            tile[:, side * inner : (side + 1) * inner],
                        )
                    return carry

                lax.fori_loop(low, low + count, down_tile, 0, unroll=count)
                if core == 1:
                    cross(low * span, count * span, low * span)
                else:
                    begin_piece(low * span, count * span, order)
                    poll()
                low += count

        def bend(core):
            def slope_tile(number, carry):
                here = pl.ds(pl.multiple_of(number * 256, 256), 256)
                cols = pl.ds(pl.multiple_of(core * units + number * 256, 256), 256)
                tile = dot(gbr[...], downw[core, here, :], NT) * slope[:, cols].astype(F32)
                tile = tile.astype(BF16)
                slope[:, cols] = tile
                ups[core, :, here] = fold8(tile.astype(F32))
                return carry

            polled_loop(0, tiles, slope_tile, 0, tiles // 2)

        down(1)
        fed = len(crossed)
        bend(1)
        down(0)
        bend(0)

        for copy in crossed[:fed]:
            copy().wait_send()
        def up(core):
            low = 0
            for part, (count, *order) in enumerate(ORDERS["up"]):
                if core == 0:
                    crossed[fed + part]().wait_recv()

                def up_tile(number, carry, core=core):
                    cols = pl.ds(pl.multiple_of(core * units + number * inner, LANES), inner)
                    for top in range(0, width, 256):
                        tile = dot(first_t[top : top + 256, :], slope[:, cols])
                        if core == 1:
                            give(number * width + top, tile)
                        else:
                            take(third + number * width + top, tile)
                    return carry

                lax.fori_loop(low, low + count, up_tile, 0)
                if core == 1:
                    cross(third + low * width, count * width, low * width)
                else:
                    begin_piece(third + low * width, count * width, order)
                poll()
                low += count

        up(1)

        def first_tile(number, carry):
            cols = pl.ds(pl.multiple_of(number * 256, 256), 256)
            wide[:, cols] = (
                gsec[:, cols]
                + dot(slope[:, :units], upw[0, cols, :], NT)
                + dot(slope[:, units:], upw[1, cols, :], NT)
            )
            return carry

        polled_loop(0, width // 256, first_tile, 0)
        up(0)
        def norm_back(number, carry):
            rows = pl.ds(pl.multiple_of(number * block, block), block)
            grad = wide[rows, :]
            normed = normed1[rows, :]
            scaled = grad * row(gain1)
            back = inverse1[rows, 0:1] * (
                scaled
                - jnp.mean(scaled, axis=-1, keepdims=True)
                - normed * jnp.mean(scaled * normed, axis=-1, keepdims=True)
            )
            wide[rows, :] = back
            gmid16[rows, :] = back.astype(BF16)
            return (
                carry[0] + fold8(back),
                carry[1] + fold8(grad * normed),
                carry[2] + fold8(grad),
            )

        totals = lax.fori_loop(0, seq // block, norm_back, (zero, zero, zero), unroll=4)
        both = [jnp.sum(total, axis=0, keepdims=True) for total in totals]
        both += [jnp.sum(total, axis=0, keepdims=True) for total in later]
        vparts[0] = jnp.zeros(vparts.shape[1:], F32)
        vparts[1] = jnp.zeros(vparts.shape[1:], F32)
        for number, line in enumerate(both):
            vparts[0, number : number + 1, :] = line
            vparts[1, number : number + 1, :] = line
        for core in range(2):
            line = jnp.sum(ups[core], axis=0, keepdims=True)
            for side in range(units // width):
                vparts[1 - core, 6 + side : 7 + side, :] = line[:, side * width : (side + 1) * width]
        poll()
        kept.wait()

    def front(upw, downw):
        pl.run_scoped(
            functools.partial(attend_phase, upw, downw),
            pltpu.VMEM((2,) + qkvw_h.shape, BF16),
            pltpu.VMEM((2 * inner, seq), BF16),
            pltpu.VMEM((seq, seq), jnp.int32),
            pltpu.VMEM((seq, seq), jnp.int32),
            pltpu.VMEM((seq, LANES), F32),
            pltpu.VMEM((heads // 2, 8, 2 * LANES), jnp.int32),
            pltpu.VMEM((heads, seq, seq), BF16),
        )
        pl.run_scoped(
            functools.partial(unit_phase, upw, downw),
            pltpu.VMEM((seq, 2 * units), BF16),
            pltpu.VMEM((seq, 2 * units), BF16),
            pltpu.VMEM((seq, width), BF16),
            pltpu.VMEM((width, seq), BF16),
            pltpu.VMEM((seq, width), F32),
            pltpu.VMEM((seq, width), F32),
            pltpu.VMEM((seq, LANES), F32),
            pltpu.VMEM((seq, width), F32),
            pltpu.VMEM((seq, width), BF16),
            pltpu.VMEM((seq, width), BF16),
        )

    pl.run_scoped(
        front,
        pltpu.VMEM((2, width, units), BF16),
        pltpu.VMEM((2, units, width), BF16),
    )

    def pair_phase(spread, gq, gk, gv, kt, dheads_t, dheads, expo, expo_sem):
        def fetch(pair):
            slot = pair % 2 if isinstance(pair, int) else lax.rem(pair, 2)
            return pltpu.make_async_copy(
                expo_h.at[pl.ds(2 * pair, 2)], expo.at[slot], expo_sem.at[slot]
            )

        fetch(0).start()

        full = len(crossed)
        for copy in crossed[full - len(ORDERS["up"]) :]:
            copy().wait_send()
        at = 2 * third
        other = dot(heads_t[inner:, :], gmid16[...])
        for side in range(split):
            give(side * inner, other[:, side * inner : (side + 1) * inner])
        cross(at, split * inner, 0)
        poll()
        for core in range(2):
            tile = dot(outw[core], gmid16[...], NT)
            for head in range(per):
                rows = slice(core * inner + head * size, core * inner + (head + 1) * size)
                part = tile[head * size : (head + 1) * size] * recip[core * per + head, 0:1, :]
                dheads_t[rows, :] = part.astype(BF16)
        dheads[...] = jnp.transpose(dheads_t[...])
        kt[...] = jnp.transpose(k[...])
        own = dot(heads_t[:inner, :], gmid16[...])
        crossed[full]().wait_recv()
        for side in range(split):
            take(at + side * inner, own[:, side * inner : (side + 1) * inner])
        begin_piece(at, split * inner, ORDERS["out"])
        poll()
        first = lax.broadcasted_iota(jnp.int32, (seq, LANES), 1) < size

        def pair_back(pair, carry):
            cols = pl.ds(pl.multiple_of(pair * LANES, LANES), LANES)
            fetch(pair).wait()

            @pl.when(pair + 1 < heads // 2)
            def _():
                fetch(pair + 1).start()

            slot = lax.rem(pair, 2)
            values, queries = v[:, cols], q[:, cols]
            grads, grads_t = dheads[:, cols], dheads_t[cols, :]
            gvs, gks, gqs = [], [], []
            for side in range(2):
                head = 2 * pair + side
                mine = first if side == 0 else jnp.logical_not(first)
                rows = pl.ds(pl.multiple_of(pair * LANES + side * size, size), size)
                shift = jnp.sum(
                    dheads_t[rows, :].astype(F32) * heads_t[rows, :].astype(F32),
                    axis=0,
                    keepdims=True,
                )
                back = dot(jnp.where(mine, values, jnp.zeros_like(values)), grads_t)
                gscore = expo[slot, side].astype(F32) * (back - shift)
                for tile in range(seq // LANES):
                    spread[pl.ds(tile * seq * 16 + head, seq, stride=16), :] = gscore[
                        :, tile * LANES : (tile + 1) * LANES
                    ]
                gscore = gscore.astype(BF16)
                gvs.append(dot(expo[slot, side], grads))
                gks.append(dot(gscore, queries))
                gqs.append(dot(kt[rows, :], gscore) * 0.125)
            gv[:, cols] = jnp.where(first, gvs[0], gvs[1]).astype(BF16)
            gk[:, cols] = jnp.where(first, gks[0], gks[1]).astype(BF16)
            gq[:, cols] = jnp.transpose(jnp.concatenate(gqs, axis=0)).astype(BF16)
            return carry

        polled_loop(0, heads // 2, pair_back, 0)

    def mix_phase(spread, gq, gk, gv, qkvw, tokens_t):
        l_qkvw = [load(qkvw_h, qkvw.at[0]), load(qkvw_o, qkvw.at[1])]
        tokens_t[...] = jnp.transpose(tokens[...])
        full = len(crossed)
        at = 2 * third + split * inner
        kinds = (gq, gk, gv)
        def mix_back(core):
            for kind in range(3):
                if core == 0:
                    crossed[full + kind]().wait_recv()
                for top in range(0, width, 256):
                    tile = dot(
                        tokens_t[top : top + 256, :],
                        kinds[kind][:, core * inner : (core + 1) * inner],
                    )
                    if core == 1:
                        give(split * inner + kind * width + top, tile)
                    else:
                        take(at + kind * width + top, tile)
                if core == 1:
                    cross(at + kind * width, width, split * inner + kind * width)
                else:
                    begin_piece(at + kind * width, width, ORDERS["mix"][kind])
                poll()

        mix_back(1)
        span = length[me]
        columns = 256
        half_range = LANES // 2
        labels = lax.broadcasted_iota(jnp.int32, (half_range, columns), 0).astype(BF16)
        tab_sum = jnp.zeros((64, half_range), F32)
        for start in range(0, seq, columns):
            here = slice(start, start + columns)
            position = lax.broadcasted_iota(jnp.int32, (1, columns), 1) + start
            inside = (position < span).astype(F32)

            def count(number, carry, here=here, start=start, inside=inside):
                for line in range(64):
                    if line % 16 == 0:
                        place = pl.multiple_of(number * 64 + line, 16)
                        index = bucket[pl.ds(place, 16), here].astype(F32)
                        upper = (index >= half_range).astype(F32)
                        index = (index - upper * half_range).astype(BF16)
                        place = pl.multiple_of(place * 16, 256)
                        grads = jnp.concatenate(
                            [
                                spread[pl.ds(tile * seq * 16 + place, 256), :]
                                for tile in range(start // LANES, (start + columns) // LANES)
                            ],
                            axis=1,
                        )
                    turn = line % 16
                    hot = jnp.where(
                        labels == index[turn : turn + 1, :],
                        jnp.ones((), BF16),
                        jnp.zeros((), BF16),
                    )
                    other = jnp.where(number * 64 + line < span, 1.0 - inside, inside)
                    some = grads[16 * turn : 16 * turn + 16]
                    far = some * other
                    both = jnp.concatenate([some - far, far], axis=0)
                    high = both * upper[turn : turn + 1, :]
                    both = jnp.concatenate([both - high, high], axis=0).astype(BF16)
                    carry = carry + dot(both, hot, NT)
                return carry

            if start == 0:
                tab_sum = polled_loop(0, 2, count, tab_sum)
                mix_back(0)
            tab_sum = polled_loop(0 if start else 2, seq // 64, count, tab_sum)

        for core in range(2):
            mine = slice(core * inner, (core + 1) * inner)
            for number, kind in ((0, gq), (1, gv)):
                line = jnp.sum(fold8(kind[:, mine].astype(F32)), axis=0, keepdims=True)
                vparts[1 - core, 8:9, number * inner : (number + 1) * inner] = line
            for part in range(2):
                lines = []
                for upper in range(2):
                    low = upper * 32 + part * 16 + core * per
                    lines.append(tab_sum[low : low + per])
                cols = slice(part * LANES, (part + 1) * LANES)
                vparts[1 - core, 10 : 10 + per, cols] = jnp.concatenate(lines, axis=1)
        Vectors(vparts, vland, small, bits, kit, vs_sem, vr_sem).run(0)
        poll()

        l_qkvw[0].wait()
        l_qkvw[1].wait()

        def token_tile(number, carry):
            cols = pl.ds(pl.multiple_of(number * 256, 256), 256)
            total = wide[:, cols]
            for core in range(2):
                for kind in range(3):
                    total = total + dot(
                        kinds[kind][:, core * inner : (core + 1) * inner],
                        qkvw[core, kind, cols, :],
                        NT,
                    )
            wide[:, cols] = total
            return carry

        polled_loop(0, width // 256, token_tile, 0)

    per = heads // 2
    size = inner // per

    def back(spread, gq, gk, gv):
        pl.run_scoped(
            functools.partial(pair_phase, spread, gq, gk, gv),
            pltpu.VMEM((2 * inner, seq), BF16),
            pltpu.VMEM((2 * inner, seq), BF16),
            pltpu.VMEM((seq, 2 * inner), BF16),
            pltpu.VMEM((2, 2, seq, seq), BF16),
            pltpu.SemaphoreType.DMA((2,)),
        )
        pl.run_scoped(
            functools.partial(mix_phase, spread, gq, gk, gv),
            pltpu.VMEM((2,) + qkvw_h.shape, BF16),
            pltpu.VMEM((width, seq), BF16),
        )

    pl.run_scoped(
        back,
        pltpu.VMEM((seq // LANES * seq * 16, LANES), F32),
        pltpu.VMEM((seq, 2 * inner), BF16),
        pltpu.VMEM((seq, 2 * inner), BF16),
        pltpu.VMEM((seq, 2 * inner), BF16),
    )
    done = store(wide, gtok_h)
    for number in range(polls[0], 1 + max(number for number in plan if number != "tail")):
        run_steps(number)
    run_steps("tail")
    done.wait()
    for piece in kit.pieces:
        piece.finish()
    for copy in crossed[-4:]:
        copy().wait_send()
    for number in range(len(halves)):
        half(number).wait_send()


def layer(plan, bits, operands):
    tokens, qkvw, qvb, tab, outw, upw, upb, downw = operands[:8]
    seq, width = tokens.shape
    inner = qkvw.shape[2]
    units = upw.shape[1]
    heads = 2 * tab.shape[0]
    shape = jax.ShapeDtypeStruct
    here = pl.BlockSpec(memory_space=pltpu.VMEM)
    away = pl.BlockSpec(memory_space=pl.ANY)
    scalar = pl.BlockSpec(memory_space=pltpu.SMEM)
    rows = (3 * width * inner + inner * width + 2 * width * units) // inner
    lands = rows - (rows >> 4) + (bits - 4) * (rows >> 4)
    pieces = len(ORDERS["down"]) + len(ORDERS["up"]) + 4
    cuts = [one for _, one, _ in ORDERS["down"] + ORDERS["up"]]
    cuts += [ORDERS["out"][0]] + [one for one, _ in ORDERS["mix"]]
    leave = sum(3 if axis == "D" else 1 for one in cuts for axis in one)
    more = pieces * (bits - 4)
    return pl.pallas_call(
        functools.partial(layer_kernel, plan, bits),
        out_shape=(
            shape((rows, inner), BF16),
            shape((seq, width), F32),
            shape((seq, width), BF16),
            shape((16, width), F32),
            shape(qkvw.shape, BF16),
            shape(outw.shape, BF16),
            shape(upw.shape, BF16),
            shape(downw.shape, BF16),
            shape((heads, seq, seq), BF16),
        ),
        in_specs=[away] * 10 + [here] * 7 + [scalar],
        out_specs=(away, away, away, here) + (away,) * 5,
        scratch_shapes=[
            pltpu.VMEM((rows, inner), BF16),
            pltpu.VMEM((rows // 3, inner), BF16),
            pltpu.VMEM((rows, inner), BF16),
            pltpu.VMEM((lands, inner), BF16),
            pltpu.VMEM((seq, width), BF16),
            pltpu.VMEM((2,) + qvb.shape, F32),
            pltpu.VMEM((2,) + tab.shape, F32),
            pltpu.VMEM(upb.shape, F32),
            pltpu.VMEM(upb.shape, F32),
            pltpu.VMEM((2, 1, units), F32),
            pltpu.VMEM((2,) + outw.shape, BF16),
            pltpu.VMEM((seq, 2 * inner), BF16),
            pltpu.VMEM((seq, 2 * inner), BF16),
            pltpu.VMEM((seq, 2 * inner), BF16),
            pltpu.VMEM((2 * inner, seq), BF16),
            pltpu.VMEM((heads, 8, seq), F32),
            pltpu.VMEM((seq, seq), BF16),
            pltpu.VMEM((seq, width), F32),
            pltpu.VMEM((seq, width), BF16),
            pltpu.VMEM((seq, width), BF16),
            pltpu.VMEM((2, 8, units), F32),
            pltpu.VMEM((bits + 1, 16, width), F32),
            pltpu.VMEM((bits + 1, 16, width), F32),
            pltpu.SemaphoreType.DMA((24,)),
            pltpu.SemaphoreType.DMA((8,)),
            pltpu.SemaphoreType.DMA((leave + more,)),
            pltpu.SemaphoreType.DMA((2 * leave + more,)),
            pltpu.SemaphoreType.DMA((pieces,)),
            pltpu.SemaphoreType.DMA((pieces,)),
            pltpu.SemaphoreType.DMA((pieces,)),
            pltpu.SemaphoreType.DMA((bits + 1,)),
            pltpu.SemaphoreType.DMA((bits + 1,)),
            pltpu.SemaphoreType.DMA((7,)),
            pltpu.SemaphoreType.DMA((7,)),
        ],
        compiler_params=pltpu.CompilerParams(
            collective_id=0, has_side_effects=True, vmem_limit_bytes=VMEM_LIMIT
        ),
    )(*operands)


def finish_kernel(
    flat_h,
    out_h,
    gtok_h,
    small,
    out_f,
    gtok_f,
    mix_f,
    gqv,
    gtab,
    gout_f,
    goutb,
    gain1,
    shift1,
    up_f,
    gupb,
    down_f,
    gdownb,
    gain2,
    shift2,
    flat,
    mix,
    gout,
    up,
    down,
    gtok,
    out,
    in_sem,
    out_sem,
):
    rows, inner = flat.shape
    units, width = down.shape
    split = width // inner
    third = rows // 3
    copies = []
    tiles = units // 256
    span = 256 * split
    sizes = (
        [span] * tiles + [width] * (units // inner) + [split * inner] + [width] * 3
    )
    loads = []
    at = 0
    for number, size in enumerate(sizes):
        here = pl.ds(at, size)
        loads.append(pltpu.make_async_copy(flat_h.at[here, :], flat.at[here, :], in_sem.at[number]))
        loads[-1].start()
        at += size

    for source, target in ((gtok_h, gtok), (out_h, out)):
        loads.append(pltpu.make_async_copy(source, target, in_sem.at[len(loads)]))
        loads[-1].start()

    def store(source, target):
        copies.append(pltpu.make_async_copy(source, target, out_sem.at[len(copies)]))
        copies[-1].start()

    def wide(start, size):
        return flat[start : start + size, :].astype(F32)

    for tile in range(tiles):
        loads[tile].wait()
        here = slice(tile * 256, tile * 256 + 256)
        for side in range(split):
            down[here, side * inner : (side + 1) * inner] = wide(tile * span + side * 256, 256)
        here = pl.ds(tile * 256, 256)
        store(down.at[here, :], down_f.at[here, :])
    for part in range(units // inner):
        loads[tiles + part].wait()
        cols = pl.ds(part * inner, inner)
        up[:, cols] = wide(third + part * width, width)
        store(up.at[:, cols], up_f.at[:, cols])
    at = 2 * third
    loads[-6].wait()
    for side in range(split):
        gout[:, side * inner : (side + 1) * inner] = wide(at + side * inner, inner)
    store(gout, gout_f)
    at += split * inner
    for kind in range(3):
        loads[kind - 5].wait()
        mix[kind] = wide(at + kind * width, width)
        store(mix.at[kind], mix_f.at[kind])
    loads[-2].wait()
    store(gtok, gtok_f)
    loads[-1].wait()
    store(out, out_f)
    for number, vector in enumerate((goutb, gain1, shift1, gdownb, gain2, shift2)):
        vector[...] = small[number : number + 1, :].reshape(width)
    gupb[...] = jnp.concatenate(
        [small[6 + side : 7 + side, :] for side in range(units // width)], axis=1
    ).reshape(units)
    for kind in range(2):
        gqv[kind : kind + 1, :] = small[8:9, kind * inner : (kind + 1) * inner]
    gtab[...] = small[10 : 10 + gtab.shape[0], : gtab.shape[1]]
    for copy in copies:
        copy.wait()


def finish(flat, small, out, grad_tokens, width, units, heads):
    shape = jax.ShapeDtypeStruct
    here = pl.BlockSpec(memory_space=pltpu.VMEM)
    away = pl.BlockSpec(memory_space=pl.ANY)
    inner = flat.shape[1]
    vector = shape((width,), F32)
    got = pl.pallas_call(
        finish_kernel,
        out_shape=(
            shape(out.shape, BF16),
            shape(grad_tokens.shape, F32),
            shape((3, width, inner), F32),
            shape((2, inner), F32),
            shape((heads, 2 * LANES), F32),
            shape((inner, width), F32),
            vector,
            vector,
            vector,
            shape((width, units), F32),
            shape((units,), F32),
            shape((units, width), F32),
            vector,
            vector,
            vector,
        ),
        in_specs=[away] * 3 + [here],
        out_specs=(away, away, away, here, here, away, here, here, here, away, here, away)
        + (here,) * 3,
        scratch_shapes=[
            pltpu.VMEM(flat.shape, BF16),
            pltpu.VMEM((3, width, inner), F32),
            pltpu.VMEM((inner, width), F32),
            pltpu.VMEM((width, units), F32),
            pltpu.VMEM((units, width), F32),
            pltpu.VMEM(grad_tokens.shape, F32),
            pltpu.VMEM(out.shape, BF16),
            pltpu.SemaphoreType.DMA((units // 256 + units // inner + 6,)),
            pltpu.SemaphoreType.DMA((units // 256 + units // inner + 6,)),
        ],
        compiler_params=pltpu.CompilerParams(vmem_limit_bytes=VMEM_LIMIT),
    )(flat, out, grad_tokens, small)
    got = list(got)
    got[2] = jnp.transpose(got[2], (1, 0, 2))
    got[4] = got[4].T
    return tuple(got)


def order_of_steps(bits):
    pieces = len(ORDERS["down"]) + len(ORDERS["up"]) + 4
    plan = dict(PAUSES)
    known = {step for steps in PAUSES.values() for step in steps} | set(TAIL)
    more = tuple((pieces, step) for step in range(1, bits + 2) if (pieces, step) not in known)
    plan["tail"] = TAIL + more
    return plan


def on_device(
    dp,
    tokens,
    qkv_weight,
    qv_bias,
    rel_table,
    out_weight,
    out_bias,
    norm1_gain,
    norm1_bias,
    up_weight,
    up_bias,
    down_weight,
    down_bias,
    norm2_gain,
    norm2_bias,
    rel_bucket,
    query_len,
    key_mask,
    upstream,
):
    width = tokens.shape[1]
    units = up_weight.shape[1]
    bits = int(math.log2(dp))
    flat, grad_tokens, out, small = layer(
        order_of_steps(bits),
        bits,
        (
            tokens,
            jnp.transpose(qkv_weight, (1, 0, 2)),
            qv_bias,
            rel_table.T,
            out_weight,
            up_weight,
            up_bias,
            down_weight,
            upstream,
            rel_bucket,
            out_bias,
            norm1_gain,
            norm1_bias,
            down_bias,
            norm2_gain,
            norm2_bias,
            key_mask,
            query_len,
        ),
    )[:4]
    return finish(flat, small, out, grad_tokens, width, units, rel_table.shape[1])


def solution(mesh):
    rows = P(("dp", "tensor"), None)
    whole = P()
    in_specs = (
        rows,
        P(None, None, "tensor"),
        P(None, "tensor"),
        P(None, "tensor"),
        P("tensor", None),
        whole,
        whole,
        whole,
        P(None, "tensor"),
        P("tensor"),
        P("tensor", None),
        whole,
        whole,
        whole,
        whole,
        P("dp"),
        P("dp", None),
        rows,
    )
    out_specs = (
        rows,
        rows,
        P(None, None, "tensor"),
        P(None, "tensor"),
        P(None, "tensor"),
        P("tensor", None),
        whole,
        whole,
        whole,
        P(None, "tensor"),
        P("tensor"),
        P("tensor", None),
        whole,
        whole,
        whole,
    )
    return jax.shard_map(
        functools.partial(on_device, mesh.shape["dp"]),
        mesh=mesh,
        in_specs=in_specs,
        out_specs=out_specs,
        check_vma=False,
    )
```

```python
import functools
import math

import jax
import jax.numpy as jnp
from jax import lax
from jax.experimental import pallas as pl
from jax.experimental.pallas import tpu as pltpu
from jax.sharding import PartitionSpec as P

EPSILON = 1e-05
FAR_BELOW = -1000000000.0
MESH = pl.DeviceIdType.MESH
F32 = jnp.float32
BF16 = jnp.bfloat16
LANES = 128
NT = (((1,), (1,)), ((), ()))
TN = (((0,), (0,)), ((), ()))
VMEM_LIMIT = 62 * 2**20
ORDERS = {
    "down": ((2, "xyD", "yxD"), (3, "yxzZ", "zZxy"), (1, "xyzZ", "xzZy")),
    "up": ((2, "xyzZ", "xyzZ"), (1, "xyzZ", "zZxy"), (1, "yxzZ", "yzZx")),
    "out": ("xyzZ", "yxzZ"),
    "mix": (("xyD", "yxD"), ("yxD", "yxD"), ("yxD", "xyD")),
}
PAUSES = {
    12: ((0, 1),),
    15: ((2, 1),),
    16: ((1, 1),),
    18: ((0, 2),),
    19: ((5, 1),),
    20: ((2, 2),),
    22: ((3, 1), (0, 3), (4, 1), (2, 3)),
    24: ((1, 2),),
    25: ((6, 1), (0, 4), (3, 2), (2, 4)),
    26: ((5, 2),),
    27: ((1, 3),),
    28: ((4, 2),),
    29: ((6, 2),),
    31: ((3, 3),),
    32: ((2, 5), (0, 5)),
    33: ((5, 3),),
    35: ((1, 4), (4, 3)),
    36: ((6, 3),),
    37: ((7, 1), (3, 4), (2, 6)),
    39: ((5, 4),),
    42: ((6, 4), (8, 1)),
    43: ((9, 1), (3, 5)),
    44: ((5, 5),),
    45: ((7, 2), (6, 5)),
    46: ((8, 2), (2, 7)),
    47: ((1, 5), (0, 6), (3, 6), (4, 4)),
    48: ((5, 6), (10, 1), (9, 2)),
    50: ((7, 3), (6, 6), (2, 8)),
}
TAIL = ((8, 3), (3, 7), (10, 2), (4, 5), (1, 6), (5, 7), (10, 3), (6, 7), (9, 3), (7, 4), (8, 4), (5, 8), (4, 6), (3, 8), (7, 5), (10, 4), (1, 7), (9, 4), (6, 8), (4, 7), (8, 5), (10, 5), (7, 6), (9, 5), (1, 8), (8, 6), (4, 8), (9, 6))


def dot(left, right, dims=None):
    if dims is None:
        return jnp.dot(left, right, preferred_element_type=F32)
    return lax.dot_general(left, right, dims, preferred_element_type=F32)


def other_core():
    return {"tensor": 1 - lax.axis_index("tensor")}


def row(ref):
    return ref[...].reshape(1, ref.shape[-1])


def fold8(block):
    return jnp.sum(block.reshape(block.shape[0] // 8, 8, block.shape[1]), axis=0)


def pack_tables(tab, packed, core):
    step = jnp.maximum(jnp.max(jnp.abs(tab[core])), 1e-30) / 32000.0
    inverse = 1.0 / step
    heads = tab.shape[1]
    for pair in range(heads // 2):
        high = tab[core, 2 * pair : 2 * pair + 1, :] * inverse
        low = jnp.round(tab[core, 2 * pair + 1 : 2 * pair + 2, :] * inverse)
        high = jnp.round(high - low * (1 / 65536.0))
        both = high.astype(jnp.int32) * 65536 + low.astype(jnp.int32)
        packed[core * (heads // 2) + pair] = jnp.broadcast_to(both, packed.shape[1:])
    return step


def attend_pair(pair, q, k, vt, packed, bucket, valid, length, step, expo, heads_t, recip):
    seq = q.shape[0]
    cols = pl.ds(pl.multiple_of(pair * LANES, LANES), LANES)
    keys = k[:, cols]
    queries = q[:, cols]
    lane = lax.broadcasted_iota(jnp.int32, (seq, LANES), 1)
    in_query = lax.broadcasted_iota(jnp.int32, (seq, LANES), 0) < length
    terms = packed[pair, 0:1, :]
    near = jnp.broadcast_to(terms[:, :LANES], (seq, LANES))
    far = jnp.broadcast_to(terms[:, LANES:], (seq, LANES))
    same = jnp.where(in_query, far, near)
    swap = jnp.where(in_query, near, far)
    pieces = ([], [])
    for start in range(0, seq, LANES):
        index = bucket[:, start : start + LANES]
        got = jnp.take_along_axis(same, index, axis=1, mode="promise_in_bounds")
        if start == 0:
            turned = jnp.take_along_axis(swap, index, axis=1, mode="promise_in_bounds")
            got = jnp.where(lane < length, turned, got)
        pieces[0].append(got.astype(F32) * (step * (1 / 65536.0)))
        pieces[1].append(jnp.left_shift(got, 16).astype(F32) * (step * (1 / 65536.0)))
    first = lane < LANES // 2
    real = jnp.concatenate([valid[...] > 0] * (seq // LANES), axis=1)
    for side in range(2):
        mine = first if side == 0 else jnp.logical_not(first)
        scores = dot(jnp.where(mine, keys, jnp.zeros_like(keys)), queries, NT)
        scores = scores + jnp.concatenate(pieces[side], axis=1)
        scores = jnp.where(real, scores, FAR_BELOW)
        highest = jnp.max(scores, axis=0, keepdims=True)
        weights = jnp.exp(scores - highest).astype(BF16)
        expo[2 * pair + side] = weights
        rows = pl.ds(pl.multiple_of(pair * LANES + side * 64, 64), 64)
        values = jnp.concatenate([vt[rows, :], jnp.ones((16, seq), BF16)], axis=0)
        got = dot(values, weights)
        inverse = 1.0 / got[64:65]
        heads_t[rows, :] = (got[:64] * inverse).astype(BF16)
        recip[2 * pair + side] = jnp.broadcast_to(inverse, recip.shape[1:])


def dp_stride(bits):
    first, second = 1 << bits[0], 1 << bits[1]
    if first == second:
        return first
    return first + lax.axis_index("tensor") * (second - first)


def dp_side(bits):
    return lax.rem(lax.div(lax.axis_index("dp"), dp_stride(bits)), 2)


def dp_partner(bits):
    return {"dp": lax.axis_index("dp") + (1 - 2 * dp_side(bits)) * dp_stride(bits)}


def dp_quarter(ahead):
    return lax.rem(lax.div(lax.axis_index("dp"), 4) + ahead, 4)


def dp_ahead(ahead):
    return {"dp": lax.axis_index("dp") + 4 * (dp_quarter(ahead) - dp_quarter(0))}


def flat_rows(start, size):
    return pl.ds(pl.multiple_of(start, 16), size)


class Kit:
    def __init__(self, acc, landing, result, send_sem, recv_sem, local_sem):
        self.acc, self.landing, self.result = acc, landing, result
        self.send_sem, self.recv_sem, self.local_sem = send_sem, recv_sem, local_sem
        self.used = [0, 0]
        self.landed = 0
        self.pieces = []

    def slot(self, kind):
        self.used[kind] += 1
        return self.used[kind] - 1

    def room(self, size):
        self.landed += size
        return self.landed - size

    def remote(self, slot, source, target, device):
        return pltpu.make_async_remote_copy(
            src_ref=source,
            dst_ref=target,
            send_sem=self.send_sem.at[slot[0]],
            recv_sem=self.recv_sem.at[slot[1]],
            device_id=device,
            device_id_type=MESH,
        )


class Piece:
    def __init__(self, start, length, stages, extra, kit):
        self.start = start
        self.stages, self.extra = stages, extra
        self.kit = kit
        self.number = len(kit.pieces)
        self.steps = 2 * len(stages) + 1
        kit.pieces.append(self)
        self.sizes = [length]
        self.cutting, self.spreading = [], []
        for stage in stages:
            parts = 4 if stage is None else 2
            size = self.sizes[-1] // parts
            self.sizes.append(size)
            leaving = [kit.slot(0) for _ in range(parts - 1)]
            self.cutting.append([((slot, kit.slot(1)), kit.room(size)) for slot in leaving])
            self.spreading.append([(slot, kit.slot(1)) for slot in leaving])
        self.crossing = [((kit.slot(0), kit.slot(1)), kit.room(self.sizes[-1])) for _ in extra]

    def begin(self, levels):
        at = self.start
        for level in range(levels):
            stage = self.stages[level]
            at = at + (dp_quarter(0) if stage is None else dp_side(stage)) * self.sizes[level + 1]
        return at

    def partners(self, stage):
        if stage is None:
            return [(dp_quarter(ahead), dp_ahead(ahead)) for ahead in (1, 2, 3)]
        return [(1 - dp_side(stage), dp_partner(stage))]

    def cut(self, level):
        kit, size = self.kit, self.sizes[level + 1]
        at = self.begin(level)
        return [
            kit.remote(
                slot,
                kit.acc.at[flat_rows(at + part * size, size), :],
                kit.landing.at[pl.ds(room, size), :],
                device,
            )
            for (slot, room), (part, device) in zip(
                self.cutting[level], self.partners(self.stages[level])
            )
        ]

    def swap(self, number):
        kit = self.kit
        slot, room = self.crossing[number]
        size = self.sizes[-1]
        return kit.remote(
            slot,
            kit.acc.at[flat_rows(self.begin(len(self.stages)), size), :],
            kit.landing.at[pl.ds(room, size), :],
            dp_partner(self.extra[number]),
        )

    def keep(self):
        kit = self.kit
        mine = flat_rows(self.begin(len(self.stages)), self.sizes[-1])
        return pltpu.make_async_copy(
            kit.acc.at[mine, :], kit.result.at[mine, :], kit.local_sem.at[self.number]
        )

    def spread(self, level):
        kit = self.kit
        mine = flat_rows(self.begin(level + 1), self.sizes[level + 1])
        source = kit.acc if level == len(self.stages) - 1 else kit.result
        return [
            kit.remote(slot, source.at[mine, :], kit.result.at[mine, :], device)
            for slot, (_, device) in zip(
                self.spreading[level], self.partners(self.stages[level])
            )
        ]

    def add(self, target, rooms, size):
        kit = self.kit
        chunk = math.gcd(size, 192)

        def some(number, carry):
            there = flat_rows(target + number * chunk, chunk)
            total = kit.acc[there, :].astype(F32)
            for room in rooms:
                total = total + kit.landing[flat_rows(room + number * chunk, chunk), :].astype(F32)
            kit.acc[there, :] = total.astype(BF16)
            return carry

        lax.fori_loop(0, size // chunk, some, 0)

    def run(self, step):
        levels = len(self.stages)
        if 0 < step <= levels:
            for copy in self.cut(step - 1):
                copy.wait_recv()
            rooms = [room for _, room in self.cutting[step - 1]]
            self.add(self.begin(step), rooms, self.sizes[step])
        if step < levels:
            for copy in self.cut(step):
                copy.start()
            return
        if step == levels:
            for number in range(len(self.extra)):
                both = self.swap(number)
                both.start()
                both.wait()
                self.add(self.begin(levels), [self.crossing[number][1]], self.sizes[-1])
            self.keep().start()
        else:
            for copy in self.spread(2 * levels - step):
                copy.wait_recv()
            if step == levels + 1:
                self.keep().wait()
        if step < 2 * levels:
            for copy in self.cut(2 * levels - 1 - step):
                copy.wait_send()
            for copy in self.spread(2 * levels - 1 - step):
                copy.start()

    def finish(self):
        for level in range(len(self.stages)):
            for copy in self.spread(level):
                copy.wait_send()


class Vectors:
    def __init__(self, parts, landing, result, bits, kit, send_sem, recv_sem):
        self.parts, self.landing, self.result = parts, landing, result
        self.bits = bits
        self.steps = bits + 2
        self.send_sem, self.recv_sem = send_sem, recv_sem
        kit.pieces.append(self)

    def exchange(self, step):
        return pltpu.make_async_remote_copy(
            src_ref=self.parts.at[step],
            dst_ref=self.landing.at[step],
            send_sem=self.send_sem.at[step],
            recv_sem=self.recv_sem.at[step],
            device_id=other_core() if step == 0 else dp_partner((step - 1, step - 1)),
            device_id_type=MESH,
        )

    def run(self, step):
        if step > 0:
            self.exchange(step - 1).wait_recv()
            total = self.parts[max(step - 1, 1)] + self.landing[step - 1]
            if step <= self.bits:
                self.parts[step] = total
            else:
                self.result[...] = total
        if step <= self.bits:
            self.exchange(step).start()

    def finish(self):
        for step in range(self.bits + 1):
            self.exchange(step).wait_send()


def layer_kernel(
    plan,
    bits,
    tokens_h,
    qkvw_h,
    qvb_h,
    tab_h,
    outw_h,
    upw_h,
    upb_h,
    downw_h,
    upstream_h,
    bucket_h,
    outb,
    gain1,
    shift1,
    downb,
    gain2,
    shift2,
    mask,
    length,
    result_h,
    gtok_h,
    out_h,
    small,
    qkvw_o,
    outw_o,
    upw_o,
    downw_o,
    expo_h,
    acc,
    xsend,
    xrecv,
    landing,
    tokens,
    qvb,
    tab,
    upb,
    upb_other,
    upb_rows,
    outw,
    q,
    k,
    v,
    heads_t,
    recip,
    bucket,
    wide,
    gmid16,
    upstream,
    ups,
    vparts,
    vland,
    in_sem,
    out_sem,
    send_sem,
    recv_sem,
    local_sem,
    xs_sem,
    xr_sem,
    vs_sem,
    vr_sem,
    ws_sem,
    wr_sem,
):
    seq, width = tokens.shape
    inner = outw.shape[1]
    units = upw_h.shape[1]
    heads = recip.shape[0]
    pairs = inner // LANES
    split = width // inner
    third = acc.shape[0] // 3

    barrier = pltpu.get_barrier_semaphore()
    pl.semaphore_signal(barrier, inc=1, device_id=other_core(), device_id_type=MESH)
    for bit in range(bits):
        pl.semaphore_signal(barrier, inc=1, device_id=dp_partner((bit, bit)), device_id_type=MESH)
    pl.semaphore_signal(
        barrier,
        inc=1,
        device_id={"dp": lax.axis_index("dp") + 12 - 8 * dp_quarter(0)},
        device_id_type=MESH,
    )

    used, stored = [], []

    def load(source, target):
        copy = pltpu.make_async_copy(source, target, in_sem.at[len(used)])
        used.append(copy)
        copy.start()
        return copy

    loaded = []

    def early(source, target):
        number = len(used)
        used.append(None)
        loaded.append(lambda: pltpu.make_async_copy(source, target(), in_sem.at[number]))
        loaded[-1]().start()

    def store(source, target):
        copy = pltpu.make_async_copy(source, target, out_sem.at[len(stored)])
        stored.append(copy)
        copy.start()
        return copy

    halves = [
        (qkvw_h, qkvw_o),
        (qvb_h, qvb.at[1]),
        (tab_h, tab.at[1]),
        (outw_h, outw_o),
        (upw_h, upw_o),
        (upb_h, upb_other),
        (downw_h, downw_o),
    ]

    def half(number):
        source, target = halves[number]
        return pltpu.make_async_remote_copy(
            src_ref=source,
            dst_ref=target,
            send_sem=ws_sem.at[number],
            recv_sem=wr_sem.at[number],
            device_id=other_core(),
            device_id_type=MESH,
        )

    kit = Kit(acc, landing, result_h, send_sem, recv_sem, local_sem)
    extra = tuple((bit, bit) for bit in range(4, bits))
    crossed = []

    def cross(start, size, place):
        number = len(crossed)

        def copy():
            return pltpu.make_async_remote_copy(
                src_ref=xsend.at[pl.ds(place, size), :],
                dst_ref=xrecv.at[pl.ds(start, size), :],
                send_sem=xs_sem.at[number],
                recv_sem=xr_sem.at[number],
                device_id=other_core(),
                device_id_type=MESH,
            )

        copy().start()
        crossed.append(copy)

    polls = [0]

    def run_steps(number):
        for piece, step in plan.get(number, ()):
            kit.pieces[piece].run(step)

    def poll():
        run_steps(polls[0])
        polls[0] += 1

    def polled_loop(low, high, body, initial, every=1):
        start = polls[0]
        pauses = (high - low) // every
        polls[0] += pauses
        busy = [number for number in range(pauses) if plan.get(start + number)]

        def turn(index, carry):
            carry = body(index, carry)
            for number in busy:

                @pl.when(index == low + (number + 1) * every - 1)
                def _():
                    run_steps(start + number)

            return carry

        return lax.fori_loop(low, high, turn, initial)

    def begin_piece(start, size, orders):
        order = tuple(
            None if one == "D" else ("xyzZ".index(one), "xyzZ".index(two))
            for one, two in zip(*orders)
        )
        fresh = Piece(start, size, order, extra, kit)
        if not any((fresh.number, 0) in steps for steps in plan.values()):
            fresh.run(0)

    def give(place, tile):
        xsend[flat_rows(place, tile.shape[0]), :] = tile.astype(BF16)

    def take(start, tile):
        there = flat_rows(start, tile.shape[0])
        acc[there, :] = (tile + xrecv[there, :].astype(F32)).astype(BF16)

    me = lax.axis_index("tensor")

    def attend_phase(upw, downw, qkvw, vt, bucket_i, bucket_t, valid, packed, expo):
        l_tokens = load(tokens_h, tokens)
        l_qkvw = load(qkvw_h, qkvw.at[0])
        l_qvb = load(qvb_h, qvb.at[0])
        l_bucket = load(bucket_h, bucket_i)
        l_tab = load(tab_h, tab.at[0])
        l_late = [load(outw_h, outw.at[0]), load(upb_h, upb)]
        early(upw_h, lambda: upw.at[0])
        early(downw_h, lambda: downw.at[0])
        early(upstream_h, lambda: upstream)
        span = length[me]
        mine = mask[pl.ds(me, 1), :].astype(F32)
        valid[...] = jnp.transpose(jnp.broadcast_to(mine, (LANES, seq)))

        def mix(core):
            rows = tokens[...]
            cols = slice(core * inner, (core + 1) * inner)
            query = dot(rows, qkvw[core, 0])
            q[:, cols] = ((query + qvb[core, 0:1, :]) * 0.125).astype(BF16)
            k[:, cols] = dot(rows, qkvw[core, 1]).astype(BF16)
            value = (dot(rows, qkvw[core, 2]) + qvb[core, 1:2, :]).astype(BF16)
            v[:, cols] = value
            vt[cols, :] = jnp.transpose(value)

        l_tokens.wait()
        l_qkvw.wait()
        l_qvb.wait()
        mix(0)
        pl.semaphore_wait(barrier, 2 + bits)
        for number in range(3):
            half(number).start()
        l_bucket.wait()
        bucket_t[...] = jnp.transpose(bucket_i[...])
        bucket[...] = bucket_t[...].astype(BF16)
        l_tab.wait()

        def attend(step, pair, carry):
            attend_pair(pair, q, k, vt, packed, bucket_t, valid, span, step, expo, heads_t, recip)
            return carry

        attend_own = functools.partial(attend, pack_tables(tab, packed, 0))

        kept = []

        def keep(low, high):
            here = pl.ds(2 * low, 2 * (high - low))
            kept.append(store(expo.at[here], expo_h.at[here]))

        lax.fori_loop(0, 2, attend_own, 0, unroll=2)
        half(0).wait_recv()
        half(1).wait_recv()
        half(2).wait_recv()
        l_other = load(qkvw_o, qkvw.at[1])
        for number in range(3, 6):
            half(number).start()
        lax.fori_loop(2, pairs, attend_own, 0, unroll=2)
        keep(0, pairs)
        l_other.wait()
        mix(1)
        attend_other = functools.partial(attend, pack_tables(tab, packed, 1))
        lax.fori_loop(pairs, pairs + 1, attend_other, 0)
        keep(pairs, pairs + 1)
        half(6).start()
        half(3).wait_recv()
        l_late.append(load(outw_o, outw.at[1]))
        lax.fori_loop(pairs + 1, 2 * pairs, attend_other, 0, unroll=2)
        keep(pairs + 1, 2 * pairs)
        half(4).wait_recv()
        early(upw_o, lambda: upw.at[1])
        for copy in l_late:
            copy.wait()
        lower = jnp.transpose(heads_t[...])

        def project(tile, carry):
            cols = pl.ds(pl.multiple_of(tile * 256, 256), 256)
            wide[:, cols] = dot(lower[:, :inner], outw[0, :, cols]) + dot(
                lower[:, inner:], outw[1, :, cols]
            )
            return carry

        lax.fori_loop(0, width // 256, project, 0, unroll=3)
        for copy in kept:
            copy.wait()

    def unit_phase(
        upw, downw, act, slope, first, first_t, first32, normed1, inverse1, gsec, gbr, out
    ):
        half(5).wait_recv()
        upb_rows[0] = row(upb)
        upb_rows[1] = row(upb_other)
        block = 128

        def norm_one(number, carry):
            rows = pl.ds(pl.multiple_of(number * block, block), block)
            value = wide[rows, :] + row(outb) + tokens[rows, :].astype(F32)
            center = value - jnp.mean(value, axis=-1, keepdims=True)
            inverse = lax.rsqrt(jnp.mean(center * center, axis=-1, keepdims=True) + EPSILON)
            normed = center * inverse
            result = normed * row(gain1) + row(shift1)
            normed1[rows, :] = normed
            inverse1[rows, :] = jnp.broadcast_to(inverse, (block, LANES))
            first32[rows, :] = result
            first[rows, :] = result.astype(BF16)
            return carry

        lax.fori_loop(0, seq // block, norm_one, 0)

        for core in range(2):
            loaded[3 * core]().wait()

            def expand(tile, carry, core=core):
                cols = pl.ds(pl.multiple_of(tile * 256, 256), 256)
                here = pl.ds(pl.multiple_of(core * units + tile * 256, 256), 256)
                hidden = dot(first[...], upw[core, :, cols]) + upb_rows[core, :, cols]
                chance = 0.5 * (1.0 + lax.erf(hidden * math.sqrt(0.5)))
                density = jnp.exp(hidden * hidden * -0.5) * (1.0 / math.sqrt(2.0 * math.pi))
                act[:, here] = (hidden * chance).astype(BF16)
                slope[:, here] = (chance + hidden * density).astype(BF16)
                return carry

            lax.fori_loop(0, units // 256, expand, 0, unroll=2)
        half(6).wait_recv()
        l_down = load(downw_o, downw.at[1])
        first_t[...] = jnp.transpose(first[...])
        loaded[1]().wait()
        l_down.wait()

        def reduce_units(tile, carry):
            cols = pl.ds(pl.multiple_of(tile * 256, 256), 256)
            wide[:, cols] = dot(act[:, :units], downw[0, :, cols]) + dot(
                act[:, units:], downw[1, :, cols]
            )
            return carry

        lax.fori_loop(0, width // 256, reduce_units, 0, unroll=3)
        loaded[2]().wait()

        def norm_two(number, carry):
            rows = pl.ds(pl.multiple_of(number * block, block), block)
            value = wide[rows, :] + row(downb) + first32[rows, :]
            center = value - jnp.mean(value, axis=-1, keepdims=True)
            inverse = lax.rsqrt(jnp.mean(center * center, axis=-1, keepdims=True) + EPSILON)
            normed = center * inverse
            out[rows, :] = (normed * row(gain2) + row(shift2)).astype(BF16)
            grad = upstream[rows, :].astype(F32)
            scaled = grad * row(gain2)
            back = inverse * (
                scaled
                - jnp.mean(scaled, axis=-1, keepdims=True)
                - normed * jnp.mean(scaled * normed, axis=-1, keepdims=True)
            )
            gsec[rows, :] = back
            gbr[rows, :] = back.astype(BF16)
            return (
                carry[0] + fold8(back),
                carry[1] + fold8(grad * normed),
                carry[2] + fold8(grad),
            )

        zero = jnp.zeros((8, width), F32)
        later = lax.fori_loop(0, seq // block, norm_two, (zero, zero, zero))
        kept = store(out, out_h)

        tiles = units // 256
        span = 256 * split

        def down(core):
            low = 0
            for part, (count, *order) in enumerate(ORDERS["down"]):
                if core == 0:
                    crossed[part]().wait_recv()

                def down_tile(number, carry, core=core):
                    cols = pl.ds(pl.multiple_of(core * units + number * 256, 256), 256)
                    tile = dot(act[:, cols], gbr[...], TN)
                    for side in range(split):
                        (give if core == 1 else take)(
                            number * span + side * 256,
                            tile[:, side * inner : (side + 1) * inner],
                        )
                    return carry

                lax.fori_loop(low, low + count, down_tile, 0)
                if core == 1:
                    cross(low * span, count * span, low * span)
                else:
                    begin_piece(low * span, count * span, order)
                    poll()
                low += count

        def bend(core):
            def slope_tile(number, carry):
                here = pl.ds(pl.multiple_of(number * 256, 256), 256)
                cols = pl.ds(pl.multiple_of(core * units + number * 256, 256), 256)
                tile = dot(gbr[...], downw[core, here, :], NT) * slope[:, cols].astype(F32)
                tile = tile.astype(BF16)
                slope[:, cols] = tile
                ups[core, :, here] = fold8(tile.astype(F32))
                return carry

            polled_loop(0, tiles, slope_tile, 0, tiles // 2)

        down(1)
        fed = len(crossed)
        bend(1)
        down(0)
        bend(0)

        for copy in crossed[:fed]:
            copy().wait_send()
        def up(core):
            low = 0
            for part, (count, *order) in enumerate(ORDERS["up"]):
                if core == 0:
                    crossed[fed + part]().wait_recv()

                def up_tile(number, carry, core=core):
                    cols = pl.ds(pl.multiple_of(core * units + number * inner, LANES), inner)
                    for top in range(0, width, 256):
                        tile = dot(first_t[top : top + 256, :], slope[:, cols])
                        if core == 1:
                            give(number * width + top, tile)
                        else:
                            take(third + number * width + top, tile)
                    return carry

                lax.fori_loop(low, low + count, up_tile, 0)
                if core == 1:
                    cross(third + low * width, count * width, low * width)
                else:
                    begin_piece(third + low * width, count * width, order)
                poll()
                low += count

        up(1)

        def first_tile(number, carry):
            cols = pl.ds(pl.multiple_of(number * 256, 256), 256)
            wide[:, cols] = (
                gsec[:, cols]
                + dot(slope[:, :units], upw[0, cols, :], NT)
                + dot(slope[:, units:], upw[1, cols, :], NT)
            )
            return carry

        polled_loop(0, width // 256, first_tile, 0)
        up(0)
        def norm_back(number, carry):
            rows = pl.ds(pl.multiple_of(number * block, block), block)
            grad = wide[rows, :]
            normed = normed1[rows, :]
            scaled = grad * row(gain1)
            back = inverse1[rows, 0:1] * (
                scaled
                - jnp.mean(scaled, axis=-1, keepdims=True)
                - normed * jnp.mean(scaled * normed, axis=-1, keepdims=True)
            )
            wide[rows, :] = back
            gmid16[rows, :] = back.astype(BF16)
            return (
                carry[0] + fold8(back),
                carry[1] + fold8(grad * normed),
                carry[2] + fold8(grad),
            )

        totals = lax.fori_loop(0, seq // block, norm_back, (zero, zero, zero))
        both = [jnp.sum(total, axis=0, keepdims=True) for total in totals]
        both += [jnp.sum(total, axis=0, keepdims=True) for total in later]
        vparts[0] = jnp.zeros(vparts.shape[1:], F32)
        vparts[1] = jnp.zeros(vparts.shape[1:], F32)
        for number, line in enumerate(both):
            vparts[0, number : number + 1, :] = line
            vparts[1, number : number + 1, :] = line
        for core in range(2):
            line = jnp.sum(ups[core], axis=0, keepdims=True)
            for side in range(units // width):
                vparts[1 - core, 6 + side : 7 + side, :] = line[:, side * width : (side + 1) * width]
        poll()
        kept.wait()

    def front(upw, downw):
        pl.run_scoped(
            functools.partial(attend_phase, upw, downw),
            pltpu.VMEM((2,) + qkvw_h.shape, BF16),
            pltpu.VMEM((2 * inner, seq), BF16),
            pltpu.VMEM((seq, seq), jnp.int32),
            pltpu.VMEM((seq, seq), jnp.int32),
            pltpu.VMEM((seq, LANES), F32),
            pltpu.VMEM((heads // 2, 8, 2 * LANES), jnp.int32),
            pltpu.VMEM((heads, seq, seq), BF16),
        )
        pl.run_scoped(
            functools.partial(unit_phase, upw, downw),
            pltpu.VMEM((seq, 2 * units), BF16),
            pltpu.VMEM((seq, 2 * units), BF16),
            pltpu.VMEM((seq, width), BF16),
            pltpu.VMEM((width, seq), BF16),
            pltpu.VMEM((seq, width), F32),
            pltpu.VMEM((seq, width), F32),
            pltpu.VMEM((seq, LANES), F32),
            pltpu.VMEM((seq, width), F32),
            pltpu.VMEM((seq, width), BF16),
            pltpu.VMEM((seq, width), BF16),
        )

    pl.run_scoped(
        front,
        pltpu.VMEM((2, width, units), BF16),
        pltpu.VMEM((2, units, width), BF16),
    )

    def pair_phase(spread, gq, gk, gv, kt, dheads_t, dheads, expo, expo_sem):
        def fetch(pair):
            slot = pair % 2 if isinstance(pair, int) else lax.rem(pair, 2)
            return pltpu.make_async_copy(
                expo_h.at[pl.ds(2 * pair, 2)], expo.at[slot], expo_sem.at[slot]
            )

        fetch(0).start()

        full = len(crossed)
        for copy in crossed[full - len(ORDERS["up"]) :]:
            copy().wait_send()
        at = 2 * third
        other = dot(heads_t[inner:, :], gmid16[...])
        for side in range(split):
            give(side * inner, other[:, side * inner : (side + 1) * inner])
        cross(at, split * inner, 0)
        poll()
        for core in range(2):
            tile = dot(outw[core], gmid16[...], NT)
            for head in range(per):
                rows = slice(core * inner + head * size, core * inner + (head + 1) * size)
                part = tile[head * size : (head + 1) * size] * recip[core * per + head, 0:1, :]
                dheads_t[rows, :] = part.astype(BF16)
        dheads[...] = jnp.transpose(dheads_t[...])
        kt[...] = jnp.transpose(k[...])
        own = dot(heads_t[:inner, :], gmid16[...])
        crossed[full]().wait_recv()
        for side in range(split):
            take(at + side * inner, own[:, side * inner : (side + 1) * inner])
        begin_piece(at, split * inner, ORDERS["out"])
        poll()
        first = lax.broadcasted_iota(jnp.int32, (seq, LANES), 1) < size

        def pair_back(pair, carry):
            cols = pl.ds(pl.multiple_of(pair * LANES, LANES), LANES)
            fetch(pair).wait()

            @pl.when(pair + 1 < heads // 2)
            def _():
                fetch(pair + 1).start()

            slot = lax.rem(pair, 2)
            values, queries = v[:, cols], q[:, cols]
            grads, grads_t = dheads[:, cols], dheads_t[cols, :]
            gvs, gks, gqs = [], [], []
            for side in range(2):
                head = 2 * pair + side
                mine = first if side == 0 else jnp.logical_not(first)
                rows = pl.ds(pl.multiple_of(pair * LANES + side * size, size), size)
                shift = jnp.sum(
                    dheads_t[rows, :].astype(F32) * heads_t[rows, :].astype(F32),
                    axis=0,
                    keepdims=True,
                )
                back = dot(jnp.where(mine, values, jnp.zeros_like(values)), grads_t)
                gscore = expo[slot, side].astype(F32) * (back - shift)
                for tile in range(seq // LANES):
                    spread[pl.ds(tile * seq * 16 + head, seq, stride=16), :] = gscore[
                        :, tile * LANES : (tile + 1) * LANES
                    ]
                gscore = gscore.astype(BF16)
                gvs.append(dot(expo[slot, side], grads))
                gks.append(dot(gscore, queries))
                gqs.append(dot(kt[rows, :], gscore) * 0.125)
            gv[:, cols] = jnp.where(first, gvs[0], gvs[1]).astype(BF16)
            gk[:, cols] = jnp.where(first, gks[0], gks[1]).astype(BF16)
            gq[:, cols] = jnp.transpose(jnp.concatenate(gqs, axis=0)).astype(BF16)
            return carry

        polled_loop(0, heads // 2, pair_back, 0)

    def mix_phase(spread, gq, gk, gv, qkvw, tokens_t):
        l_qkvw = [load(qkvw_h, qkvw.at[0]), load(qkvw_o, qkvw.at[1])]
        tokens_t[...] = jnp.transpose(tokens[...])
        full = len(crossed)
        at = 2 * third + split * inner
        kinds = (gq, gk, gv)
        def mix_back(core):
            for kind in range(3):
                if core == 0:
                    crossed[full + kind]().wait_recv()
                for top in range(0, width, 256):
                    tile = dot(
                        tokens_t[top : top + 256, :],
                        kinds[kind][:, core * inner : (core + 1) * inner],
                    )
                    if core == 1:
                        give(split * inner + kind * width + top, tile)
                    else:
                        take(at + kind * width + top, tile)
                if core == 1:
                    cross(at + kind * width, width, split * inner + kind * width)
                else:
                    begin_piece(at + kind * width, width, ORDERS["mix"][kind])
                poll()

        mix_back(1)
        span = length[me]
        columns = 256
        half_range = LANES // 2
        labels = lax.broadcasted_iota(jnp.int32, (half_range, columns), 0).astype(BF16)
        tab_sum = jnp.zeros((64, half_range), F32)
        for start in range(0, seq, columns):
            here = slice(start, start + columns)
            position = lax.broadcasted_iota(jnp.int32, (1, columns), 1) + start
            inside = (position < span).astype(F32)

            def count(number, carry, here=here, start=start, inside=inside):
                for line in range(64):
                    if line % 16 == 0:
                        place = pl.multiple_of(number * 64 + line, 16)
                        index = bucket[pl.ds(place, 16), here].astype(F32)
                        upper = (index >= half_range).astype(F32)
                        index = (index - upper * half_range).astype(BF16)
                        place = pl.multiple_of(place * 16, 256)
                        grads = jnp.concatenate(
                            [
                                spread[pl.ds(tile * seq * 16 + place, 256), :]
                                for tile in range(start // LANES, (start + columns) // LANES)
                            ],
                            axis=1,
                        )
                    turn = line % 16
                    hot = jnp.where(
                        labels == index[turn : turn + 1, :],
                        jnp.ones((), BF16),
                        jnp.zeros((), BF16),
                    )
                    other = jnp.where(number * 64 + line < span, 1.0 - inside, inside)
                    some = grads[16 * turn : 16 * turn + 16]
                    far = some * other
                    both = jnp.concatenate([some - far, far], axis=0)
                    high = both * upper[turn : turn + 1, :]
                    both = jnp.concatenate([both - high, high], axis=0).astype(BF16)
                    carry = carry + dot(both, hot, NT)
                return carry

            if start == 0:
                tab_sum = polled_loop(0, 2, count, tab_sum)
                mix_back(0)
            tab_sum = polled_loop(0 if start else 2, seq // 64, count, tab_sum)

        for core in range(2):
            mine = slice(core * inner, (core + 1) * inner)
            for number, kind in ((0, gq), (1, gv)):
                line = jnp.sum(fold8(kind[:, mine].astype(F32)), axis=0, keepdims=True)
                vparts[1 - core, 8:9, number * inner : (number + 1) * inner] = line
            for part in range(2):
                lines = []
                for upper in range(2):
                    low = upper * 32 + part * 16 + core * per
                    lines.append(tab_sum[low : low + per])
                cols = slice(part * LANES, (part + 1) * LANES)
                vparts[1 - core, 10 : 10 + per, cols] = jnp.concatenate(lines, axis=1)
        Vectors(vparts, vland, small, bits, kit, vs_sem, vr_sem).run(0)
        poll()

        l_qkvw[0].wait()
        l_qkvw[1].wait()

        def token_tile(number, carry):
            cols = pl.ds(pl.multiple_of(number * 256, 256), 256)
            total = wide[:, cols]
            for core in range(2):
                for kind in range(3):
                    total = total + dot(
                        kinds[kind][:, core * inner : (core + 1) * inner],
                        qkvw[core, kind, cols, :],
                        NT,
                    )
            wide[:, cols] = total
            return carry

        polled_loop(0, width // 256, token_tile, 0)

    per = heads // 2
    size = inner // per

    def back(spread, gq, gk, gv):
        pl.run_scoped(
            functools.partial(pair_phase, spread, gq, gk, gv),
            pltpu.VMEM((2 * inner, seq), BF16),
            pltpu.VMEM((2 * inner, seq), BF16),
            pltpu.VMEM((seq, 2 * inner), BF16),
            pltpu.VMEM((2, 2, seq, seq), BF16),
            pltpu.SemaphoreType.DMA((2,)),
        )
        pl.run_scoped(
            functools.partial(mix_phase, spread, gq, gk, gv),
            pltpu.VMEM((2,) + qkvw_h.shape, BF16),
            pltpu.VMEM((width, seq), BF16),
        )

    pl.run_scoped(
        back,
        pltpu.VMEM((seq // LANES * seq * 16, LANES), F32),
        pltpu.VMEM((seq, 2 * inner), BF16),
        pltpu.VMEM((seq, 2 * inner), BF16),
        pltpu.VMEM((seq, 2 * inner), BF16),
    )
    done = store(wide, gtok_h)
    for number in range(polls[0], 1 + max(number for number in plan if number != "tail")):
        run_steps(number)
    run_steps("tail")
    done.wait()
    for piece in kit.pieces:
        piece.finish()
    for copy in crossed[-4:]:
        copy().wait_send()
    for number in range(len(halves)):
        half(number).wait_send()


def layer(plan, bits, operands):
    tokens, qkvw, qvb, tab, outw, upw, upb, downw = operands[:8]
    seq, width = tokens.shape
    inner = qkvw.shape[2]
    units = upw.shape[1]
    heads = 2 * tab.shape[0]
    shape = jax.ShapeDtypeStruct
    here = pl.BlockSpec(memory_space=pltpu.VMEM)
    away = pl.BlockSpec(memory_space=pl.ANY)
    scalar = pl.BlockSpec(memory_space=pltpu.SMEM)
    rows = (3 * width * inner + inner * width + 2 * width * units) // inner
    lands = rows - (rows >> 4) + (bits - 4) * (rows >> 4)
    pieces = len(ORDERS["down"]) + len(ORDERS["up"]) + 4
    cuts = [one for _, one, _ in ORDERS["down"] + ORDERS["up"]]
    cuts += [ORDERS["out"][0]] + [one for one, _ in ORDERS["mix"]]
    leave = sum(3 if axis == "D" else 1 for one in cuts for axis in one)
    more = pieces * (bits - 4)
    return pl.pallas_call(
        functools.partial(layer_kernel, plan, bits),
        out_shape=(
            shape((rows, inner), BF16),
            shape((seq, width), F32),
            shape((seq, width), BF16),
            shape((16, width), F32),
            shape(qkvw.shape, BF16),
            shape(outw.shape, BF16),
            shape(upw.shape, BF16),
            shape(downw.shape, BF16),
            shape((heads, seq, seq), BF16),
        ),
        in_specs=[away] * 10 + [here] * 7 + [scalar],
        out_specs=(away, away, away, here) + (away,) * 5,
        scratch_shapes=[
            pltpu.VMEM((rows, inner), BF16),
            pltpu.VMEM((rows // 3, inner), BF16),
            pltpu.VMEM((rows, inner), BF16),
            pltpu.VMEM((lands, inner), BF16),
            pltpu.VMEM((seq, width), BF16),
            pltpu.VMEM((2,) + qvb.shape, F32),
            pltpu.VMEM((2,) + tab.shape, F32),
            pltpu.VMEM(upb.shape, F32),
            pltpu.VMEM(upb.shape, F32),
            pltpu.VMEM((2, 1, units), F32),
            pltpu.VMEM((2,) + outw.shape, BF16),
            pltpu.VMEM((seq, 2 * inner), BF16),
            pltpu.VMEM((seq, 2 * inner), BF16),
            pltpu.VMEM((seq, 2 * inner), BF16),
            pltpu.VMEM((2 * inner, seq), BF16),
            pltpu.VMEM((heads, 8, seq), F32),
            pltpu.VMEM((seq, seq), BF16),
            pltpu.VMEM((seq, width), F32),
            pltpu.VMEM((seq, width), BF16),
            pltpu.VMEM((seq, width), BF16),
            pltpu.VMEM((2, 8, units), F32),
            pltpu.VMEM((bits + 1, 16, width), F32),
            pltpu.VMEM((bits + 1, 16, width), F32),
            pltpu.SemaphoreType.DMA((24,)),
            pltpu.SemaphoreType.DMA((8,)),
            pltpu.SemaphoreType.DMA((leave + more,)),
            pltpu.SemaphoreType.DMA((2 * leave + more,)),
            pltpu.SemaphoreType.DMA((pieces,)),
            pltpu.SemaphoreType.DMA((pieces,)),
            pltpu.SemaphoreType.DMA((pieces,)),
            pltpu.SemaphoreType.DMA((bits + 1,)),
            pltpu.SemaphoreType.DMA((bits + 1,)),
            pltpu.SemaphoreType.DMA((7,)),
            pltpu.SemaphoreType.DMA((7,)),
        ],
        compiler_params=pltpu.CompilerParams(
            collective_id=0, has_side_effects=True, vmem_limit_bytes=VMEM_LIMIT
        ),
    )(*operands)


def finish_kernel(
    flat_h,
    out_h,
    gtok_h,
    small,
    out_f,
    gtok_f,
    mix_f,
    gqv,
    gtab,
    gout_f,
    goutb,
    gain1,
    shift1,
    up_f,
    gupb,
    down_f,
    gdownb,
    gain2,
    shift2,
    flat,
    mix,
    gout,
    up,
    down,
    gtok,
    out,
    in_sem,
    out_sem,
):
    rows, inner = flat.shape
    units, width = down.shape
    split = width // inner
    third = rows // 3
    copies = []
    tiles = units // 256
    span = 256 * split
    sizes = (
        [span] * tiles + [width] * (units // inner) + [split * inner] + [width] * 3
    )
    loads = []
    at = 0
    for number, size in enumerate(sizes):
        here = pl.ds(at, size)
        loads.append(pltpu.make_async_copy(flat_h.at[here, :], flat.at[here, :], in_sem.at[number]))
        loads[-1].start()
        at += size

    for source, target in ((gtok_h, gtok), (out_h, out)):
        loads.append(pltpu.make_async_copy(source, target, in_sem.at[len(loads)]))
        loads[-1].start()

    def store(source, target):
        copies.append(pltpu.make_async_copy(source, target, out_sem.at[len(copies)]))
        copies[-1].start()

    def wide(start, size):
        return flat[start : start + size, :].astype(F32)

    for tile in range(tiles):
        loads[tile].wait()
        here = slice(tile * 256, tile * 256 + 256)
        for side in range(split):
            down[here, side * inner : (side + 1) * inner] = wide(tile * span + side * 256, 256)
        here = pl.ds(tile * 256, 256)
        store(down.at[here, :], down_f.at[here, :])
    for part in range(units // inner):
        loads[tiles + part].wait()
        cols = pl.ds(part * inner, inner)
        up[:, cols] = wide(third + part * width, width)
        store(up.at[:, cols], up_f.at[:, cols])
    at = 2 * third
    loads[-6].wait()
    for side in range(split):
        gout[:, side * inner : (side + 1) * inner] = wide(at + side * inner, inner)
    store(gout, gout_f)
    at += split * inner
    for kind in range(3):
        loads[kind - 5].wait()
        mix[kind] = wide(at + kind * width, width)
        store(mix.at[kind], mix_f.at[kind])
    loads[-2].wait()
    store(gtok, gtok_f)
    loads[-1].wait()
    store(out, out_f)
    for number, vector in enumerate((goutb, gain1, shift1, gdownb, gain2, shift2)):
        vector[...] = small[number : number + 1, :].reshape(width)
    gupb[...] = jnp.concatenate(
        [small[6 + side : 7 + side, :] for side in range(units // width)], axis=1
    ).reshape(units)
    for kind in range(2):
        gqv[kind : kind + 1, :] = small[8:9, kind * inner : (kind + 1) * inner]
    gtab[...] = small[10 : 10 + gtab.shape[0], : gtab.shape[1]]
    for copy in copies:
        copy.wait()


def finish(flat, small, out, grad_tokens, width, units, heads):
    shape = jax.ShapeDtypeStruct
    here = pl.BlockSpec(memory_space=pltpu.VMEM)
    away = pl.BlockSpec(memory_space=pl.ANY)
    inner = flat.shape[1]
    vector = shape((width,), F32)
    got = pl.pallas_call(
        finish_kernel,
        out_shape=(
            shape(out.shape, BF16),
            shape(grad_tokens.shape, F32),
            shape((3, width, inner), F32),
            shape((2, inner), F32),
            shape((heads, 2 * LANES), F32),
            shape((inner, width), F32),
            vector,
            vector,
            vector,
            shape((width, units), F32),
            shape((units,), F32),
            shape((units, width), F32),
            vector,
            vector,
            vector,
        ),
        in_specs=[away] * 3 + [here],
        out_specs=(away, away, away, here, here, away, here, here, here, away, here, away)
        + (here,) * 3,
        scratch_shapes=[
            pltpu.VMEM(flat.shape, BF16),
            pltpu.VMEM((3, width, inner), F32),
            pltpu.VMEM((inner, width), F32),
            pltpu.VMEM((width, units), F32),
            pltpu.VMEM((units, width), F32),
            pltpu.VMEM(grad_tokens.shape, F32),
            pltpu.VMEM(out.shape, BF16),
            pltpu.SemaphoreType.DMA((units // 256 + units // inner + 6,)),
            pltpu.SemaphoreType.DMA((units // 256 + units // inner + 6,)),
        ],
        compiler_params=pltpu.CompilerParams(vmem_limit_bytes=VMEM_LIMIT),
    )(flat, out, grad_tokens, small)
    got = list(got)
    got[2] = jnp.transpose(got[2], (1, 0, 2))
    got[4] = got[4].T
    return tuple(got)


def order_of_steps(bits):
    pieces = len(ORDERS["down"]) + len(ORDERS["up"]) + 4
    plan = dict(PAUSES)
    known = {step for steps in PAUSES.values() for step in steps} | set(TAIL)
    more = tuple((pieces, step) for step in range(1, bits + 2) if (pieces, step) not in known)
    plan["tail"] = TAIL + more
    return plan


def on_device(
    dp,
    tokens,
    qkv_weight,
    qv_bias,
    rel_table,
    out_weight,
    out_bias,
    norm1_gain,
    norm1_bias,
    up_weight,
    up_bias,
    down_weight,
    down_bias,
    norm2_gain,
    norm2_bias,
    rel_bucket,
    query_len,
    key_mask,
    upstream,
):
    width = tokens.shape[1]
    units = up_weight.shape[1]
    bits = int(math.log2(dp))
    flat, grad_tokens, out, small = layer(
        order_of_steps(bits),
        bits,
        (
            tokens,
            jnp.transpose(qkv_weight, (1, 0, 2)),
            qv_bias,
            rel_table.T,
            out_weight,
            up_weight,
            up_bias,
            down_weight,
            upstream,
            rel_bucket,
            out_bias,
            norm1_gain,
            norm1_bias,
            down_bias,
            norm2_gain,
            norm2_bias,
            key_mask,
            query_len,
        ),
    )[:4]
    return finish(flat, small, out, grad_tokens, width, units, rel_table.shape[1])


def solution(mesh):
    rows = P(("dp", "tensor"), None)
    whole = P()
    in_specs = (
        rows,
        P(None, None, "tensor"),
        P(None, "tensor"),
        P(None, "tensor"),
        P("tensor", None),
        whole,
        whole,
        whole,
        P(None, "tensor"),
        P("tensor"),
        P("tensor", None),
        whole,
        whole,
        whole,
        whole,
        P("dp"),
        P("dp", None),
        rows,
    )
    out_specs = (
        rows,
        rows,
        P(None, None, "tensor"),
        P(None, "tensor"),
        P(None, "tensor"),
        P("tensor", None),
        whole,
        whole,
        whole,
        P(None, "tensor"),
        P("tensor"),
        P("tensor", None),
        whole,
        whole,
        whole,
    )
    return jax.shard_map(
        functools.partial(on_device, mesh.shape["dp"]),
        mesh=mesh,
        in_specs=in_specs,
        out_specs=out_specs,
        check_vma=False,
    )
```

```python
import functools
import math

import jax
import jax.numpy as jnp
from jax import lax
from jax.experimental import pallas as pl
from jax.experimental.pallas import tpu as pltpu
from jax.sharding import PartitionSpec as P

EPSILON = 1e-05
FAR_BELOW = -1000000000.0
MESH = pl.DeviceIdType.MESH
F32 = jnp.float32
BF16 = jnp.bfloat16
LANES = 128
NT = (((1,), (1,)), ((), ()))
TN = (((0,), (0,)), ((), ()))
VMEM_LIMIT = 62 * 2**20
ORDERS = {
    "down": ((2, "xyD", "yxD"), (3, "yxzZ", "zZxy"), (1, "xyzZ", "xzZy")),
    "up": ((2, "xyzZ", "xyzZ"), (1, "xyzZ", "zZxy"), (1, "yxzZ", "yzZx")),
    "out": ("xyzZ", "yxzZ"),
    "mix": (("xyD", "yxD"), ("yxD", "yxD"), ("yxD", "xyD")),
}
PAUSES = {
    12: ((0, 1),),
    15: ((2, 1),),
    16: ((1, 1),),
    18: ((0, 2),),
    19: ((5, 1),),
    20: ((2, 2),),
    22: ((3, 1), (0, 3), (4, 1), (2, 3)),
    24: ((1, 2),),
    25: ((6, 1), (0, 4), (3, 2), (2, 4)),
    26: ((5, 2),),
    27: ((1, 3),),
    28: ((4, 2),),
    29: ((6, 2),),
    31: ((3, 3),),
    32: ((2, 5), (0, 5)),
    33: ((5, 3),),
    35: ((1, 4), (4, 3)),
    36: ((6, 3),),
    37: ((7, 1), (3, 4), (2, 6)),
    39: ((5, 4),),
    42: ((6, 4), (8, 1)),
    43: ((9, 1), (3, 5)),
    44: ((5, 5),),
    45: ((7, 2), (6, 5)),
    46: ((8, 2), (2, 7)),
    47: ((1, 5), (0, 6), (3, 6), (4, 4)),
    48: ((5, 6), (10, 1), (9, 2)),
    50: ((7, 3), (6, 6), (2, 8)),
}
TAIL = ((8, 3), (3, 7), (10, 2), (4, 5), (1, 6), (5, 7), (10, 3), (6, 7), (9, 3), (7, 4), (8, 4), (5, 8), (4, 6), (3, 8), (7, 5), (10, 4), (1, 7), (9, 4), (6, 8), (4, 7), (8, 5), (10, 5), (7, 6), (9, 5), (1, 8), (8, 6), (4, 8), (9, 6))


def dot(left, right, dims=None):
    if dims is None:
        return jnp.dot(left, right, preferred_element_type=F32)
    return lax.dot_general(left, right, dims, preferred_element_type=F32)


def other_core():
    return {"tensor": 1 - lax.axis_index("tensor")}


def row(ref):
    return ref[...].reshape(1, ref.shape[-1])


def fold8(block):
    return jnp.sum(block.reshape(block.shape[0] // 8, 8, block.shape[1]), axis=0)


def pack_tables(tab, packed, core):
    step = jnp.maximum(jnp.max(jnp.abs(tab[core])), 1e-30) / 32000.0
    inverse = 1.0 / step
    heads = tab.shape[1]
    for pair in range(heads // 2):
        high = tab[core, 2 * pair : 2 * pair + 1, :] * inverse
        low = jnp.round(tab[core, 2 * pair + 1 : 2 * pair + 2, :] * inverse)
        high = jnp.round(high - low * (1 / 65536.0))
        both = high.astype(jnp.int32) * 65536 + low.astype(jnp.int32)
        packed[core * (heads // 2) + pair] = jnp.broadcast_to(both, packed.shape[1:])
    return step


def attend_pair(pair, q, k, vt, packed, bucket, valid, length, step, expo, heads_t, recip):
    seq = q.shape[0]
    cols = pl.ds(pl.multiple_of(pair * LANES, LANES), LANES)
    keys = k[:, cols]
    queries = q[:, cols]
    lane = lax.broadcasted_iota(jnp.int32, (seq, LANES), 1)
    in_query = lax.broadcasted_iota(jnp.int32, (seq, LANES), 0) < length
    terms = packed[pair, 0:1, :]
    near = jnp.broadcast_to(terms[:, :LANES], (seq, LANES))
    far = jnp.broadcast_to(terms[:, LANES:], (seq, LANES))
    same = jnp.where(in_query, far, near)
    swap = jnp.where(in_query, near, far)
    pieces = ([], [])
    for start in range(0, seq, LANES):
        index = bucket[:, start : start + LANES]
        got = jnp.take_along_axis(same, index, axis=1, mode="promise_in_bounds")
        if start == 0:
            turned = jnp.take_along_axis(swap, index, axis=1, mode="promise_in_bounds")
            got = jnp.where(lane < length, turned, got)
        pieces[0].append(got.astype(F32) * (step * (1 / 65536.0)))
        pieces[1].append(jnp.left_shift(got, 16).astype(F32) * (step * (1 / 65536.0)))
    first = lane < LANES // 2
    real = jnp.concatenate([valid[...] > 0] * (seq // LANES), axis=1)
    for side in range(2):
        mine = first if side == 0 else jnp.logical_not(first)
        scores = dot(jnp.where(mine, keys, jnp.zeros_like(keys)), queries, NT)
        scores = scores + jnp.concatenate(pieces[side], axis=1)
        scores = jnp.where(real, scores, FAR_BELOW)
        highest = jnp.max(scores, axis=0, keepdims=True)
        weights = jnp.exp(scores - highest).astype(BF16)
        expo[2 * pair + side] = weights
        rows = pl.ds(pl.multiple_of(pair * LANES + side * 64, 64), 64)
        values = jnp.concatenate([vt[rows, :], jnp.ones((16, seq), BF16)], axis=0)
        got = dot(values, weights)
        inverse = 1.0 / got[64:65]
        heads_t[rows, :] = (got[:64] * inverse).astype(BF16)
        recip[2 * pair + side] = jnp.broadcast_to(inverse, recip.shape[1:])


def dp_stride(bits):
    first, second = 1 << bits[0], 1 << bits[1]
    if first == second:
        return first
    return first + lax.axis_index("tensor") * (second - first)


def dp_side(bits):
    return lax.rem(lax.div(lax.axis_index("dp"), dp_stride(bits)), 2)


def dp_partner(bits):
    return {"dp": lax.axis_index("dp") + (1 - 2 * dp_side(bits)) * dp_stride(bits)}


def dp_quarter(ahead):
    return lax.rem(lax.div(lax.axis_index("dp"), 4) + ahead, 4)


def dp_ahead(ahead):
    return {"dp": lax.axis_index("dp") + 4 * (dp_quarter(ahead) - dp_quarter(0))}


def flat_rows(start, size):
    return pl.ds(pl.multiple_of(start, 16), size)


class Kit:
    def __init__(self, acc, landing, result, send_sem, recv_sem, local_sem):
        self.acc, self.landing, self.result = acc, landing, result
        self.send_sem, self.recv_sem, self.local_sem = send_sem, recv_sem, local_sem
        self.used = [0, 0]
        self.landed = 0
        self.pieces = []

    def slot(self, kind):
        self.used[kind] += 1
        return self.used[kind] - 1

    def room(self, size):
        self.landed += size
        return self.landed - size

    def remote(self, slot, source, target, device):
        return pltpu.make_async_remote_copy(
            src_ref=source,
            dst_ref=target,
            send_sem=self.send_sem.at[slot[0]],
            recv_sem=self.recv_sem.at[slot[1]],
            device_id=device,
            device_id_type=MESH,
        )


class Piece:
    def __init__(self, start, length, stages, extra, kit):
        self.start = start
        self.stages, self.extra = stages, extra
        self.kit = kit
        self.number = len(kit.pieces)
        self.steps = 2 * len(stages) + 1
        kit.pieces.append(self)
        self.sizes = [length]
        self.cutting, self.spreading = [], []
        for stage in stages:
            parts = 4 if stage is None else 2
            size = self.sizes[-1] // parts
            self.sizes.append(size)
            leaving = [kit.slot(0) for _ in range(parts - 1)]
            self.cutting.append([((slot, kit.slot(1)), kit.room(size)) for slot in leaving])
            self.spreading.append([(slot, kit.slot(1)) for slot in leaving])
        self.crossing = [((kit.slot(0), kit.slot(1)), kit.room(self.sizes[-1])) for _ in extra]

    def begin(self, levels):
        at = self.start
        for level in range(levels):
            stage = self.stages[level]
            at = at + (dp_quarter(0) if stage is None else dp_side(stage)) * self.sizes[level + 1]
        return at

    def partners(self, stage):
        if stage is None:
            return [(dp_quarter(ahead), dp_ahead(ahead)) for ahead in (1, 2, 3)]
        return [(1 - dp_side(stage), dp_partner(stage))]

    def cut(self, level):
        kit, size = self.kit, self.sizes[level + 1]
        at = self.begin(level)
        return [
            kit.remote(
                slot,
                kit.acc.at[flat_rows(at + part * size, size), :],
                kit.landing.at[pl.ds(room, size), :],
                device,
            )
            for (slot, room), (part, device) in zip(
                self.cutting[level], self.partners(self.stages[level])
            )
        ]

    def swap(self, number):
        kit = self.kit
        slot, room = self.crossing[number]
        size = self.sizes[-1]
        return kit.remote(
            slot,
            kit.acc.at[flat_rows(self.begin(len(self.stages)), size), :],
            kit.landing.at[pl.ds(room, size), :],
            dp_partner(self.extra[number]),
        )

    def keep(self):
        kit = self.kit
        mine = flat_rows(self.begin(len(self.stages)), self.sizes[-1])
        return pltpu.make_async_copy(
            kit.acc.at[mine, :], kit.result.at[mine, :], kit.local_sem.at[self.number]
        )

    def spread(self, level):
        kit = self.kit
        mine = flat_rows(self.begin(level + 1), self.sizes[level + 1])
        source = kit.acc if level == len(self.stages) - 1 else kit.result
        return [
            kit.remote(slot, source.at[mine, :], kit.result.at[mine, :], device)
            for slot, (_, device) in zip(
                self.spreading[level], self.partners(self.stages[level])
            )
        ]

    def add(self, target, rooms, size):
        kit = self.kit
        chunk = math.gcd(size, 192)

        def some(number, carry):
            there = flat_rows(target + number * chunk, chunk)
            total = kit.acc[there, :].astype(F32)
            for room in rooms:
                total = total + kit.landing[flat_rows(room + number * chunk, chunk), :].astype(F32)
            kit.acc[there, :] = total.astype(BF16)
            return carry

        lax.fori_loop(0, size // chunk, some, 0)

    def run(self, step):
        levels = len(self.stages)
        if 0 < step <= levels:
            for copy in self.cut(step - 1):
                copy.wait_recv()
            rooms = [room for _, room in self.cutting[step - 1]]
            self.add(self.begin(step), rooms, self.sizes[step])
        if step < levels:
            for copy in self.cut(step):
                copy.start()
            return
        if step == levels:
            for number in range(len(self.extra)):
                both = self.swap(number)
                both.start()
                both.wait()
                self.add(self.begin(levels), [self.crossing[number][1]], self.sizes[-1])
            self.keep().start()
        else:
            for copy in self.spread(2 * levels - step):
                copy.wait_recv()
            if step == levels + 1:
                self.keep().wait()
        if step < 2 * levels:
            for copy in self.cut(2 * levels - 1 - step):
                copy.wait_send()
            for copy in self.spread(2 * levels - 1 - step):
                copy.start()

    def finish(self):
        for level in range(len(self.stages)):
            for copy in self.spread(level):
                copy.wait_send()


class Vectors:
    def __init__(self, parts, landing, result, bits, kit, send_sem, recv_sem):
        self.parts, self.landing, self.result = parts, landing, result
        self.bits = bits
        self.steps = bits + 2
        self.send_sem, self.recv_sem = send_sem, recv_sem
        kit.pieces.append(self)

    def exchange(self, step):
        return pltpu.make_async_remote_copy(
            src_ref=self.parts.at[step],
            dst_ref=self.landing.at[step],
            send_sem=self.send_sem.at[step],
            recv_sem=self.recv_sem.at[step],
            device_id=other_core() if step == 0 else dp_partner((step - 1, step - 1)),
            device_id_type=MESH,
        )

    def run(self, step):
        if step > 0:
            self.exchange(step - 1).wait_recv()
            total = self.parts[max(step - 1, 1)] + self.landing[step - 1]
            if step <= self.bits:
                self.parts[step] = total
            else:
                self.result[...] = total
        if step <= self.bits:
            self.exchange(step).start()

    def finish(self):
        for step in range(self.bits + 1):
            self.exchange(step).wait_send()


def layer_kernel(
    plan,
    bits,
    tokens_h,
    qkvw_h,
    qvb_h,
    tab_h,
    outw_h,
    upw_h,
    upb_h,
    downw_h,
    upstream_h,
    bucket_h,
    outb,
    gain1,
    shift1,
    downb,
    gain2,
    shift2,
    mask,
    length,
    result_h,
    gtok_h,
    out_h,
    small,
    qkvw_o,
    outw_o,
    upw_o,
    downw_o,
    expo_h,
    acc,
    xsend,
    xrecv,
    landing,
    tokens,
    qvb,
    tab,
    upb,
    upb_other,
    upb_rows,
    outw,
    q,
    k,
    v,
    heads_t,
    recip,
    bucket,
    wide,
    gmid16,
    upstream,
    ups,
    vparts,
    vland,
    in_sem,
    out_sem,
    send_sem,
    recv_sem,
    local_sem,
    xs_sem,
    xr_sem,
    vs_sem,
    vr_sem,
    ws_sem,
    wr_sem,
):
    seq, width = tokens.shape
    inner = outw.shape[1]
    units = upw_h.shape[1]
    heads = recip.shape[0]
    pairs = inner // LANES
    split = width // inner
    third = acc.shape[0] // 3

    barrier = pltpu.get_barrier_semaphore()
    pl.semaphore_signal(barrier, inc=1, device_id=other_core(), device_id_type=MESH)
    for bit in range(bits):
        pl.semaphore_signal(barrier, inc=1, device_id=dp_partner((bit, bit)), device_id_type=MESH)
    pl.semaphore_signal(
        barrier,
        inc=1,
        device_id={"dp": lax.axis_index("dp") + 12 - 8 * dp_quarter(0)},
        device_id_type=MESH,
    )

    used, stored = [], []

    def load(source, target):
        copy = pltpu.make_async_copy(source, target, in_sem.at[len(used)])
        used.append(copy)
        copy.start()
        return copy

    loaded = []

    def early(source, target):
        number = len(used)
        used.append(None)
        loaded.append(lambda: pltpu.make_async_copy(source, target(), in_sem.at[number]))
        loaded[-1]().start()

    def store(source, target):
        copy = pltpu.make_async_copy(source, target, out_sem.at[len(stored)])
        stored.append(copy)
        copy.start()
        return copy

    halves = [
        (qkvw_h, qkvw_o),
        (qvb_h, qvb.at[1]),
        (tab_h, tab.at[1]),
        (outw_h, outw_o),
        (upw_h, upw_o),
        (upb_h, upb_other),
        (downw_h, downw_o),
    ]

    def half(number):
        source, target = halves[number]
        return pltpu.make_async_remote_copy(
            src_ref=source,
            dst_ref=target,
            send_sem=ws_sem.at[number],
            recv_sem=wr_sem.at[number],
            device_id=other_core(),
            device_id_type=MESH,
        )

    kit = Kit(acc, landing, result_h, send_sem, recv_sem, local_sem)
    extra = tuple((bit, bit) for bit in range(4, bits))
    crossed = []

    def cross(start, size, place):
        number = len(crossed)

        def copy():
            return pltpu.make_async_remote_copy(
                src_ref=xsend.at[pl.ds(place, size), :],
                dst_ref=xrecv.at[pl.ds(start, size), :],
                send_sem=xs_sem.at[number],
                recv_sem=xr_sem.at[number],
                device_id=other_core(),
                device_id_type=MESH,
            )

        copy().start()
        crossed.append(copy)

    polls = [0]

    def run_steps(number):
        for piece, step in plan.get(number, ()):
            kit.pieces[piece].run(step)

    def poll():
        run_steps(polls[0])
        polls[0] += 1

    def polled_loop(low, high, body, initial, every=1):
        start = polls[0]
        pauses = (high - low) // every
        polls[0] += pauses
        busy = [number for number in range(pauses) if plan.get(start + number)]

        def turn(index, carry):
            carry = body(index, carry)
            for number in busy:

                @pl.when(index == low + (number + 1) * every - 1)
                def _():
                    run_steps(start + number)

            return carry

        return lax.fori_loop(low, high, turn, initial)

    def begin_piece(start, size, orders):
        order = tuple(
            None if one == "D" else ("xyzZ".index(one), "xyzZ".index(two))
            for one, two in zip(*orders)
        )
        fresh = Piece(start, size, order, extra, kit)
        if not any((fresh.number, 0) in steps for steps in plan.values()):
            fresh.run(0)

    def give(place, tile):
        xsend[flat_rows(place, tile.shape[0]), :] = tile.astype(BF16)

    def take(start, tile):
        there = flat_rows(start, tile.shape[0])
        acc[there, :] = (tile + xrecv[there, :].astype(F32)).astype(BF16)

    me = lax.axis_index("tensor")

    def attend_phase(upw, downw, qkvw, vt, bucket_i, bucket_t, valid, packed, expo):
        l_tokens = load(tokens_h, tokens)
        l_qkvw = load(qkvw_h, qkvw.at[0])
        l_qvb = load(qvb_h, qvb.at[0])
        l_bucket = load(bucket_h, bucket_i)
        l_tab = load(tab_h, tab.at[0])
        l_late = [load(outw_h, outw.at[0]), load(upb_h, upb)]
        early(upw_h, lambda: upw.at[0])
        early(downw_h, lambda: downw.at[0])
        early(upstream_h, lambda: upstream)
        span = length[me]
        mine = mask[pl.ds(me, 1), :].astype(F32)
        valid[...] = jnp.transpose(jnp.broadcast_to(mine, (LANES, seq)))

        def mix(core):
            rows = tokens[...]
            cols = slice(core * inner, (core + 1) * inner)
            query = dot(rows, qkvw[core, 0])
            q[:, cols] = ((query + qvb[core, 0:1, :]) * 0.125).astype(BF16)
            k[:, cols] = dot(rows, qkvw[core, 1]).astype(BF16)
            value = (dot(rows, qkvw[core, 2]) + qvb[core, 1:2, :]).astype(BF16)
            v[:, cols] = value
            vt[cols, :] = jnp.transpose(value)

        l_tokens.wait()
        l_qkvw.wait()
        l_qvb.wait()
        mix(0)
        pl.semaphore_wait(barrier, 2 + bits)
        for number in range(3):
            half(number).start()
        l_bucket.wait()
        bucket_t[...] = jnp.transpose(bucket_i[...])
        bucket[...] = bucket_t[...].astype(BF16)
        l_tab.wait()

        def attend(step, pair, carry):
            attend_pair(pair, q, k, vt, packed, bucket_t, valid, span, step, expo, heads_t, recip)
            return carry

        attend_own = functools.partial(attend, pack_tables(tab, packed, 0))

        kept = []

        def keep(low, high):
            here = pl.ds(2 * low, 2 * (high - low))
            kept.append(store(expo.at[here], expo_h.at[here]))

        lax.fori_loop(0, 2, attend_own, 0, unroll=2)
        half(0).wait_recv()
        half(1).wait_recv()
        half(2).wait_recv()
        l_other = load(qkvw_o, qkvw.at[1])
        for number in range(3, 6):
            half(number).start()
        lax.fori_loop(2, pairs, attend_own, 0, unroll=2)
        keep(0, pairs)
        l_other.wait()
        mix(1)
        attend_other = functools.partial(attend, pack_tables(tab, packed, 1))
        lax.fori_loop(pairs, pairs + 1, attend_other, 0)
        keep(pairs, pairs + 1)
        half(6).start()
        half(3).wait_recv()
        l_late.append(load(outw_o, outw.at[1]))
        lax.fori_loop(pairs + 1, 2 * pairs, attend_other, 0, unroll=2)
        keep(pairs + 1, 2 * pairs)
        half(4).wait_recv()
        early(upw_o, lambda: upw.at[1])
        for copy in l_late:
            copy.wait()
        lower = jnp.transpose(heads_t[...])

        def project(tile, carry):
            cols = pl.ds(pl.multiple_of(tile * 256, 256), 256)
            wide[:, cols] = dot(lower[:, :inner], outw[0, :, cols]) + dot(
                lower[:, inner:], outw[1, :, cols]
            )
            return carry

        lax.fori_loop(0, width // 256, project, 0, unroll=3)
        for copy in kept:
            copy.wait()

    def unit_phase(
        upw, downw, act, slope, first, first_t, first32, normed1, inverse1, gsec, gbr, out
    ):
        half(5).wait_recv()
        upb_rows[0] = row(upb)
        upb_rows[1] = row(upb_other)
        block = 128

        def norm_one(number, carry):
            rows = pl.ds(pl.multiple_of(number * block, block), block)
            value = wide[rows, :] + row(outb) + tokens[rows, :].astype(F32)
            center = value - jnp.mean(value, axis=-1, keepdims=True)
            inverse = lax.rsqrt(jnp.mean(center * center, axis=-1, keepdims=True) + EPSILON)
            normed = center * inverse
            result = normed * row(gain1) + row(shift1)
            normed1[rows, :] = normed
            inverse1[rows, :] = jnp.broadcast_to(inverse, (block, LANES))
            first32[rows, :] = result
            first[rows, :] = result.astype(BF16)
            return carry

        lax.fori_loop(0, seq // block, norm_one, 0)

        for core in range(2):
            loaded[3 * core]().wait()

            def expand(tile, carry, core=core):
                cols = pl.ds(pl.multiple_of(tile * 256, 256), 256)
                here = pl.ds(pl.multiple_of(core * units + tile * 256, 256), 256)
                hidden = dot(first[...], upw[core, :, cols]) + upb_rows[core, :, cols]
                chance = 0.5 * (1.0 + lax.erf(hidden * math.sqrt(0.5)))
                density = jnp.exp(hidden * hidden * -0.5) * (1.0 / math.sqrt(2.0 * math.pi))
                act[:, here] = (hidden * chance).astype(BF16)
                slope[:, here] = (chance + hidden * density).astype(BF16)
                return carry

            lax.fori_loop(0, units // 256, expand, 0, unroll=2)
        half(6).wait_recv()
        l_down = load(downw_o, downw.at[1])
        first_t[...] = jnp.transpose(first[...])
        loaded[1]().wait()
        l_down.wait()

        def reduce_units(tile, carry):
            cols = pl.ds(pl.multiple_of(tile * 256, 256), 256)
            wide[:, cols] = dot(act[:, :units], downw[0, :, cols]) + dot(
                act[:, units:], downw[1, :, cols]
            )
            return carry

        lax.fori_loop(0, width // 256, reduce_units, 0, unroll=3)
        loaded[2]().wait()

        def norm_two(number, carry):
            rows = pl.ds(pl.multiple_of(number * block, block), block)
            value = wide[rows, :] + row(downb) + first32[rows, :]
            center = value - jnp.mean(value, axis=-1, keepdims=True)
            inverse = lax.rsqrt(jnp.mean(center * center, axis=-1, keepdims=True) + EPSILON)
            normed = center * inverse
            out[rows, :] = (normed * row(gain2) + row(shift2)).astype(BF16)
            grad = upstream[rows, :].astype(F32)
            scaled = grad * row(gain2)
            back = inverse * (
                scaled
                - jnp.mean(scaled, axis=-1, keepdims=True)
                - normed * jnp.mean(scaled * normed, axis=-1, keepdims=True)
            )
            gsec[rows, :] = back
            gbr[rows, :] = back.astype(BF16)
            return (
                carry[0] + fold8(back),
                carry[1] + fold8(grad * normed),
                carry[2] + fold8(grad),
            )

        zero = jnp.zeros((8, width), F32)
        later = lax.fori_loop(0, seq // block, norm_two, (zero, zero, zero))
        kept = store(out, out_h)

        tiles = units // 256
        span = 256 * split

        def down(core):
            low = 0
            for part, (count, *order) in enumerate(ORDERS["down"]):
                if core == 0:
                    crossed[part]().wait_recv()

                def down_tile(number, carry, core=core):
                    cols = pl.ds(pl.multiple_of(core * units + number * 256, 256), 256)
                    tile = dot(act[:, cols], gbr[...], TN)
                    for side in range(split):
                        (give if core == 1 else take)(
                            number * span + side * 256,
                            tile[:, side * inner : (side + 1) * inner],
                        )
                    return carry

                lax.fori_loop(low, low + count, down_tile, 0)
                if core == 1:
                    cross(low * span, count * span, low * span)
                else:
                    begin_piece(low * span, count * span, order)
                    poll()
                low += count

        def bend(core):
            def slope_tile(number, carry):
                here = pl.ds(pl.multiple_of(number * 256, 256), 256)
                cols = pl.ds(pl.multiple_of(core * units + number * 256, 256), 256)
                tile = dot(gbr[...], downw[core, here, :], NT) * slope[:, cols].astype(F32)
                tile = tile.astype(BF16)
                slope[:, cols] = tile
                ups[core, :, here] = fold8(tile.astype(F32))
                return carry

            polled_loop(0, tiles, slope_tile, 0, tiles // 2)

        down(1)
        fed = len(crossed)
        bend(1)
        down(0)
        bend(0)

        for copy in crossed[:fed]:
            copy().wait_send()
        def up(core):
            low = 0
            for part, (count, *order) in enumerate(ORDERS["up"]):
                if core == 0:
                    crossed[fed + part]().wait_recv()

                def up_tile(number, carry, core=core):
                    cols = pl.ds(pl.multiple_of(core * units + number * inner, LANES), inner)
                    for top in range(0, width, 256):
                        tile = dot(first_t[top : top + 256, :], slope[:, cols])
                        if core == 1:
                            give(number * width + top, tile)
                        else:
                            take(third + number * width + top, tile)
                    return carry

                lax.fori_loop(low, low + count, up_tile, 0)
                if core == 1:
                    cross(third + low * width, count * width, low * width)
                else:
                    begin_piece(third + low * width, count * width, order)
                poll()
                low += count

        up(1)

        def first_tile(number, carry):
            cols = pl.ds(pl.multiple_of(number * 256, 256), 256)
            wide[:, cols] = (
                gsec[:, cols]
                + dot(slope[:, :units], upw[0, cols, :], NT)
                + dot(slope[:, units:], upw[1, cols, :], NT)
            )
            return carry

        polled_loop(0, width // 256, first_tile, 0)
        up(0)
        def norm_back(number, carry):
            rows = pl.ds(pl.multiple_of(number * block, block), block)
            grad = wide[rows, :]
            normed = normed1[rows, :]
            scaled = grad * row(gain1)
            back = inverse1[rows, 0:1] * (
                scaled
                - jnp.mean(scaled, axis=-1, keepdims=True)
                - normed * jnp.mean(scaled * normed, axis=-1, keepdims=True)
            )
            wide[rows, :] = back
            gmid16[rows, :] = back.astype(BF16)
            return (
                carry[0] + fold8(back),
                carry[1] + fold8(grad * normed),
                carry[2] + fold8(grad),
            )

        totals = lax.fori_loop(0, seq // block, norm_back, (zero, zero, zero))
        both = [jnp.sum(total, axis=0, keepdims=True) for total in totals]
        both += [jnp.sum(total, axis=0, keepdims=True) for total in later]
        vparts[0] = jnp.zeros(vparts.shape[1:], F32)
        vparts[1] = jnp.zeros(vparts.shape[1:], F32)
        for number, line in enumerate(both):
            vparts[0, number : number + 1, :] = line
            vparts[1, number : number + 1, :] = line
        for core in range(2):
            line = jnp.sum(ups[core], axis=0, keepdims=True)
            for side in range(units // width):
                vparts[1 - core, 6 + side : 7 + side, :] = line[:, side * width : (side + 1) * width]
        poll()
        kept.wait()

    def front(upw, downw):
        pl.run_scoped(
            functools.partial(attend_phase, upw, downw),
            pltpu.VMEM((2,) + qkvw_h.shape, BF16),
            pltpu.VMEM((2 * inner, seq), BF16),
            pltpu.VMEM((seq, seq), jnp.int32),
            pltpu.VMEM((seq, seq), jnp.int32),
            pltpu.VMEM((seq, LANES), F32),
            pltpu.VMEM((heads // 2, 8, 2 * LANES), jnp.int32),
            pltpu.VMEM((heads, seq, seq), BF16),
        )
        pl.run_scoped(
            functools.partial(unit_phase, upw, downw),
            pltpu.VMEM((seq, 2 * units), BF16),
            pltpu.VMEM((seq, 2 * units), BF16),
            pltpu.VMEM((seq, width), BF16),
            pltpu.VMEM((width, seq), BF16),
            pltpu.VMEM((seq, width), F32),
            pltpu.VMEM((seq, width), F32),
            pltpu.VMEM((seq, LANES), F32),
            pltpu.VMEM((seq, width), F32),
            pltpu.VMEM((seq, width), BF16),
            pltpu.VMEM((seq, width), BF16),
        )

    pl.run_scoped(
        front,
        pltpu.VMEM((2, width, units), BF16),
        pltpu.VMEM((2, units, width), BF16),
    )

    def pair_phase(spread, gq, gk, gv, kt, dheads_t, dheads, expo, expo_sem):
        def fetch(pair):
            slot = pair % 2 if isinstance(pair, int) else lax.rem(pair, 2)
            return pltpu.make_async_copy(
                expo_h.at[pl.ds(2 * pair, 2)], expo.at[slot], expo_sem.at[slot]
            )

        fetch(0).start()

        full = len(crossed)
        for copy in crossed[full - len(ORDERS["up"]) :]:
            copy().wait_send()
        at = 2 * third
        other = dot(heads_t[inner:, :], gmid16[...])
        for side in range(split):
            give(side * inner, other[:, side * inner : (side + 1) * inner])
        cross(at, split * inner, 0)
        poll()
        for core in range(2):
            tile = dot(outw[core], gmid16[...], NT)
            for head in range(per):
                rows = slice(core * inner + head * size, core * inner + (head + 1) * size)
                part = tile[head * size : (head + 1) * size] * recip[core * per + head, 0:1, :]
                dheads_t[rows, :] = part.astype(BF16)
        dheads[...] = jnp.transpose(dheads_t[...])
        kt[...] = jnp.transpose(k[...])
        own = dot(heads_t[:inner, :], gmid16[...])
        crossed[full]().wait_recv()
        for side in range(split):
            take(at + side * inner, own[:, side * inner : (side + 1) * inner])
        begin_piece(at, split * inner, ORDERS["out"])
        poll()
        first = lax.broadcasted_iota(jnp.int32, (seq, LANES), 1) < size

        def pair_back(pair, carry):
            cols = pl.ds(pl.multiple_of(pair * LANES, LANES), LANES)
            fetch(pair).wait()

            @pl.when(pair + 1 < heads // 2)
            def _():
                fetch(pair + 1).start()

            slot = lax.rem(pair, 2)
            values, queries = v[:, cols], q[:, cols]
            grads, grads_t = dheads[:, cols], dheads_t[cols, :]
            gvs, gks, gqs = [], [], []
            for side in range(2):
                head = 2 * pair + side
                mine = first if side == 0 else jnp.logical_not(first)
                rows = pl.ds(pl.multiple_of(pair * LANES + side * size, size), size)
                shift = jnp.sum(
                    dheads_t[rows, :].astype(F32) * heads_t[rows, :].astype(F32),
                    axis=0,
                    keepdims=True,
                )
                back = dot(jnp.where(mine, values, jnp.zeros_like(values)), grads_t)
                gscore = expo[slot, side].astype(F32) * (back - shift)
                for tile in range(seq // LANES):
                    spread[pl.ds(tile * seq * 16 + head, seq, stride=16), :] = gscore[
                        :, tile * LANES : (tile + 1) * LANES
                    ]
                gscore = gscore.astype(BF16)
                gvs.append(dot(expo[slot, side], grads))
                gks.append(dot(gscore, queries))
                gqs.append(dot(kt[rows, :], gscore) * 0.125)
            gv[:, cols] = jnp.where(first, gvs[0], gvs[1]).astype(BF16)
            gk[:, cols] = jnp.where(first, gks[0], gks[1]).astype(BF16)
            gq[:, cols] = jnp.transpose(jnp.concatenate(gqs, axis=0)).astype(BF16)
            return carry

        polled_loop(0, heads // 2, pair_back, 0)

    def mix_phase(spread, gq, gk, gv, qkvw, tokens_t):
        l_qkvw = [load(qkvw_h, qkvw.at[0]), load(qkvw_o, qkvw.at[1])]
        tokens_t[...] = jnp.transpose(tokens[...])
        full = len(crossed)
        at = 2 * third + split * inner
        kinds = (gq, gk, gv)
        def mix_back(core):
            for kind in range(3):
                if core == 0:
                    crossed[full + kind]().wait_recv()
                for top in range(0, width, 256):
                    tile = dot(
                        tokens_t[top : top + 256, :],
                        kinds[kind][:, core * inner : (core + 1) * inner],
                    )
                    if core == 1:
                        give(split * inner + kind * width + top, tile)
                    else:
                        take(at + kind * width + top, tile)
                if core == 1:
                    cross(at + kind * width, width, split * inner + kind * width)
                else:
                    begin_piece(at + kind * width, width, ORDERS["mix"][kind])
                poll()

        mix_back(1)
        span = length[me]
        columns = 256
        half_range = LANES // 2
        labels = lax.broadcasted_iota(jnp.int32, (half_range, columns), 0).astype(BF16)
        tab_sum = jnp.zeros((64, half_range), F32)
        for start in range(0, seq, columns):
            here = slice(start, start + columns)
            position = lax.broadcasted_iota(jnp.int32, (1, columns), 1) + start
            inside = (position < span).astype(F32)

            def count(number, carry, here=here, start=start, inside=inside):
                for line in range(64):
                    if line % 16 == 0:
                        place = pl.multiple_of(number * 64 + line, 16)
                        index = bucket[pl.ds(place, 16), here].astype(F32)
                        upper = (index >= half_range).astype(F32)
                        index = (index - upper * half_range).astype(BF16)
                        place = pl.multiple_of(place * 16, 256)
                        grads = jnp.concatenate(
                            [
                                spread[pl.ds(tile * seq * 16 + place, 256), :]
                                for tile in range(start // LANES, (start + columns) // LANES)
                            ],
                            axis=1,
                        )
                    turn = line % 16
                    hot = jnp.where(
                        labels == index[turn : turn + 1, :],
                        jnp.ones((), BF16),
                        jnp.zeros((), BF16),
                    )
                    other = jnp.where(number * 64 + line < span, 1.0 - inside, inside)
                    some = grads[16 * turn : 16 * turn + 16]
                    far = some * other
                    both = jnp.concatenate([some - far, far], axis=0)
                    high = both * upper[turn : turn + 1, :]
                    both = jnp.concatenate([both - high, high], axis=0).astype(BF16)
                    carry = carry + dot(both, hot, NT)
                return carry

            if start == 0:
                tab_sum = polled_loop(0, 2, count, tab_sum)
                mix_back(0)
            tab_sum = polled_loop(0 if start else 2, seq // 64, count, tab_sum)

        for core in range(2):
            mine = slice(core * inner, (core + 1) * inner)
            for number, kind in ((0, gq), (1, gv)):
                line = jnp.sum(fold8(kind[:, mine].astype(F32)), axis=0, keepdims=True)
                vparts[1 - core, 8:9, number * inner : (number + 1) * inner] = line
            for part in range(2):
                lines = []
                for upper in range(2):
                    low = upper * 32 + part * 16 + core * per
                    lines.append(tab_sum[low : low + per])
                cols = slice(part * LANES, (part + 1) * LANES)
                vparts[1 - core, 10 : 10 + per, cols] = jnp.concatenate(lines, axis=1)
        Vectors(vparts, vland, small, bits, kit, vs_sem, vr_sem).run(0)
        poll()

        l_qkvw[0].wait()
        l_qkvw[1].wait()

        def token_tile(number, carry):
            cols = pl.ds(pl.multiple_of(number * 256, 256), 256)
            total = wide[:, cols]
            for core in range(2):
                for kind in range(3):
                    total = total + dot(
                        kinds[kind][:, core * inner : (core + 1) * inner],
                        qkvw[core, kind, cols, :],
                        NT,
                    )
            wide[:, cols] = total
            return carry

        polled_loop(0, width // 256, token_tile, 0)

    per = heads // 2
    size = inner // per

    def back(spread, gq, gk, gv):
        pl.run_scoped(
            functools.partial(pair_phase, spread, gq, gk, gv),
            pltpu.VMEM((2 * inner, seq), BF16),
            pltpu.VMEM((2 * inner, seq), BF16),
            pltpu.VMEM((seq, 2 * inner), BF16),
            pltpu.VMEM((2, 2, seq, seq), BF16),
            pltpu.SemaphoreType.DMA((2,)),
        )
        pl.run_scoped(
            functools.partial(mix_phase, spread, gq, gk, gv),
            pltpu.VMEM((2,) + qkvw_h.shape, BF16),
            pltpu.VMEM((width, seq), BF16),
        )

    pl.run_scoped(
        back,
        pltpu.VMEM((seq // LANES * seq * 16, LANES), F32),
        pltpu.VMEM((seq, 2 * inner), BF16),
        pltpu.VMEM((seq, 2 * inner), BF16),
        pltpu.VMEM((seq, 2 * inner), BF16),
    )
    done = store(wide, gtok_h)
    for number in range(polls[0], 1 + max(number for number in plan if number != "tail")):
        run_steps(number)
    run_steps("tail")
    done.wait()
    for piece in kit.pieces:
        piece.finish()
    for copy in crossed[-4:]:
        copy().wait_send()
    for number in range(len(halves)):
        half(number).wait_send()


def layer(plan, bits, operands):
    tokens, qkvw, qvb, tab, outw, upw, upb, downw = operands[:8]
    seq, width = tokens.shape
    inner = qkvw.shape[2]
    units = upw.shape[1]
    heads = 2 * tab.shape[0]
    shape = jax.ShapeDtypeStruct
    here = pl.BlockSpec(memory_space=pltpu.VMEM)
    away = pl.BlockSpec(memory_space=pl.ANY)
    scalar = pl.BlockSpec(memory_space=pltpu.SMEM)
    rows = (3 * width * inner + inner * width + 2 * width * units) // inner
    lands = rows - (rows >> 4) + (bits - 4) * (rows >> 4)
    pieces = len(ORDERS["down"]) + len(ORDERS["up"]) + 4
    cuts = [one for _, one, _ in ORDERS["down"] + ORDERS["up"]]
    cuts += [ORDERS["out"][0]] + [one for one, _ in ORDERS["mix"]]
    leave = sum(3 if axis == "D" else 1 for one in cuts for axis in one)
    more = pieces * (bits - 4)
    return pl.pallas_call(
        functools.partial(layer_kernel, plan, bits),
        out_shape=(
            shape((rows, inner), BF16),
            shape((seq, width), F32),
            shape((seq, width), BF16),
            shape((16, width), F32),
            shape(qkvw.shape, BF16),
            shape(outw.shape, BF16),
            shape(upw.shape, BF16),
            shape(downw.shape, BF16),
            shape((heads, seq, seq), BF16),
        ),
        in_specs=[away] * 10 + [here] * 7 + [scalar],
        out_specs=(away, away, away, here) + (away,) * 5,
        scratch_shapes=[
            pltpu.VMEM((rows, inner), BF16),
            pltpu.VMEM((rows // 3, inner), BF16),
            pltpu.VMEM((rows, inner), BF16),
            pltpu.VMEM((lands, inner), BF16),
            pltpu.VMEM((seq, width), BF16),
            pltpu.VMEM((2,) + qvb.shape, F32),
            pltpu.VMEM((2,) + tab.shape, F32),
            pltpu.VMEM(upb.shape, F32),
            pltpu.VMEM(upb.shape, F32),
            pltpu.VMEM((2, 1, units), F32),
            pltpu.VMEM((2,) + outw.shape, BF16),
            pltpu.VMEM((seq, 2 * inner), BF16),
            pltpu.VMEM((seq, 2 * inner), BF16),
            pltpu.VMEM((seq, 2 * inner), BF16),
            pltpu.VMEM((2 * inner, seq), BF16),
            pltpu.VMEM((heads, 8, seq), F32),
            pltpu.VMEM((seq, seq), BF16),
            pltpu.VMEM((seq, width), F32),
            pltpu.VMEM((seq, width), BF16),
            pltpu.VMEM((seq, width), BF16),
            pltpu.VMEM((2, 8, units), F32),
            pltpu.VMEM((bits + 1, 16, width), F32),
            pltpu.VMEM((bits + 1, 16, width), F32),
            pltpu.SemaphoreType.DMA((24,)),
            pltpu.SemaphoreType.DMA((8,)),
            pltpu.SemaphoreType.DMA((leave + more,)),
            pltpu.SemaphoreType.DMA((2 * leave + more,)),
            pltpu.SemaphoreType.DMA((pieces,)),
            pltpu.SemaphoreType.DMA((pieces,)),
            pltpu.SemaphoreType.DMA((pieces,)),
            pltpu.SemaphoreType.DMA((bits + 1,)),
            pltpu.SemaphoreType.DMA((bits + 1,)),
            pltpu.SemaphoreType.DMA((7,)),
            pltpu.SemaphoreType.DMA((7,)),
        ],
        compiler_params=pltpu.CompilerParams(
            collective_id=0, has_side_effects=True, vmem_limit_bytes=VMEM_LIMIT
        ),
    )(*operands)


def finish_kernel(
    flat_h,
    out_h,
    gtok_h,
    small,
    out_f,
    gtok_f,
    mix_f,
    gqv,
    gtab,
    gout_f,
    goutb,
    gain1,
    shift1,
    up_f,
    gupb,
    down_f,
    gdownb,
    gain2,
    shift2,
    flat,
    mix,
    gout,
    up,
    down,
    gtok,
    out,
    in_sem,
    out_sem,
):
    rows, inner = flat.shape
    units, width = down.shape
    split = width // inner
    third = rows // 3
    copies = []
    tiles = units // 256
    span = 256 * split
    sizes = (
        [span] * tiles + [width] * (units // inner) + [split * inner] + [width] * 3
    )
    loads = []
    at = 0
    for number, size in enumerate(sizes):
        here = pl.ds(at, size)
        loads.append(pltpu.make_async_copy(flat_h.at[here, :], flat.at[here, :], in_sem.at[number]))
        loads[-1].start()
        at += size

    for source, target in ((gtok_h, gtok), (out_h, out)):
        loads.append(pltpu.make_async_copy(source, target, in_sem.at[len(loads)]))
        loads[-1].start()

    def store(source, target):
        copies.append(pltpu.make_async_copy(source, target, out_sem.at[len(copies)]))
        copies[-1].start()

    def wide(start, size):
        return flat[start : start + size, :].astype(F32)

    for tile in range(tiles):
        loads[tile].wait()
        here = slice(tile * 256, tile * 256 + 256)
        for side in range(split):
            down[here, side * inner : (side + 1) * inner] = wide(tile * span + side * 256, 256)
        if tile % 2:
            here = pl.ds(tile * 256 - 256, 512)
            store(down.at[here, :], down_f.at[here, :])
    parts = units // inner
    for part in range(parts):
        loads[tiles + part].wait()
    for top in range(0, width, 256):
        for part in range(parts):
            cols = slice(part * inner, (part + 1) * inner)
            up[top : top + 256, cols] = wide(third + part * width + top, 256)
        here = pl.ds(top, 256)
        store(up.at[here, :], up_f.at[here, :])
    at = 2 * third
    loads[-6].wait()
    for side in range(split):
        gout[:, side * inner : (side + 1) * inner] = wide(at + side * inner, inner)
    store(gout, gout_f)
    at += split * inner
    for kind in range(3):
        loads[kind - 5].wait()
        mix[kind] = wide(at + kind * width, width)
        store(mix.at[kind], mix_f.at[kind])
    loads[-2].wait()
    store(gtok, gtok_f)
    loads[-1].wait()
    store(out, out_f)
    for number, vector in enumerate((goutb, gain1, shift1, gdownb, gain2, shift2)):
        vector[...] = small[number : number + 1, :].reshape(width)
    gupb[...] = jnp.concatenate(
        [small[6 + side : 7 + side, :] for side in range(units // width)], axis=1
    ).reshape(units)
    for kind in range(2):
        gqv[kind : kind + 1, :] = small[8:9, kind * inner : (kind + 1) * inner]
    gtab[...] = small[10 : 10 + gtab.shape[0], : gtab.shape[1]]
    for copy in copies:
        copy.wait()


def finish(flat, small, out, grad_tokens, width, units, heads):
    shape = jax.ShapeDtypeStruct
    here = pl.BlockSpec(memory_space=pltpu.VMEM)
    away = pl.BlockSpec(memory_space=pl.ANY)
    inner = flat.shape[1]
    vector = shape((width,), F32)
    got = pl.pallas_call(
        finish_kernel,
        out_shape=(
            shape(out.shape, BF16),
            shape(grad_tokens.shape, F32),
            shape((3, width, inner), F32),
            shape((2, inner), F32),
            shape((heads, 2 * LANES), F32),
            shape((inner, width), F32),
            vector,
            vector,
            vector,
            shape((width, units), F32),
            shape((units,), F32),
            shape((units, width), F32),
            vector,
            vector,
            vector,
        ),
        in_specs=[away] * 3 + [here],
        out_specs=(away, away, away, here, here, away, here, here, here, away, here, away)
        + (here,) * 3,
        scratch_shapes=[
            pltpu.VMEM(flat.shape, BF16),
            pltpu.VMEM((3, width, inner), F32),
            pltpu.VMEM((inner, width), F32),
            pltpu.VMEM((width, units), F32),
            pltpu.VMEM((units, width), F32),
            pltpu.VMEM(grad_tokens.shape, F32),
            pltpu.VMEM(out.shape, BF16),
            pltpu.SemaphoreType.DMA((units // 256 + units // inner + 6,)),
            pltpu.SemaphoreType.DMA((units // 256 + units // inner + 6,)),
        ],
        compiler_params=pltpu.CompilerParams(vmem_limit_bytes=VMEM_LIMIT),
    )(flat, out, grad_tokens, small)
    got = list(got)
    got[2] = jnp.transpose(got[2], (1, 0, 2))
    got[4] = got[4].T
    return tuple(got)


def order_of_steps(bits):
    pieces = len(ORDERS["down"]) + len(ORDERS["up"]) + 4
    plan = dict(PAUSES)
    known = {step for steps in PAUSES.values() for step in steps} | set(TAIL)
    more = tuple((pieces, step) for step in range(1, bits + 2) if (pieces, step) not in known)
    plan["tail"] = TAIL + more
    return plan


def on_device(
    dp,
    tokens,
    qkv_weight,
    qv_bias,
    rel_table,
    out_weight,
    out_bias,
    norm1_gain,
    norm1_bias,
    up_weight,
    up_bias,
    down_weight,
    down_bias,
    norm2_gain,
    norm2_bias,
    rel_bucket,
    query_len,
    key_mask,
    upstream,
):
    width = tokens.shape[1]
    units = up_weight.shape[1]
    bits = int(math.log2(dp))
    flat, grad_tokens, out, small = layer(
        order_of_steps(bits),
        bits,
        (
            tokens,
            jnp.transpose(qkv_weight, (1, 0, 2)),
            qv_bias,
            rel_table.T,
            out_weight,
            up_weight,
            up_bias,
            down_weight,
            upstream,
            rel_bucket,
            out_bias,
            norm1_gain,
            norm1_bias,
            down_bias,
            norm2_gain,
            norm2_bias,
            key_mask,
            query_len,
        ),
    )[:4]
    return finish(flat, small, out, grad_tokens, width, units, rel_table.shape[1])


def solution(mesh):
    rows = P(("dp", "tensor"), None)
    whole = P()
    in_specs = (
        rows,
        P(None, None, "tensor"),
        P(None, "tensor"),
        P(None, "tensor"),
        P("tensor", None),
        whole,
        whole,
        whole,
        P(None, "tensor"),
        P("tensor"),
        P("tensor", None),
        whole,
        whole,
        whole,
        whole,
        P("dp"),
        P("dp", None),
        rows,
    )
    out_specs = (
        rows,
        rows,
        P(None, None, "tensor"),
        P(None, "tensor"),
        P(None, "tensor"),
        P("tensor", None),
        whole,
        whole,
        whole,
        P(None, "tensor"),
        P("tensor"),
        P("tensor", None),
        whole,
        whole,
        whole,
    )
    return jax.shard_map(
        functools.partial(on_device, mesh.shape["dp"]),
        mesh=mesh,
        in_specs=in_specs,
        out_specs=out_specs,
        check_vma=False,
    )
```
